128 devices in a mesh: row: 4 (over x_hi, core), col: 32 (over y, x_lo, z).
Axes of the slice: x: 4 (x_hi: 2, x_lo: 2; x = x_hi * 2 + x_lo), y: 4, z: 4, core: 2. Of those that a mesh axis runs over, the one named last changes fastest.
Arguments:
- adjusted_weight: bfloat16 [8192, 53248], P('row', 'col'), may hold values from -0.05416994 to 0.05416994
- base_weight: bfloat16 [8192, 53248], P('row', 'col'), may hold values from -0.026434931 to 0.026434931
- test_matrix: float32 [53248, 512], P('col'), may hold values from -6 to 6
Outputs:
- basis: float32 [8192, 512], P(('row', 'col'))
The draws below stay inside these ranges and needn't reach their ends.
All inputs are finite; a program needn't handle non-finite values.
Results may differ from the reference program's by a relative error of at most 0.0015.
Values sent between devices are 32-bit elements; how exact they have to be, the bound alone decides.
A program may use at most 128 MiB of HBM per device.

```python
import jax
import jax.numpy as jnp
from jax import lax

M = 8192
N = 53248
K = 512


def shared_order(key):
    return jax.random.permutation(jax.random.fold_in(key, 303), N).astype(jnp.float32) + 1.0


def pair_from(base_value, delta_value, rank_order, decay_power, scale_ratio):
    weight_scale = jnp.float32(N) ** (-0.5)
    floor_scale = 0.01 * weight_scale
    leading = scale_ratio * floor_scale * rank_order ** (-decay_power)
    column_scale = jnp.sqrt(leading * leading + floor_scale * floor_scale)
    base_rounded = (weight_scale * base_value).astype(jnp.bfloat16)
    adjusted_rounded = (base_rounded.astype(jnp.float32) + delta_value * column_scale[None, :]).astype(jnp.bfloat16)
    return (adjusted_rounded, base_rounded)


def draw_pair(key):
    rank_order = shared_order(key)
    base_key = jax.random.fold_in(key, 101)
    delta_key = jax.random.fold_in(key, 202)
    base_value = jnp.clip(jax.random.normal(base_key, (M, N), jnp.float32), -6.0, 6.0)
    delta_value = jnp.clip(jax.random.normal(delta_key, (M, N), jnp.float32), -6.0, 6.0)
    return pair_from(base_value, delta_value, rank_order, 0.6, 100.0)


def draw_adjusted_weight(key, part):
    adjusted_rounded, base_rounded = draw_pair(key)
    return adjusted_rounded


def draw_base_weight(key, part):
    adjusted_rounded, base_rounded = draw_pair(key)
    return base_rounded


def level_of(own_key, shape, split, least, largest):
    factor_of = 1.0
    for dim, parts in split:
        heights = jax.random.uniform(jax.random.fold_in(jax.random.fold_in(own_key, 6), dim), (parts,), jnp.float32, least / len(split), largest / len(split))
        factor_of = factor_of * jnp.repeat(jnp.exp(heights), shape[dim] // parts).reshape((-1,) + (1,) * (len(shape) - 1 - dim))
    return factor_of


def centred(rng, extent, scale, most, pieces=(), held_as=jnp.bfloat16):
    factor_of = level_of(rng, extent, pieces, -0.22, 0.18) if pieces else 1.0
    array = jax.random.normal(rng, extent, jnp.float32) * scale * factor_of
    return jnp.minimum(jnp.maximum(array, -most), most).astype(held_as)


def setup_inputs(seed: int = 0) -> dict:
    key_of = jax.random.split(jax.random.key(seed), 4)
    adjusted_weight = draw_adjusted_weight(jax.random.fold_in(key_of[3], 71), 0)
    base_weight = draw_base_weight(jax.random.fold_in(key_of[3], 71), 0)
    test_matrix = centred(key_of[2], (N, K), 1.0, 6.0, ((0, 32),), jnp.float32)
    return {"adjusted_weight": adjusted_weight, "base_weight": base_weight, "test_matrix": test_matrix}


def cholesky_basis(sketch):
    gram_matrix = jnp.einsum('ik,il->kl', sketch, sketch, precision=lax.Precision.HIGHEST)
    factor_low = jnp.linalg.cholesky(gram_matrix)
    return lax.linalg.triangular_solve(factor_low, sketch, left_side=False, lower=True, transpose_a=True)

def reference(adjusted_weight, base_weight, test_matrix):
    delta_full = adjusted_weight.astype(jnp.float32) - base_weight.astype(jnp.float32)
    sketch = jnp.dot(delta_full.astype(jnp.float32), test_matrix.astype(jnp.float32), precision=lax.Precision.HIGHEST, preferred_element_type=jnp.float32)
    first_basis = cholesky_basis(sketch)
    cosketch = jnp.einsum('mn,mk->nk', delta_full, first_basis, precision=lax.Precision.HIGHEST)
    second_basis = cholesky_basis(cosketch)
    resketch = jnp.dot(delta_full.astype(jnp.float32), second_basis.astype(jnp.float32), precision=lax.Precision.HIGHEST, preferred_element_type=jnp.float32)
    return jnp.sqrt(jnp.float32(M)) * cholesky_basis(resketch)
```

```python
import jax
import jax.numpy as jnp
from jax import lax
from jax.experimental import pallas as pl
from jax.experimental.pallas import tpu as pltpu
from jax.sharding import PartitionSpec as P

MESH = pl.DeviceIdType.MESH
VM = pl.BlockSpec(memory_space=pltpu.VMEM)

def place():
    r = lax.axis_index("row"); c = lax.axis_index("col")
    y = lax.div(c, 8); x = lax.rem(lax.div(c, 4), 2); z = lax.rem(c, 4)
    def dev(yy, xx, zz):
        return (r, yy*8 + xx*4 + zz)
    return r, y, x, z, dev

def barrier(devs):
    sem = pltpu.get_barrier_semaphore()
    for d in devs:
        pl.semaphore_signal(sem, inc=1, device_id=d, device_id_type=MESH)
    pl.semaphore_wait(sem, len(devs))

def rc(src, dst, ssem, rsem, dev):
    return pltpu.make_async_remote_copy(src_ref=src, dst_ref=dst, send_sem=ssem, recv_sem=rsem, device_id=dev, device_id_type=MESH)

class RingRS:
    def __init__(self, part, me, devp, devm, relay, fin, ssem, rsem):
        self.part, self.me, self.devp, self.devm, self.relay, self.fin = part, me, devp, devm, relay, fin
        up = lax.rem(me+1, 4); dn = lax.rem(me+3, 4); far = lax.rem(me+2, 4)
        self.up, self.dn = up, dn
        self.c = [
            rc(part(far, 0), relay.at[0], ssem.at[0], rsem.at[0], devp),
            rc(part(far, 1), relay.at[1], ssem.at[1], rsem.at[1], devm),
            rc(part(up, 1), fin.at[0, 1], ssem.at[2], rsem.at[2], devp),
            rc(part(dn, 0), fin.at[1, 0], ssem.at[3], rsem.at[3], devm),
            rc(relay.at[0], fin.at[0, 0], ssem.at[4], rsem.at[4], devp),
            rc(relay.at[1], fin.at[1, 1], ssem.at[5], rsem.at[5], devm),
        ]
    def start(self):
        for i in range(4): self.c[i].start()
    def forward(self):
        self.c[0].wait_recv()
        self.relay[0] = self.relay[0] + self.part(self.up, 0)[...]
        self.c[4].start()
        self.c[1].wait_recv()
        self.relay[1] = self.relay[1] + self.part(self.dn, 1)[...]
        self.c[5].start()
    def finish(self, out):
        for i in (2, 3, 4, 5): self.c[i].wait_recv()
        for h in range(2):
            out[h] = self.part(self.me, h)[...] + self.fin[0, h] + self.fin[1, h]
    def drain(self):
        for i in range(6): self.c[i].wait_send()

def rs_col_kernel(p, o, relA, finA, relB, finB, qa, qb, relA2, finA2, relB2, finB2, ra, rb, recx, ss, rs, sx, rx):
    r, y, x, z, dev = place()
    yp, ym = dev(lax.rem(y+1,4),x,z), dev(lax.rem(y+3,4),x,z)
    zp, zm = dev(y,x,lax.rem(z+1,4)), dev(y,x,lax.rem(z+3,4))
    xd = dev(y,1-x,z)
    barrier([yp, ym, zp, zm, xd])
    A = pl.ds(0,256); Bc = pl.ds(256,256)
    a1 = RingRS(lambda k,h: p.at[k,h,:,:,A], y, yp, ym, relA, finA, ss.at[0], rs.at[0])
    b1 = RingRS(lambda k,h: p.at[:,h,k,:,Bc], z, zp, zm, relB, finB, ss.at[1], rs.at[1])
    a1.start(); b1.start(); a1.forward(); b1.forward()
    a1.finish(qa)
    a2 = RingRS(lambda k,h: qa.at[h,k], z, zp, zm, relA2, finA2, ss.at[2], rs.at[2])
    a2.start()
    b1.finish(qb)
    b2 = RingRS(lambda k,h: qb.at[h,k], y, yp, ym, relB2, finB2, ss.at[3], rs.at[3])
    b2.start()
    a2.forward(); b2.forward()
    a2.finish(ra)
    cxa = rc(ra.at[1-x], recx.at[0], sx.at[0], rx.at[0], xd); cxa.start()
    b2.finish(rb)
    cxb = rc(rb.at[1-x], recx.at[1], sx.at[1], rx.at[1], xd); cxb.start()
    cxa.wait_recv()
    o[:, 0:256] = ra[x] + recx[0]
    cxb.wait_recv()
    o[:, 256:512] = rb[x] + recx[1]
    for t in (a1, b1, a2, b2): t.drain()
    cxa.wait_send(); cxb.wait_send()

def rs_col(p, cid=1):
    S = 64
    f = jnp.float32
    V = lambda *s: pltpu.VMEM(s, f)
    return pl.pallas_call(rs_col_kernel, out_shape=jax.ShapeDtypeStruct((S,512), f), in_specs=[VM], out_specs=VM,
        scratch_shapes=[V(2,4,S,256), V(2,2,4,S,256), V(2,4,S,256), V(2,2,4,S,256), V(2,4,S,256), V(2,4,S,256),
            V(2,S,256), V(2,2,S,256), V(2,S,256), V(2,2,S,256), V(2,S,256), V(2,S,256), V(2,S,256),
            pltpu.SemaphoreType.DMA((4,6)), pltpu.SemaphoreType.DMA((4,6)), pltpu.SemaphoreType.DMA((2,)), pltpu.SemaphoreType.DMA((2,))],
        compiler_params=pltpu.CompilerParams(collective_id=cid, has_side_effects=True, vmem_limit_bytes=56*2**20), name="rs_col")(p.reshape(4,2,4,S,512))

class RingAG:
    def __init__(self, part, me, devp, devm, ssem, rsem):
        up = lax.rem(me+1, 4); dn = lax.rem(me+3, 4)
        far = lax.rem(me+2, 4)
        self.s = [rc(part(me,0), part(me,0), ssem.at[0], rsem.at[0], devp),
                  rc(part(me,1), part(me,1), ssem.at[1], rsem.at[1], devm),
                  rc(part(me,1), part(me,1), ssem.at[2], rsem.at[2], devp),
                  rc(part(me,0), part(me,0), ssem.at[3], rsem.at[3], devm),
                  rc(part(dn,0), part(dn,0), ssem.at[4], rsem.at[4], devp),
                  rc(part(up,1), part(up,1), ssem.at[5], rsem.at[5], devm)]
        self.r = [rc(part(dn,0), part(dn,0), ssem.at[0], rsem.at[0], devp),
                  rc(part(up,1), part(up,1), ssem.at[1], rsem.at[1], devm),
                  rc(part(dn,1), part(dn,1), ssem.at[2], rsem.at[2], devp),
                  rc(part(up,0), part(up,0), ssem.at[3], rsem.at[3], devm),
                  rc(part(far,0), part(far,0), ssem.at[4], rsem.at[4], devp),
                  rc(part(far,1), part(far,1), ssem.at[5], rsem.at[5], devm)]
    def start(self):
        for i in range(4): self.s[i].start()
    def forward(self):
        self.r[0].wait_recv(); self.s[4].start()
        self.r[1].wait_recv(); self.s[5].start()
    def finish(self):
        for i in (2,3,4,5): self.r[i].wait_recv()
    def drain(self):
        for i in range(6): self.s[i].wait_send()

def ag_col_kernel(p, o, ss, rs, sx, rx):
    r, y, x, z, dev = place()
    yp, ym = dev(lax.rem(y+1,4),x,z), dev(lax.rem(y+3,4),x,z)
    zp, zm = dev(y,x,lax.rem(z+1,4)), dev(y,x,lax.rem(z+3,4))
    xd = dev(y,1-x,z)
    o[y,x,z] = p[...]
    barrier([yp, ym, zp, zm, xd])
    cx = rc(o.at[y,x,z], o.at[y,x,z], sx.at[0], rx.at[0], xd)
    cxr = rc(o.at[y,1-x,z], o.at[y,1-x,z], sx.at[0], rx.at[0], xd)
    cx.start()
    A = pl.ds(0,256); Bc = pl.ds(256,256)
    cxr.wait_recv()
    a1 = RingAG(lambda k,h: o.at[y,h,k,:,A], z, zp, zm, ss.at[0], rs.at[0])
    b1 = RingAG(lambda k,h: o.at[k,h,z,:,Bc], y, yp, ym, ss.at[1], rs.at[1])
    a1.start(); b1.start()
    a1.forward(); b1.forward()
    a1.finish()
    a2 = RingAG(lambda k,h: o.at[k,h,:,:,A], y, yp, ym, ss.at[2], rs.at[2])
    a2.start()
    b1.finish()
    b2 = RingAG(lambda k,h: o.at[:,h,k,:,Bc], z, zp, zm, ss.at[3], rs.at[3])
    b2.start()
    a2.forward(); b2.forward()
    a2.finish(); b2.finish()
    for t in (a1,b1,a2,b2): t.drain()
    cx.wait_send()

def ag_col(p, cid=2):
    S = 64
    o = pl.pallas_call(ag_col_kernel, out_shape=jax.ShapeDtypeStruct((4,2,4,S,512), jnp.float32), in_specs=[VM], out_specs=VM,
        scratch_shapes=[pltpu.SemaphoreType.DMA((4,6)), pltpu.SemaphoreType.DMA((4,6)), pltpu.SemaphoreType.DMA((1,)), pltpu.SemaphoreType.DMA((1,))],
        compiler_params=pltpu.CompilerParams(collective_id=cid, has_side_effects=True, vmem_limit_bytes=56*2**20), name="ag_col")(p)
    return o.reshape(32*S, 512)

def rs_row_kernel(p, o, rec1, q, rec2, s1, r1, s2, r2):
    r = lax.axis_index("row"); c = lax.axis_index("col")
    h = lax.div(r,2); k = lax.rem(r,2)
    other = (h*2 + 1-k, c); far = ((1-h)*2 + k, c)
    barrier([other, far])
    cs = [rc(p.at[1-h, 1-k], rec1.at[0], s1.at[0], r1.at[0], other), rc(p.at[h, 1-k], rec1.at[1], s1.at[1], r1.at[1], other)]
    for t in cs: t.start()
    cs[0].wait_recv()
    q[...] = p[1-h, k] + rec1[0]
    c2 = rc(q, rec2, s2.at[0], r2.at[0], far); c2.start()
    cs[1].wait_recv()
    o[...] = p[h, k] + rec1[1]
    c2.wait_recv()
    o[...] = o[...] + rec2[...]
    for t in cs: t.wait_send()
    c2.wait_send()

def rs_row(p, cid=3):
    n = p.shape[0]//4
    V = lambda *s: pltpu.VMEM(s, jnp.float32)
    D = pltpu.SemaphoreType.DMA
    return pl.pallas_call(rs_row_kernel, out_shape=jax.ShapeDtypeStruct((n,512), jnp.float32), in_specs=[VM], out_specs=VM,
        scratch_shapes=[V(2,n,512), V(n,512), V(n,512), D((2,)), D((2,)), D((1,)), D((1,))],
        compiler_params=pltpu.CompilerParams(collective_id=cid, has_side_effects=True, vmem_limit_bytes=56*2**20), name="rs_row")(p.reshape(2,2,n,512))

def ag_row_kernel(p, o, s1, r1, s2, r2):
    r = lax.axis_index("row"); c = lax.axis_index("col")
    h = lax.div(r,2); k = lax.rem(r,2)
    other = (h*2 + 1-k, c); far = ((1-h)*2 + k, c)
    o[h, k] = p[...]
    barrier([other, far])
    cf = rc(o.at[h,k], o.at[h,k], s1.at[0], r1.at[0], far)
    cfr = rc(o.at[1-h,k], o.at[1-h,k], s1.at[0], r1.at[0], far)
    cf.start()
    co = rc(o.at[h,k], o.at[h,k], s2.at[0], r2.at[0], other)
    cor = rc(o.at[h,1-k], o.at[h,1-k], s2.at[0], r2.at[0], other)
    co.start()
    cfr.wait_recv()
    co2 = rc(o.at[1-h,k], o.at[1-h,k], s2.at[1], r2.at[1], other)
    co2r = rc(o.at[1-h,1-k], o.at[1-h,1-k], s2.at[1], r2.at[1], other)
    co2.start()
    cor.wait_recv(); co2r.wait_recv()
    cf.wait_send(); co.wait_send(); co2.wait_send()

def ag_row(p, cid=4):
    n = p.shape[0]
    D = pltpu.SemaphoreType.DMA
    o = pl.pallas_call(ag_row_kernel, out_shape=jax.ShapeDtypeStruct((2,2,n,512), jnp.float32), in_specs=[VM], out_specs=VM,
        scratch_shapes=[D((1,)), D((1,)), D((2,)), D((2,))],
        compiler_params=pltpu.CompilerParams(collective_id=cid, has_side_effects=True, vmem_limit_bytes=56*2**20), name="ag_row")(p)
    return o.reshape(4*n, 512)
HI = lax.Precision.HIGHEST
PAIRS = [(i, k) for i in range(4) for k in range(i, 4)]
GROUPS = [(0, 2, "zyx"), (2, 2, "yxz"), (4, 1, "xzy")]

def gram_kernel(s, o, g, crec, *rest):
    bufs, (ssc, rsc, ss, rs) = rest[:-4], rest[-4:]
    r = lax.axis_index("row"); c = lax.axis_index("col")
    xh = lax.div(r, 2); k = lax.rem(r, 2)
    y = lax.div(c, 8); xl = lax.rem(lax.div(c, 4), 2); z = lax.rem(c, 4)
    x = xh*2 + xl
    at = {"x": x, "y": y, "z": z}
    def dev(q):
        return (lax.div(q["x"], 2)*2 + k, q["y"]*8 + lax.rem(q["x"], 2)*4 + q["z"])
    def peer(ax, d):
        q = dict(at); q[ax] = lax.rem(at[ax]+d, 4)
        return q[ax], dev(q)
    other = (xh*2 + 1-k, c)
    barrier([other] + [peer(ax, d)[1] for ax in "xyz" for d in (1,2,3)])
    n = 0
    for i in range(4):
        w = jnp.einsum("ni,nk->ik", s[:, i*128:(i+1)*128], s[:, i*128:], precision=HI, preferred_element_type=jnp.float32)
        for j in range(i, 4):
            g[n//5, n%5] = w[:, (j-i)*128:(j-i+1)*128]
            n += 1
    cc = rc(g.at[1-k], crec, ssc.at[0], rsc.at[0], other)
    cc.start()
    cc.wait_recv()
    g[k] = g[k] + crec[...]
    sends = []
    def exchange(src, buf, ax, sem):
        me = at[ax]
        cs = []
        for d in (1, 3, 2):
            to, dv = peer(ax, d)
            t = rc(src(to), buf.at[me], ss.at[sem, d], rs.at[sem, me], dv)
            t.start(); cs.append(t)
        sends.extend(cs)
        def done():
            for d in (1, 3, 2):
                fr, dv = peer(ax, d)
                rc(src(fr), buf.at[fr], ss.at[sem, d], rs.at[sem, fr], dv).wait_recv()
        return done
    def gather(view, ax, sem):
        me = at[ax]
        cs = []
        for d in (1, 3, 2):
            to, dv = peer(ax, d)
            t = rc(view(me), view(me), ss.at[sem, d], rs.at[sem, me], dv)
            t.start(); cs.append(t)
        sends.extend(cs)
        def done():
            for d in (1, 3, 2):
                fr, dv = peer(ax, d)
                rc(view(fr), view(fr), ss.at[sem, d], rs.at[sem, fr], dv).wait_recv()
        return done
    G3 = range(3)

    b1 = [bufs[3*i] for i in G3]; b2 = [bufs[3*i+1] for i in G3]; b3 = [bufs[3*i+2] for i in G3]
    f = []
    for i, (b0, nb, od) in enumerate(GROUPS):
        f.append(exchange(lambda q, b0=b0, nb=nb: g.at[k, pl.ds(b0, nb), pl.ds(pl.multiple_of(q*32, 32), 32)], b1[i], od[0], i*5))
    for i, (b0, nb, od) in enumerate(GROUPS):
        b1[i][at[od[0]]] = g[k, b0:b0+nb, pl.ds(pl.multiple_of(at[od[0]]*32, 32), 32)]
    f2 = []
    for i, (b0, nb, od) in enumerate(GROUPS):
        f[i]()
        b1[i][4] = (b1[i][0] + b1[i][1]) + (b1[i][2] + b1[i][3])
        f2.append(exchange(lambda q, i=i: b1[i].at[4, :, pl.ds(pl.multiple_of(q*8, 8), 8)], b2[i], od[1], i*5+1))
        b2[i][at[od[1]]] = b1[i][4, :, pl.ds(pl.multiple_of(at[od[1]]*8, 8), 8)]
    f3 = []
    for i, (b0, nb, od) in enumerate(GROUPS):
        f2[i]()
        b3[i][at[od[2]]] = (b2[i][0] + b2[i][1]) + (b2[i][2] + b2[i][3])
        f3.append(gather(lambda q, i=i: b3[i].at[q], od[2], i*5+2))
    f4 = []
    for i, (b0, nb, od) in enumerate(GROUPS):
        f3[i]()
        rows = lambda q, i=i, b0=b0, nb=nb, od=od: o.at[k, pl.ds(b0, nb), pl.ds(pl.multiple_of(at[od[0]]*32 + q*8, 8), 8)]
        rows(at[od[1]])[...] = (b3[i][0] + b3[i][1]) + (b3[i][2] + b3[i][3])
        f4.append(gather(rows, od[1], i*5+3))
    f5 = []
    for i, (b0, nb, od) in enumerate(GROUPS):
        f4[i]()
        f5.append(gather(lambda q, b0=b0, nb=nb: o.at[k, pl.ds(b0, nb), pl.ds(pl.multiple_of(q*32, 32), 32)], od[0], i*5+4))
    for t in f5: t()
    co = rc(o.at[k], o.at[k], ssc.at[1], rsc.at[1], other)
    co.start()
    rc(o.at[1-k], o.at[1-k], ssc.at[1], rsc.at[1], other).wait_recv()
    for t in sends: t.wait_send()
    cc.wait_send(); co.wait_send()

def gram_blocks(s, cid):
    V = lambda *sh: pltpu.VMEM(sh, jnp.float32)
    D = pltpu.SemaphoreType.DMA
    bufs = []
    for b0, nb, od in GROUPS:
        bufs += [V(5, nb, 32, 128), V(4, nb, 8, 128), V(4, nb, 8, 128)]
    return pl.pallas_call(gram_kernel, out_shape=jax.ShapeDtypeStruct((2,5,128,128), jnp.float32), in_specs=[VM], out_specs=VM,
        scratch_shapes=[V(2,5,128,128), V(5,128,128)] + bufs + [D((2,)), D((2,)), D((15,4)), D((15,4))],
        compiler_params=pltpu.CompilerParams(collective_id=cid, has_side_effects=True, vmem_limit_bytes=56*2**20), name="gram")(s)
HI = lax.Precision.HIGHEST
B = 128

def mm(a, b):
    return jnp.dot(a, b, precision=HI, preferred_element_type=jnp.float32)

def leaf_inverse(a):
    n = B // 8
    lane = lax.broadcasted_iota(jnp.int32, (1, B), 1)
    sub = lax.broadcasted_iota(jnp.int32, (8, B), 0)
    lane8 = lax.broadcasted_iota(jnp.int32, (8, B), 1)
    ch = [a[8*t:8*t+8, :] for t in range(n)]
    drow = jnp.zeros((8, B), jnp.float32)
    for t in range(n):
        drow = drow + jnp.where(lane8 == sub + 8*t, ch[t], 0.0)
    srow = lax.rsqrt(jnp.sum(drow, axis=0, keepdims=True))
    srow8 = jnp.broadcast_to(srow, (8, B))
    for t in range(n):
        scol = jnp.sum(jnp.where(lane8 == sub + 8*t, srow8, 0.0), axis=1, keepdims=True)
        ch[t] = ch[t] * srow8 * scol
    for j in range(0, B, 4):
        t0, s = divmod(j, 8)
        c = [jnp.broadcast_to(ch[t0][:, j+b:j+b+1], (8, B)) for b in range(4)]
        pv = lambda i, k: c[k][s+i:s+i+1]
        piv = [lane == j+b for b in range(4)]
        inpiv = (lane >= j) & (lane < j+4)
        R = [jnp.where(piv[b], 1.0, jnp.where(inpiv, 0.0, ch[t0][s+b:s+b+1, :])) for b in range(4)]
        p, q, d = pv(0, 0), pv(1, 0), pv(1, 1)
        det = p*d - q*q
        idet = 1.0 / det
        ip, iq, iD = d*idet, -q*idet, p*idet
        t00 = pv(2,0)*ip + pv(2,1)*iq; t01 = pv(2,0)*iq + pv(2,1)*iD
        t10 = pv(3,0)*ip + pv(3,1)*iq; t11 = pv(3,0)*iq + pv(3,1)*iD
        s00 = pv(2,2) - (t00*pv(2,0) + t01*pv(2,1))
        s10 = pv(3,2) - (t10*pv(2,0) + t11*pv(2,1))
        s11 = pv(3,3) - (t10*pv(3,0) + t11*pv(3,1))
        dets = s00*s11 - s10*s10
        idets = 1.0 / dets
        v0 = R[2] - (t00*R[0] + t01*R[1])
        v1 = R[3] - (t10*R[0] + t11*R[1])
        w2 = (s11*v0 - s10*v1) * idets
        w3 = (s00*v1 - s10*v0) * idets
        w0 = (ip*R[0] + iq*R[1]) - (t00*w2 + t10*w3)
        w1 = (iq*R[0] + iD*R[1]) - (t01*w2 + t11*w3)
        W = [jnp.broadcast_to(w, (8, B)) for w in (w0, w1, w2, w3)]
        ipp = 1.0 / p; iss = 1.0 / s00
        F = [R[0]*lax.rsqrt(p), (R[1] - (q*ipp)*R[0])*lax.rsqrt(det*ipp), v0*lax.rsqrt(s00), (v1 - (s10*iss)*v0)*lax.rsqrt(dets*iss)]
        inpiv8 = (lane8 >= j) & (lane8 < j+4)
        for t in range(t0, n):
            if t == t0:
                m = [jnp.where(sub > s+3, c[b], 0.0) for b in range(4)]
            else:
                m = [jnp.broadcast_to(ch[t][:, j+b:j+b+1], (8, B)) for b in range(4)]
            u = (m[0]*W[0] + m[1]*W[1]) + (m[2]*W[2] + m[3]*W[3])
            ch[t] = jnp.where(inpiv8, 0.0, ch[t]) - u
            if t == t0:
                for b in range(4):
                    ch[t] = jnp.where(sub == s+b, jnp.broadcast_to(jnp.where(lane <= j+b, F[b], 0.0), (8, B)), ch[t])

    return jnp.concatenate([x * srow8 for x in ch], 0)

def chol_kernel(g_ref, x_ref):
    n = 0
    for i in range(4):
        for k in range(4):
            if k >= i:
                x_ref[i*B:(i+1)*B, k*B:(k+1)*B] = g_ref[n]
                n += 1
            else:
                x_ref[i*B:(i+1)*B, k*B:(k+1)*B] = jnp.zeros((B, B), jnp.float32)
    for J in range(4):
        lo, hi = J*B, (J+1)*B
        x = leaf_inverse(x_ref[lo:hi, lo:hi])
        x_ref[lo:hi, lo:hi] = x
        if J > 0:
            x_ref[lo:hi, 0:lo] = mm(x, x_ref[lo:hi, 0:lo])
        if J < 3:
            right = mm(x, x_ref[lo:hi, hi:])
            rt = right.T
            x_ref[lo:hi, hi:] = right
            x_ref[hi:, hi:] = x_ref[hi:, hi:] - mm(rt, right)
            left = mm(rt, x_ref[lo:hi, 0:hi])
            if J > 0:
                x_ref[hi:, 0:lo] = x_ref[hi:, 0:lo] - left[:, 0:lo]
            x_ref[hi:, lo:hi] = -left[:, lo:hi]
            x_ref[lo:hi, hi:] = jnp.zeros_like(right)

def chol_inverse(g):
    return pl.pallas_call(chol_kernel, out_shape=jax.ShapeDtypeStruct((4*B, 4*B), jnp.float32),
        in_specs=[pl.BlockSpec(memory_space=pltpu.VMEM)], out_specs=pl.BlockSpec(memory_space=pltpu.VMEM),
        compiler_params=pltpu.CompilerParams(vmem_limit_bytes=48*2**20), name="chol")(g)
M = 8192


def apply_inverse(rows, x):
    return lax.dot_general(rows, x, (((1,), (1,)), ((), ())), precision=HI, preferred_element_type=jnp.float32)


def shards(adjusted_weight, base_weight, test_matrix):
    delta = adjusted_weight.astype(jnp.float32) - base_weight.astype(jnp.float32)
    scale_out = jnp.sqrt(jnp.float32(M))
    own = rs_col(mm(delta, test_matrix))
    x1 = chol_inverse(gram_blocks(own, 5).reshape(10, B, B))
    sketch = ag_col(own)
    raw = rs_row(jnp.einsum("mn,mk->nk", delta, sketch, precision=HI, preferred_element_type=jnp.float32))
    own_co = apply_inverse(raw, x1)
    x2 = chol_inverse(gram_blocks(own_co, 6).reshape(10, B, B))
    cosketch = ag_row(own_co)
    own = apply_inverse(rs_col(mm(delta, cosketch)), x2)
    x3 = chol_inverse(gram_blocks(own, 5).reshape(10, B, B))
    return scale_out * apply_inverse(own, x3)


def solution(mesh):
    return jax.shard_map(
        shards,
        mesh=mesh,
        in_specs=(P("row", "col"), P("row", "col"), P("col", None)),
        out_specs=P(("row", "col"), None),
        check_vma=False,
    )
```

```python
import jax
import jax.numpy as jnp
from jax import lax
from jax.experimental import pallas as pl
from jax.experimental.pallas import tpu as pltpu
from jax.sharding import PartitionSpec as P

MESH = pl.DeviceIdType.MESH
VM = pl.BlockSpec(memory_space=pltpu.VMEM)

def place():
    r = lax.axis_index("row"); c = lax.axis_index("col")
    y = lax.div(c, 8); x = lax.rem(lax.div(c, 4), 2); z = lax.rem(c, 4)
    def dev(yy, xx, zz):
        return (r, yy*8 + xx*4 + zz)
    return r, y, x, z, dev

def barrier(devs):
    sem = pltpu.get_barrier_semaphore()
    for d in devs:
        pl.semaphore_signal(sem, inc=1, device_id=d, device_id_type=MESH)
    pl.semaphore_wait(sem, len(devs))

def rc(src, dst, ssem, rsem, dev):
    return pltpu.make_async_remote_copy(src_ref=src, dst_ref=dst, send_sem=ssem, recv_sem=rsem, device_id=dev, device_id_type=MESH)

class RingRS:
    def __init__(self, part, me, devp, devm, relay, fin, ssem, rsem):
        self.part, self.me, self.devp, self.devm, self.relay, self.fin = part, me, devp, devm, relay, fin
        up = lax.rem(me+1, 4); dn = lax.rem(me+3, 4); far = lax.rem(me+2, 4)
        self.up, self.dn = up, dn
        self.c = [
            rc(part(far, 0), relay.at[0], ssem.at[0], rsem.at[0], devp),
            rc(part(far, 1), relay.at[1], ssem.at[1], rsem.at[1], devm),
            rc(part(up, 1), fin.at[0, 1], ssem.at[2], rsem.at[2], devp),
            rc(part(dn, 0), fin.at[1, 0], ssem.at[3], rsem.at[3], devm),
            rc(relay.at[0], fin.at[0, 0], ssem.at[4], rsem.at[4], devp),
            rc(relay.at[1], fin.at[1, 1], ssem.at[5], rsem.at[5], devm),
        ]
    def start(self):
        for i in range(4): self.c[i].start()
    def forward(self):
        self.c[0].wait_recv()
        self.relay[0] = self.relay[0] + self.part(self.up, 0)[...]
        self.c[4].start()
        self.c[1].wait_recv()
        self.relay[1] = self.relay[1] + self.part(self.dn, 1)[...]
        self.c[5].start()
    def finish(self, out):
        for i in (2, 3, 4, 5): self.c[i].wait_recv()
        for h in range(2):
            out[h] = self.part(self.me, h)[...] + self.fin[0, h] + self.fin[1, h]
    def drain(self):
        for i in range(6): self.c[i].wait_send()

def rs_col_kernel(p, o, relA, finA, relB, finB, qa, qb, relA2, finA2, relB2, finB2, ra, rb, recx, ss, rs, sx, rx):
    r, y, x, z, dev = place()
    yp, ym = dev(lax.rem(y+1,4),x,z), dev(lax.rem(y+3,4),x,z)
    zp, zm = dev(y,x,lax.rem(z+1,4)), dev(y,x,lax.rem(z+3,4))
    xd = dev(y,1-x,z)
    barrier([yp, ym, zp, zm, xd])
    A = pl.ds(0,256); Bc = pl.ds(256,256)
    a1 = RingRS(lambda k,h: p.at[k,h,:,:,A], y, yp, ym, relA, finA, ss.at[0], rs.at[0])
    b1 = RingRS(lambda k,h: p.at[:,h,k,:,Bc], z, zp, zm, relB, finB, ss.at[1], rs.at[1])
    a1.start(); b1.start(); a1.forward(); b1.forward()
    a1.finish(qa)
    a2 = RingRS(lambda k,h: qa.at[h,k], z, zp, zm, relA2, finA2, ss.at[2], rs.at[2])
    a2.start()
    b1.finish(qb)
    b2 = RingRS(lambda k,h: qb.at[h,k], y, yp, ym, relB2, finB2, ss.at[3], rs.at[3])
    b2.start()
    a2.forward(); b2.forward()
    a2.finish(ra)
    cxa = rc(ra.at[1-x], recx.at[0], sx.at[0], rx.at[0], xd); cxa.start()
    b2.finish(rb)
    cxb = rc(rb.at[1-x], recx.at[1], sx.at[1], rx.at[1], xd); cxb.start()
    cxa.wait_recv()
    o[:, 0:256] = ra[x] + recx[0]
    cxb.wait_recv()
    o[:, 256:512] = rb[x] + recx[1]
    for t in (a1, b1, a2, b2): t.drain()
    cxa.wait_send(); cxb.wait_send()

def rs_col(p, cid=1):
    S = 64
    f = jnp.float32
    V = lambda *s: pltpu.VMEM(s, f)
    return pl.pallas_call(rs_col_kernel, out_shape=jax.ShapeDtypeStruct((S,512), f), in_specs=[VM], out_specs=VM,
        scratch_shapes=[V(2,4,S,256), V(2,2,4,S,256), V(2,4,S,256), V(2,2,4,S,256), V(2,4,S,256), V(2,4,S,256),
            V(2,S,256), V(2,2,S,256), V(2,S,256), V(2,2,S,256), V(2,S,256), V(2,S,256), V(2,S,256),
            pltpu.SemaphoreType.DMA((4,6)), pltpu.SemaphoreType.DMA((4,6)), pltpu.SemaphoreType.DMA((2,)), pltpu.SemaphoreType.DMA((2,))],
        compiler_params=pltpu.CompilerParams(collective_id=cid, has_side_effects=True, vmem_limit_bytes=56*2**20), name="rs_col")(p.reshape(4,2,4,S,512))

class RingAG:
    def __init__(self, part, me, devp, devm, ssem, rsem):
        up = lax.rem(me+1, 4); dn = lax.rem(me+3, 4)
        far = lax.rem(me+2, 4)
        self.s = [rc(part(me,0), part(me,0), ssem.at[0], rsem.at[0], devp),
                  rc(part(me,1), part(me,1), ssem.at[1], rsem.at[1], devm),
                  rc(part(me,1), part(me,1), ssem.at[2], rsem.at[2], devp),
                  rc(part(me,0), part(me,0), ssem.at[3], rsem.at[3], devm),
                  rc(part(dn,0), part(dn,0), ssem.at[4], rsem.at[4], devp),
                  rc(part(up,1), part(up,1), ssem.at[5], rsem.at[5], devm)]
        self.r = [rc(part(dn,0), part(dn,0), ssem.at[0], rsem.at[0], devp),
                  rc(part(up,1), part(up,1), ssem.at[1], rsem.at[1], devm),
                  rc(part(dn,1), part(dn,1), ssem.at[2], rsem.at[2], devp),
                  rc(part(up,0), part(up,0), ssem.at[3], rsem.at[3], devm),
                  rc(part(far,0), part(far,0), ssem.at[4], rsem.at[4], devp),
                  rc(part(far,1), part(far,1), ssem.at[5], rsem.at[5], devm)]
    def start(self):
        for i in range(4): self.s[i].start()
    def forward(self):
        self.r[0].wait_recv(); self.s[4].start()
        self.r[1].wait_recv(); self.s[5].start()
    def finish(self):
        for i in (2,3,4,5): self.r[i].wait_recv()
    def drain(self):
        for i in range(6): self.s[i].wait_send()

def ag_col_kernel(p, o, ss, rs, sx, rx):
    r, y, x, z, dev = place()
    yp, ym = dev(lax.rem(y+1,4),x,z), dev(lax.rem(y+3,4),x,z)
    zp, zm = dev(y,x,lax.rem(z+1,4)), dev(y,x,lax.rem(z+3,4))
    xd = dev(y,1-x,z)
    o[y,x,z] = p[...]
    barrier([yp, ym, zp, zm, xd])
    cx = rc(o.at[y,x,z], o.at[y,x,z], sx.at[0], rx.at[0], xd)
    cxr = rc(o.at[y,1-x,z], o.at[y,1-x,z], sx.at[0], rx.at[0], xd)
    cx.start()
    A = pl.ds(0,256); Bc = pl.ds(256,256)
    cxr.wait_recv()
    a1 = RingAG(lambda k,h: o.at[y,h,k,:,A], z, zp, zm, ss.at[0], rs.at[0])
    b1 = RingAG(lambda k,h: o.at[k,h,z,:,Bc], y, yp, ym, ss.at[1], rs.at[1])
    a1.start(); b1.start()
    a1.forward(); b1.forward()
    a1.finish()
    a2 = RingAG(lambda k,h: o.at[k,h,:,:,A], y, yp, ym, ss.at[2], rs.at[2])
    a2.start()
    b1.finish()
    b2 = RingAG(lambda k,h: o.at[:,h,k,:,Bc], z, zp, zm, ss.at[3], rs.at[3])
    b2.start()
    a2.forward(); b2.forward()
    a2.finish(); b2.finish()
    for t in (a1,b1,a2,b2): t.drain()
    cx.wait_send()

def ag_col(p, cid=2):
    S = 64
    o = pl.pallas_call(ag_col_kernel, out_shape=jax.ShapeDtypeStruct((4,2,4,S,512), jnp.float32), in_specs=[VM], out_specs=VM,
        scratch_shapes=[pltpu.SemaphoreType.DMA((4,6)), pltpu.SemaphoreType.DMA((4,6)), pltpu.SemaphoreType.DMA((1,)), pltpu.SemaphoreType.DMA((1,))],
        compiler_params=pltpu.CompilerParams(collective_id=cid, has_side_effects=True, vmem_limit_bytes=56*2**20), name="ag_col")(p)
    return o.reshape(32*S, 512)

def rs_row_kernel(p, o, rec1, q, rec2, s1, r1, s2, r2):
    r = lax.axis_index("row"); c = lax.axis_index("col")
    h = lax.div(r,2); k = lax.rem(r,2)
    other = (h*2 + 1-k, c); far = ((1-h)*2 + k, c)
    barrier([other, far])
    cs = [rc(p.at[1-h, 1-k], rec1.at[0], s1.at[0], r1.at[0], other), rc(p.at[h, 1-k], rec1.at[1], s1.at[1], r1.at[1], other)]
    for t in cs: t.start()
    cs[0].wait_recv()
    q[...] = p[1-h, k] + rec1[0]
    c2 = rc(q, rec2, s2.at[0], r2.at[0], far); c2.start()
    cs[1].wait_recv()
    o[...] = p[h, k] + rec1[1]
    c2.wait_recv()
    o[...] = o[...] + rec2[...]
    for t in cs: t.wait_send()
    c2.wait_send()

def rs_row(p, cid=3):
    n = p.shape[0]//4
    V = lambda *s: pltpu.VMEM(s, jnp.float32)
    D = pltpu.SemaphoreType.DMA
    return pl.pallas_call(rs_row_kernel, out_shape=jax.ShapeDtypeStruct((n,512), jnp.float32), in_specs=[VM], out_specs=VM,
        scratch_shapes=[V(2,n,512), V(n,512), V(n,512), D((2,)), D((2,)), D((1,)), D((1,))],
        compiler_params=pltpu.CompilerParams(collective_id=cid, has_side_effects=True, vmem_limit_bytes=56*2**20), name="rs_row")(p.reshape(2,2,n,512))

def ag_row_kernel(p, o, s1, r1, s2, r2):
    r = lax.axis_index("row"); c = lax.axis_index("col")
    h = lax.div(r,2); k = lax.rem(r,2)
    other = (h*2 + 1-k, c); far = ((1-h)*2 + k, c)
    o[h, k] = p[...]
    barrier([other, far])
    cf = rc(o.at[h,k], o.at[h,k], s1.at[0], r1.at[0], far)
    cfr = rc(o.at[1-h,k], o.at[1-h,k], s1.at[0], r1.at[0], far)
    cf.start()
    co = rc(o.at[h,k], o.at[h,k], s2.at[0], r2.at[0], other)
    cor = rc(o.at[h,1-k], o.at[h,1-k], s2.at[0], r2.at[0], other)
    co.start()
    cfr.wait_recv()
    co2 = rc(o.at[1-h,k], o.at[1-h,k], s2.at[1], r2.at[1], other)
    co2r = rc(o.at[1-h,1-k], o.at[1-h,1-k], s2.at[1], r2.at[1], other)
    co2.start()
    cor.wait_recv(); co2r.wait_recv()
    cf.wait_send(); co.wait_send(); co2.wait_send()

def ag_row(p, cid=4):
    n = p.shape[0]
    D = pltpu.SemaphoreType.DMA
    o = pl.pallas_call(ag_row_kernel, out_shape=jax.ShapeDtypeStruct((2,2,n,512), jnp.float32), in_specs=[VM], out_specs=VM,
        scratch_shapes=[D((1,)), D((1,)), D((2,)), D((2,))],
        compiler_params=pltpu.CompilerParams(collective_id=cid, has_side_effects=True, vmem_limit_bytes=56*2**20), name="ag_row")(p)
    return o.reshape(4*n, 512)
HI = lax.Precision.HIGHEST
PAIRS = [(i, k) for i in range(4) for k in range(i, 4)]
GROUPS = [(0, 2, "zyx"), (2, 2, "yxz"), (4, 1, "xzy")]

def gram_kernel(s, o, g, crec, *rest):
    bufs, (ssc, rsc, ss, rs) = rest[:-4], rest[-4:]
    r = lax.axis_index("row"); c = lax.axis_index("col")
    xh = lax.div(r, 2); k = lax.rem(r, 2)
    y = lax.div(c, 8); xl = lax.rem(lax.div(c, 4), 2); z = lax.rem(c, 4)
    x = xh*2 + xl
    at = {"x": x, "y": y, "z": z}
    def dev(q):
        return (lax.div(q["x"], 2)*2 + k, q["y"]*8 + lax.rem(q["x"], 2)*4 + q["z"])
    def peer(ax, d):
        q = dict(at); q[ax] = lax.rem(at[ax]+d, 4)
        return q[ax], dev(q)
    other = (xh*2 + 1-k, c)
    barrier([other] + [peer(ax, d)[1] for ax in "xyz" for d in (1,2,3)])
    n = 0
    for i in range(4):
        w = jnp.einsum("ni,nk->ik", s[:, i*128:(i+1)*128], s[:, i*128:], precision=HI, preferred_element_type=jnp.float32)
        for j in range(i, 4):
            g[n//5, n%5] = w[:, (j-i)*128:(j-i+1)*128]
            n += 1
    cc = rc(g.at[1-k], crec, ssc.at[0], rsc.at[0], other)
    cc.start()
    cc.wait_recv()
    g[k] = g[k] + crec[...]
    sends = []
    def exchange(src, buf, ax, sem):
        me = at[ax]
        cs = []
        for d in (1, 3, 2):
            to, dv = peer(ax, d)
            t = rc(src(to), buf.at[me], ss.at[sem, d], rs.at[sem, me], dv)
            t.start(); cs.append(t)
        sends.extend(cs)
        def done():
            for d in (1, 3, 2):
                fr, dv = peer(ax, d)
                rc(src(fr), buf.at[fr], ss.at[sem, d], rs.at[sem, fr], dv).wait_recv()
        return done
    def gather(view, ax, sem):
        me = at[ax]
        cs = []
        for d in (1, 3, 2):
            to, dv = peer(ax, d)
            t = rc(view(me), view(me), ss.at[sem, d], rs.at[sem, me], dv)
            t.start(); cs.append(t)
        sends.extend(cs)
        def done():
            for d in (1, 3, 2):
                fr, dv = peer(ax, d)
                rc(view(fr), view(fr), ss.at[sem, d], rs.at[sem, fr], dv).wait_recv()
        return done
    G3 = range(3)

    b1 = [bufs[3*i] for i in G3]; b2 = [bufs[3*i+1] for i in G3]; b3 = [bufs[3*i+2] for i in G3]
    f = []
    for i, (b0, nb, od) in enumerate(GROUPS):
        f.append(exchange(lambda q, b0=b0, nb=nb: g.at[k, pl.ds(b0, nb), pl.ds(pl.multiple_of(q*32, 32), 32)], b1[i], od[0], i*5))
    for i, (b0, nb, od) in enumerate(GROUPS):
        b1[i][at[od[0]]] = g[k, b0:b0+nb, pl.ds(pl.multiple_of(at[od[0]]*32, 32), 32)]
    f2 = []
    for i, (b0, nb, od) in enumerate(GROUPS):
        f[i]()
        b1[i][4] = (b1[i][0] + b1[i][1]) + (b1[i][2] + b1[i][3])
        f2.append(exchange(lambda q, i=i: b1[i].at[4, :, pl.ds(pl.multiple_of(q*8, 8), 8)], b2[i], od[1], i*5+1))
        b2[i][at[od[1]]] = b1[i][4, :, pl.ds(pl.multiple_of(at[od[1]]*8, 8), 8)]
    f3 = []
    for i, (b0, nb, od) in enumerate(GROUPS):
        f2[i]()
        b3[i][at[od[2]]] = (b2[i][0] + b2[i][1]) + (b2[i][2] + b2[i][3])
        f3.append(gather(lambda q, i=i: b3[i].at[q], od[2], i*5+2))
    f4 = []
    for i, (b0, nb, od) in enumerate(GROUPS):
        f3[i]()
        rows = lambda q, i=i, b0=b0, nb=nb, od=od: o.at[k, pl.ds(b0, nb), pl.ds(pl.multiple_of(at[od[0]]*32 + q*8, 8), 8)]
        rows(at[od[1]])[...] = (b3[i][0] + b3[i][1]) + (b3[i][2] + b3[i][3])
        f4.append(gather(rows, od[1], i*5+3))
    f5 = []
    for i, (b0, nb, od) in enumerate(GROUPS):
        f4[i]()
        f5.append(gather(lambda q, b0=b0, nb=nb: o.at[k, pl.ds(b0, nb), pl.ds(pl.multiple_of(q*32, 32), 32)], od[0], i*5+4))
    for t in f5: t()
    co = rc(o.at[k], o.at[k], ssc.at[1], rsc.at[1], other)
    co.start()
    rc(o.at[1-k], o.at[1-k], ssc.at[1], rsc.at[1], other).wait_recv()
    for t in sends: t.wait_send()
    cc.wait_send(); co.wait_send()

def gram_blocks(s, cid):
    V = lambda *sh: pltpu.VMEM(sh, jnp.float32)
    D = pltpu.SemaphoreType.DMA
    bufs = []
    for b0, nb, od in GROUPS:
        bufs += [V(5, nb, 32, 128), V(4, nb, 8, 128), V(4, nb, 8, 128)]
    return pl.pallas_call(gram_kernel, out_shape=jax.ShapeDtypeStruct((2,5,128,128), jnp.float32), in_specs=[VM], out_specs=VM,
        scratch_shapes=[V(2,5,128,128), V(5,128,128)] + bufs + [D((2,)), D((2,)), D((15,4)), D((15,4))],
        compiler_params=pltpu.CompilerParams(collective_id=cid, has_side_effects=True, vmem_limit_bytes=56*2**20), name="gram")(s)
HI = lax.Precision.HIGHEST
B = 128

def mm(a, b):
    return jnp.dot(a, b, precision=HI, preferred_element_type=jnp.float32)

def leaf_inverse(a):
    n = B // 8
    lane = lax.broadcasted_iota(jnp.int32, (1, B), 1)
    sub = lax.broadcasted_iota(jnp.int32, (8, B), 0)
    lane8 = lax.broadcasted_iota(jnp.int32, (8, B), 1)
    ch = [a[8*t:8*t+8, :] for t in range(n)]
    drow = jnp.zeros((8, B), jnp.float32)
    for t in range(n):
        drow = drow + jnp.where(lane8 == sub + 8*t, ch[t], 0.0)
    srow = lax.rsqrt(jnp.sum(drow, axis=0, keepdims=True))
    srow8 = jnp.broadcast_to(srow, (8, B))
    for t in range(n):
        scol = jnp.sum(jnp.where(lane8 == sub + 8*t, srow8, 0.0), axis=1, keepdims=True)
        ch[t] = ch[t] * srow8 * scol
    for j in range(0, B, 4):
        t0, s = divmod(j, 8)
        c = [jnp.broadcast_to(ch[t0][:, j+b:j+b+1], (8, B)) for b in range(4)]
        pv = lambda i, k: c[k][s+i:s+i+1]
        piv = [lane == j+b for b in range(4)]
        inpiv = (lane >= j) & (lane < j+4)
        R = [jnp.where(piv[b], 1.0, jnp.where(inpiv, 0.0, ch[t0][s+b:s+b+1, :])) for b in range(4)]
        p, q, d = pv(0, 0), pv(1, 0), pv(1, 1)
        det = p*d - q*q
        idet = 1.0 / det
        ip, iq, iD = d*idet, -q*idet, p*idet
        t00 = pv(2,0)*ip + pv(2,1)*iq; t01 = pv(2,0)*iq + pv(2,1)*iD
        t10 = pv(3,0)*ip + pv(3,1)*iq; t11 = pv(3,0)*iq + pv(3,1)*iD
        s00 = pv(2,2) - (t00*pv(2,0) + t01*pv(2,1))
        s10 = pv(3,2) - (t10*pv(2,0) + t11*pv(2,1))
        s11 = pv(3,3) - (t10*pv(3,0) + t11*pv(3,1))
        dets = s00*s11 - s10*s10
        idets = 1.0 / dets
        v0 = R[2] - (t00*R[0] + t01*R[1])
        v1 = R[3] - (t10*R[0] + t11*R[1])
        w2 = (s11*v0 - s10*v1) * idets
        w3 = (s00*v1 - s10*v0) * idets
        w0 = (ip*R[0] + iq*R[1]) - (t00*w2 + t10*w3)
        w1 = (iq*R[0] + iD*R[1]) - (t01*w2 + t11*w3)
        W = [jnp.broadcast_to(w, (8, B)) for w in (w0, w1, w2, w3)]
        ipp = 1.0 / p; iss = 1.0 / s00
        F = [R[0]*lax.rsqrt(p), (R[1] - (q*ipp)*R[0])*lax.rsqrt(det*ipp), v0*lax.rsqrt(s00), (v1 - (s10*iss)*v0)*lax.rsqrt(dets*iss)]
        inpiv8 = (lane8 >= j) & (lane8 < j+4)
        for t in range(t0, n):
            if t == t0:
                m = [jnp.where(sub > s+3, c[b], 0.0) for b in range(4)]
            else:
                m = [jnp.broadcast_to(ch[t][:, j+b:j+b+1], (8, B)) for b in range(4)]
            u = (m[0]*W[0] + m[1]*W[1]) + (m[2]*W[2] + m[3]*W[3])
            ch[t] = jnp.where(inpiv8, 0.0, ch[t]) - u
            if t == t0:
                for b in range(4):
                    ch[t] = jnp.where(sub == s+b, jnp.broadcast_to(jnp.where(lane <= j+b, F[b], 0.0), (8, B)), ch[t])

    return jnp.concatenate([x * srow8 for x in ch], 0)

def chol_kernel(g_ref, x_ref):
    n = 0
    for i in range(4):
        for k in range(4):
            if k >= i:
                x_ref[i*B:(i+1)*B, k*B:(k+1)*B] = g_ref[n]
                n += 1
            else:
                x_ref[i*B:(i+1)*B, k*B:(k+1)*B] = jnp.zeros((B, B), jnp.float32)
    for J in range(4):
        lo, hi = J*B, (J+1)*B
        x = leaf_inverse(x_ref[lo:hi, lo:hi])
        x_ref[lo:hi, lo:hi] = x
        if J > 0:
            x_ref[lo:hi, 0:lo] = mm(x, x_ref[lo:hi, 0:lo])
        if J < 3:
            right = mm(x, x_ref[lo:hi, hi:])
            rt = right.T
            x_ref[lo:hi, hi:] = right
            x_ref[hi:, hi:] = x_ref[hi:, hi:] - mm(rt, right)
            left = mm(rt, x_ref[lo:hi, 0:hi])
            if J > 0:
                x_ref[hi:, 0:lo] = x_ref[hi:, 0:lo] - left[:, 0:lo]
            x_ref[hi:, lo:hi] = -left[:, lo:hi]
            x_ref[lo:hi, hi:] = jnp.zeros_like(right)

def chol_inverse(g):
    return pl.pallas_call(chol_kernel, out_shape=jax.ShapeDtypeStruct((4*B, 4*B), jnp.float32),
        in_specs=[pl.BlockSpec(memory_space=pltpu.VMEM)], out_specs=pl.BlockSpec(memory_space=pltpu.VMEM),
        compiler_params=pltpu.CompilerParams(vmem_limit_bytes=48*2**20), name="chol")(g)

def chol_load(g, x_ref):
    n = 0
    for i in range(4):
        for k in range(4):
            if k >= i:
                x_ref[i*B:(i+1)*B, k*B:(k+1)*B] = g[n]
                n += 1
            else:
                x_ref[i*B:(i+1)*B, k*B:(k+1)*B] = jnp.zeros((B, B), jnp.float32)

def chol_steps(g, x_ref):
    chol_load(g, x_ref)
    for J in range(4):
        lo, hi = J*B, (J+1)*B
        x = leaf_inverse(x_ref[lo:hi, lo:hi])
        x_ref[lo:hi, lo:hi] = x
        if J > 0:
            x_ref[lo:hi, 0:lo] = mm(x, x_ref[lo:hi, 0:lo])
        if J < 3:
            right = mm(x, x_ref[lo:hi, hi:])
            rt = right.T
            x_ref[lo:hi, hi:] = right
            x_ref[hi:, hi:] = x_ref[hi:, hi:] - mm(rt, right)
            left = mm(rt, x_ref[lo:hi, 0:hi])
            if J > 0:
                x_ref[hi:, 0:lo] = x_ref[hi:, 0:lo] - left[:, 0:lo]
            x_ref[hi:, lo:hi] = -left[:, lo:hi]
            x_ref[lo:hi, hi:] = jnp.zeros_like(right)
        yield

def run(gen):
    for _ in gen:
        pass

def alternate(first, *others):
    gens = [first, *others]
    while gens:
        for t in list(gens):
            try:
                next(t)
            except StopIteration:
                gens.remove(t)

def mesh_place():
    r = lax.axis_index("row"); c = lax.axis_index("col")
    q = {"xh": lax.div(r, 2), "core": lax.rem(r, 2), "y": lax.div(c, 8), "xl": lax.rem(lax.div(c, 4), 2), "z": lax.rem(c, 4)}
    q["x"] = q["xh"]*2 + q["xl"]
    return r, c, q

def col_neighbours(r, q):
    def dev(y, x, z):
        return (r, y*8 + x*4 + z)
    y, x, z = q["y"], q["xl"], q["z"]
    return {"yp": dev(lax.rem(y+1,4),x,z), "ym": dev(lax.rem(y+3,4),x,z), "zp": dev(y,x,lax.rem(z+1,4)), "zm": dev(y,x,lax.rem(z+3,4)), "xd": dev(y,1-x,z)}

def row_neighbours(c, q):
    h, k = q["xh"], q["core"]
    return {"other": (h*2 + 1-k, c), "far": ((1-h)*2 + k, c)}

def axis_peer(q, ax, d):
    t = dict(q); t[ax] = lax.rem(q[ax]+d, 4)
    return t[ax], (lax.div(t["x"], 2)*2 + t["core"], t["y"]*8 + lax.rem(t["x"], 2)*4 + t["z"])

def gram_devices(c, q):
    return [row_neighbours(c, q)["other"]] + [axis_peer(q, ax, d)[1] for ax in "xyz" for d in (1, 2, 3)]

def gram_scratch():
    V = lambda *sh: pltpu.VMEM(sh, jnp.float32)
    D = pltpu.SemaphoreType.DMA
    bufs = [V(2,5,128,128), V(5,128,128)]
    for b0, nb, od in GROUPS:
        bufs += [V(5, nb, 32, 128), V(4, nb, 8, 128), V(4, nb, 8, 128)]
    return bufs + [D((2,)), D((2,)), D((15,4)), D((15,4))]
NGRAM = 15

def gram_steps(s, o, c, q, scr):
    g, crec, bufs, (ssc, rsc, ss, rs) = scr[0], scr[1], scr[2:11], scr[11:]
    k = q["core"]; at = q
    other = row_neighbours(c, q)["other"]
    n = 0
    for i in range(4):
        w = jnp.einsum("ni,nk->ik", s[:, i*128:(i+1)*128], s[:, i*128:], precision=HI, preferred_element_type=jnp.float32)
        for j in range(i, 4):
            g[n//5, n%5] = w[:, (j-i)*128:(j-i+1)*128]
            n += 1
    cc = rc(g.at[1-k], crec, ssc.at[0], rsc.at[0], other)
    cc.start()
    yield
    cc.wait_recv()
    g[k] = g[k] + crec[...]
    sends = []
    def exchange(src, buf, ax, sem):
        me = at[ax]
        for d in (1, 3, 2):
            to, dv = axis_peer(q, ax, d)
            t = rc(src(to), buf.at[me], ss.at[sem, d], rs.at[sem, me], dv)
            t.start(); sends.append(t)
        def done():
            for d in (1, 3, 2):
                fr, dv = axis_peer(q, ax, d)
                rc(src(fr), buf.at[fr], ss.at[sem, d], rs.at[sem, fr], dv).wait_recv()
        return done
    def gather(view, ax, sem):
        me = at[ax]
        for d in (1, 3, 2):
            to, dv = axis_peer(q, ax, d)
            t = rc(view(me), view(me), ss.at[sem, d], rs.at[sem, me], dv)
            t.start(); sends.append(t)
        def done():
            for d in (1, 3, 2):
                fr, dv = axis_peer(q, ax, d)
                rc(view(fr), view(fr), ss.at[sem, d], rs.at[sem, fr], dv).wait_recv()
        return done
    b1 = [bufs[3*i] for i in range(3)]; b2 = [bufs[3*i+1] for i in range(3)]; b3 = [bufs[3*i+2] for i in range(3)]
    m32 = lambda i: pl.ds(pl.multiple_of(i*32, 32), 32)
    m8 = lambda i: pl.ds(pl.multiple_of(i*8, 8), 8)
    f = []
    for i, (b0, nb, od) in enumerate(GROUPS):
        f.append(exchange(lambda t, b0=b0, nb=nb: g.at[k, pl.ds(b0, nb), m32(t)], b1[i], od[0], i*5))
    for i, (b0, nb, od) in enumerate(GROUPS):
        b1[i][at[od[0]]] = g[k, b0:b0+nb, m32(at[od[0]])]
    yield
    f2 = []
    for i, (b0, nb, od) in enumerate(GROUPS):
        f[i]()
        b1[i][4] = (b1[i][0] + b1[i][1]) + (b1[i][2] + b1[i][3])
        f2.append(exchange(lambda t, i=i: b1[i].at[4, :, m8(t)], b2[i], od[1], i*5+1))
        b2[i][at[od[1]]] = b1[i][4, :, m8(at[od[1]])]
    yield
    f3 = []
    for i, (b0, nb, od) in enumerate(GROUPS):
        f2[i]()
        b3[i][at[od[2]]] = (b2[i][0] + b2[i][1]) + (b2[i][2] + b2[i][3])
        f3.append(gather(lambda t, i=i: b3[i].at[t], od[2], i*5+2))
    yield
    f4 = []
    for i, (b0, nb, od) in enumerate(GROUPS):
        f3[i]()
        rows = lambda t, b0=b0, nb=nb, od=od: o.at[k, pl.ds(b0, nb), pl.ds(pl.multiple_of(at[od[0]]*32 + t*8, 8), 8)]
        rows(at[od[1]])[...] = (b3[i][0] + b3[i][1]) + (b3[i][2] + b3[i][3])
        f4.append(gather(rows, od[1], i*5+3))
    yield
    f5 = []
    for i, (b0, nb, od) in enumerate(GROUPS):
        f4[i]()
        f5.append(gather(lambda t, b0=b0, nb=nb: o.at[k, pl.ds(b0, nb), m32(t)], od[0], i*5+4))
    yield
    for t in f5: t()
    co = rc(o.at[k], o.at[k], ssc.at[1], rsc.at[1], other)
    co.start()
    yield
    rc(o.at[1-k], o.at[1-k], ssc.at[1], rsc.at[1], other).wait_recv()
    for t in sends: t.wait_send()
    cc.wait_send(); co.wait_send()

A = pl.ds(0, 256); Bc = pl.ds(256, 256)

def rs_scratch():
    S = 64
    V = lambda *s: pltpu.VMEM(s, jnp.float32)
    D = pltpu.SemaphoreType.DMA
    return [V(2,4,S,256), V(2,2,4,S,256), V(2,4,S,256), V(2,2,4,S,256), V(2,4,S,256), V(2,4,S,256),
            V(2,S,256), V(2,2,S,256), V(2,S,256), V(2,2,S,256), V(2,S,256), V(2,S,256), V(2,S,256),
            D((4,6)), D((4,6)), D((2,)), D((2,))]

def rs_steps(p, o, q, nb, scr):
    relA, finA, relB, finB, qa, qb, relA2, finA2, relB2, finB2, ra, rb, recx, ss, rs, sx, rx = scr
    y, x, z = q["y"], q["xl"], q["z"]
    yp, ym, zp, zm, xd = nb["yp"], nb["ym"], nb["zp"], nb["zm"], nb["xd"]
    a1 = RingRS(lambda k,h: p.at[k,h,:,:,A], y, yp, ym, relA, finA, ss.at[0], rs.at[0])
    b1 = RingRS(lambda k,h: p.at[:,h,k,:,Bc], z, zp, zm, relB, finB, ss.at[1], rs.at[1])
    a1.start(); b1.start()
    yield
    a1.forward(); b1.forward()
    yield
    a1.finish(qa)
    a2 = RingRS(lambda k,h: qa.at[h,k], z, zp, zm, relA2, finA2, ss.at[2], rs.at[2])
    a2.start()
    b1.finish(qb)
    b2 = RingRS(lambda k,h: qb.at[h,k], y, yp, ym, relB2, finB2, ss.at[3], rs.at[3])
    b2.start()
    a2.forward(); b2.forward()
    yield
    a2.finish(ra)
    cxa = rc(ra.at[1-x], recx.at[0], sx.at[0], rx.at[0], xd); cxa.start()
    b2.finish(rb)
    cxb = rc(rb.at[1-x], recx.at[1], sx.at[1], rx.at[1], xd); cxb.start()
    cxa.wait_recv()
    o[:, 0:256] = ra[x] + recx[0]
    cxb.wait_recv()
    o[:, 256:512] = rb[x] + recx[1]
    for t in (a1, b1, a2, b2): t.drain()
    cxa.wait_send(); cxb.wait_send()

def ag_scratch():
    D = pltpu.SemaphoreType.DMA
    return [D((4,6)), D((4,6)), D((1,)), D((1,))]

def ag_steps(o, q, nb, scr):
    ss, rs, sx, rx = scr
    y, x, z = q["y"], q["xl"], q["z"]
    yp, ym, zp, zm, xd = nb["yp"], nb["ym"], nb["zp"], nb["zm"], nb["xd"]
    cx = rc(o.at[y,x,z], o.at[y,x,z], sx.at[0], rx.at[0], xd)
    cxr = rc(o.at[y,1-x,z], o.at[y,1-x,z], sx.at[0], rx.at[0], xd)
    cx.start()
    yield
    cxr.wait_recv()
    a1 = RingAG(lambda k,h: o.at[y,h,k,:,A], z, zp, zm, ss.at[0], rs.at[0])
    b1 = RingAG(lambda k,h: o.at[k,h,z,:,Bc], y, yp, ym, ss.at[1], rs.at[1])
    a1.start(); b1.start()
    yield
    a1.forward(); b1.forward()
    yield
    a1.finish()
    a2 = RingAG(lambda k,h: o.at[k,h,:,:,A], y, yp, ym, ss.at[2], rs.at[2])
    a2.start()
    b1.finish()
    b2 = RingAG(lambda k,h: o.at[:,h,k,:,Bc], z, zp, zm, ss.at[3], rs.at[3])
    b2.start()
    yield
    a2.forward(); b2.forward()
    yield
    a2.finish(); b2.finish()
    for t in (a1,b1,a2,b2): t.drain()
    cx.wait_send()

def row_rs_scratch(n):
    V = lambda *s: pltpu.VMEM(s, jnp.float32)
    D = pltpu.SemaphoreType.DMA
    return [V(2,n,512), V(n,512), V(n,512), D((2,)), D((2,)), D((1,)), D((1,))]

def row_rs_steps(p, o, q, nb, scr):
    rec1, qf, rec2, s1, r1, s2, r2 = scr
    h, k = q["xh"], q["core"]
    cs = [rc(p.at[1-h, 1-k], rec1.at[0], s1.at[0], r1.at[0], nb["other"]), rc(p.at[h, 1-k], rec1.at[1], s1.at[1], r1.at[1], nb["other"])]
    for t in cs: t.start()
    cs[0].wait_recv()
    qf[...] = p[1-h, k] + rec1[0]
    c2 = rc(qf, rec2, s2.at[0], r2.at[0], nb["far"]); c2.start()
    cs[1].wait_recv()
    o[...] = p[h, k] + rec1[1]
    yield
    c2.wait_recv()
    o[...] = o[...] + rec2[...]
    for t in cs: t.wait_send()
    c2.wait_send()

def row_ag_scratch():
    D = pltpu.SemaphoreType.DMA
    return [D((1,)), D((1,)), D((2,)), D((2,))]

def row_ag_steps(o, q, nb, scr):
    s1, r1, s2, r2 = scr
    h, k = q["xh"], q["core"]
    cf = rc(o.at[h,k], o.at[h,k], s1.at[0], r1.at[0], nb["far"])
    cfr = rc(o.at[1-h,k], o.at[1-h,k], s1.at[0], r1.at[0], nb["far"])
    cf.start()
    co = rc(o.at[h,k], o.at[h,k], s2.at[0], r2.at[0], nb["other"])
    cor = rc(o.at[h,1-k], o.at[h,1-k], s2.at[0], r2.at[0], nb["other"])
    co.start()
    yield
    cor.wait_recv()
    yield
    cfr.wait_recv()
    co2 = rc(o.at[1-h,k], o.at[1-h,k], s2.at[1], r2.at[1], nb["other"])
    co2r = rc(o.at[1-h,1-k], o.at[1-h,1-k], s2.at[1], r2.at[1], nb["other"])
    co2.start()
    yield
    co2r.wait_recv()
    cf.wait_send(); co.wait_send(); co2.wait_send()


def call(kernel, name, cid, outs, scratch, *args):
    return pl.pallas_call(kernel, out_shape=[jax.ShapeDtypeStruct(s, jnp.float32) for s in outs],
        in_specs=[VM]*len(args), out_specs=[VM]*len(outs), scratch_shapes=scratch,
        compiler_params=pltpu.CompilerParams(collective_id=cid, has_side_effects=True, vmem_limit_bytes=60*2**20), name=name)(*args)

def gather_gram_kernel(p, o, gb, *scr):
    r, c, q = mesh_place()
    nb = col_neighbours(r, q)
    o[q["y"], q["xl"], q["z"]] = p[...]
    barrier(list(nb.values()) + gram_devices(c, q))
    alternate(ag_steps(o, q, nb, scr[NGRAM:]), gram_steps(p, gb, c, q, scr[:NGRAM]))

def gather_gram(own):
    o, g = call(gather_gram_kernel, "gather_gram", 1, [(4,2,4,64,512), (2,5,B,B)], gram_scratch() + ag_scratch(), own)
    return o.reshape(2048, 512), g

def row_sum_chol_kernel(p, g, o, x, *scr):
    r, c, q = mesh_place()
    nb = row_neighbours(c, q)
    barrier(list(nb.values()))
    alternate(row_rs_steps(p, o, q, nb, scr), chol_steps_once(g, x))

def chol_steps_once(g, x):
    run(chol_steps(g, x))
    yield

def row_sum_chol(w, g):
    n = w.shape[0]//4
    return call(row_sum_chol_kernel, "row_sum_chol", 2, [(n, 512), (512, 512)], row_rs_scratch(n), w.reshape(2,2,n,512), g.reshape(10,B,B))

def apply_t(rows, x):
    return lax.dot_general(rows, x, (((1,), (1,)), ((), ())), precision=HI, preferred_element_type=jnp.float32)

def norm_gather_kernel(p, x, o, gb, own, *scr):
    r, c, q = mesh_place()
    nb = row_neighbours(c, q)
    own[...] = apply_t(p[...], x[...])
    o[q["xh"], q["core"]] = own[...]
    barrier([nb["far"]] + gram_devices(c, q))
    alternate(row_ag_steps(o, q, nb, scr[NGRAM:]), gram_steps(own, gb, c, q, scr[:NGRAM]))

def norm_gather(raw, x):
    n = raw.shape[0]
    o, g = call(norm_gather_kernel, "norm_gather", 3, [(2,2,n,512), (2,5,B,B)], [pltpu.VMEM((n,512), jnp.float32)] + gram_scratch() + row_ag_scratch(), raw, x)
    return o.reshape(4*n, 512), g

def col_sum_kernel(p, o, *scr):
    r, c, q = mesh_place()
    nb = col_neighbours(r, q)
    barrier(list(nb.values()))
    run(rs_steps(p, o, q, nb, scr))

def col_sum(p):
    return call(col_sum_kernel, "col_sum", 4, [(64,512)], rs_scratch(), p.reshape(4,2,4,64,512))[0]

def col_sum_chol_kernel(p, g, o, x, *scr):
    r, c, q = mesh_place()
    nb = col_neighbours(r, q)
    barrier(list(nb.values()))
    rsg = rs_steps(p, o, q, nb, scr); ch = chol_steps(g, x)
    next(rsg); next(ch)
    next(rsg); next(ch); next(ch)
    next(rsg); next(ch)
    run(rsg); run(ch)

def col_sum_chol(p, g):
    return call(col_sum_chol_kernel, "col_sum_chol", 5, [(64,512), (512,512)], rs_scratch(), p.reshape(4,2,4,64,512), g.reshape(10,B,B))

def last_kernel(p, x2, o, own, gb, x3, *scr):
    r, c, q = mesh_place()
    own[...] = apply_t(p[...], x2[...])
    barrier(gram_devices(c, q))
    run(gram_steps(own, gb, c, q, scr))
    run(chol_steps(Blocks(gb), x3))
    o[...] = SCALE * apply_t(own[...], x3[...])

class Blocks:
    def __init__(self, ref): self.ref = ref
    def __getitem__(self, n): return self.ref[n//5, n%5]

SCALE = float(8192.0 ** 0.5)

def last(raw, x2):
    V = lambda *s: pltpu.VMEM(s, jnp.float32)
    return call(last_kernel, "last", 6, [(64,512)], [V(64,512), V(2,5,B,B), V(512,512)] + gram_scratch(), raw, x2)[0]
def shards(adjusted_weight, base_weight, test_matrix):
    delta = adjusted_weight.astype(jnp.float32) - base_weight.astype(jnp.float32)
    own = col_sum(mm(delta, test_matrix))
    sketch, g1 = gather_gram(own)
    raw, x1 = row_sum_chol(jnp.einsum("mn,mk->nk", delta, sketch, precision=HI, preferred_element_type=jnp.float32), g1)
    cosketch, g2 = norm_gather(raw, x1)
    raw, x2 = col_sum_chol(mm(delta, cosketch), g2)
    return last(raw, x2)


def solution(mesh):
    return jax.shard_map(
        shards,
        mesh=mesh,
        in_specs=(P("row", "col"), P("row", "col"), P("col", None)),
        out_specs=P(("row", "col"), None),
        check_vma=False,
    )
```

```python
import jax
import jax.numpy as jnp
from jax import lax
from jax.experimental import pallas as pl
from jax.experimental.pallas import tpu as pltpu
from jax.sharding import PartitionSpec as P

MESH = pl.DeviceIdType.MESH
VM = pl.BlockSpec(memory_space=pltpu.VMEM)

def place():
    r = lax.axis_index("row"); c = lax.axis_index("col")
    y = lax.div(c, 8); x = lax.rem(lax.div(c, 4), 2); z = lax.rem(c, 4)
    def dev(yy, xx, zz):
        return (r, yy*8 + xx*4 + zz)
    return r, y, x, z, dev

def barrier(devs):
    sem = pltpu.get_barrier_semaphore()
    for d in devs:
        pl.semaphore_signal(sem, inc=1, device_id=d, device_id_type=MESH)
    pl.semaphore_wait(sem, len(devs))

def rc(src, dst, ssem, rsem, dev):
    return pltpu.make_async_remote_copy(src_ref=src, dst_ref=dst, send_sem=ssem, recv_sem=rsem, device_id=dev, device_id_type=MESH)

class RingRS:
    def __init__(self, part, me, devp, devm, relay, fin, ssem, rsem):
        self.part, self.me, self.devp, self.devm, self.relay, self.fin = part, me, devp, devm, relay, fin
        up = lax.rem(me+1, 4); dn = lax.rem(me+3, 4); far = lax.rem(me+2, 4)
        self.up, self.dn = up, dn
        self.c = [
            rc(part(far, 0), relay.at[0], ssem.at[0], rsem.at[0], devp),
            rc(part(far, 1), relay.at[1], ssem.at[1], rsem.at[1], devm),
            rc(part(up, 1), fin.at[0, 1], ssem.at[2], rsem.at[2], devp),
            rc(part(dn, 0), fin.at[1, 0], ssem.at[3], rsem.at[3], devm),
            rc(relay.at[0], fin.at[0, 0], ssem.at[4], rsem.at[4], devp),
            rc(relay.at[1], fin.at[1, 1], ssem.at[5], rsem.at[5], devm),
        ]
    def start(self):
        for i in range(4): self.c[i].start()
    def forward(self):
        self.c[0].wait_recv()
        self.relay[0] = self.relay[0] + self.part(self.up, 0)[...]
        self.c[4].start()
        self.c[1].wait_recv()
        self.relay[1] = self.relay[1] + self.part(self.dn, 1)[...]
        self.c[5].start()
    def finish(self, out):
        for i in (2, 3, 4, 5): self.c[i].wait_recv()
        for h in range(2):
            out[h] = self.part(self.me, h)[...] + self.fin[0, h] + self.fin[1, h]
    def drain(self):
        for i in range(6): self.c[i].wait_send()

def rs_col_kernel(p, o, relA, finA, relB, finB, qa, qb, relA2, finA2, relB2, finB2, ra, rb, recx, ss, rs, sx, rx):
    r, y, x, z, dev = place()
    yp, ym = dev(lax.rem(y+1,4),x,z), dev(lax.rem(y+3,4),x,z)
    zp, zm = dev(y,x,lax.rem(z+1,4)), dev(y,x,lax.rem(z+3,4))
    xd = dev(y,1-x,z)
    barrier([yp, ym, zp, zm, xd])
    A = pl.ds(0,256); Bc = pl.ds(256,256)
    a1 = RingRS(lambda k,h: p.at[k,h,:,:,A], y, yp, ym, relA, finA, ss.at[0], rs.at[0])
    b1 = RingRS(lambda k,h: p.at[:,h,k,:,Bc], z, zp, zm, relB, finB, ss.at[1], rs.at[1])
    a1.start(); b1.start(); a1.forward(); b1.forward()
    a1.finish(qa)
    a2 = RingRS(lambda k,h: qa.at[h,k], z, zp, zm, relA2, finA2, ss.at[2], rs.at[2])
    a2.start()
    b1.finish(qb)
    b2 = RingRS(lambda k,h: qb.at[h,k], y, yp, ym, relB2, finB2, ss.at[3], rs.at[3])
    b2.start()
    a2.forward(); b2.forward()
    a2.finish(ra)
    cxa = rc(ra.at[1-x], recx.at[0], sx.at[0], rx.at[0], xd); cxa.start()
    b2.finish(rb)
    cxb = rc(rb.at[1-x], recx.at[1], sx.at[1], rx.at[1], xd); cxb.start()
    cxa.wait_recv()
    o[:, 0:256] = ra[x] + recx[0]
    cxb.wait_recv()
    o[:, 256:512] = rb[x] + recx[1]
    for t in (a1, b1, a2, b2): t.drain()
    cxa.wait_send(); cxb.wait_send()

def rs_col(p, cid=1):
    S = 64
    f = jnp.float32
    V = lambda *s: pltpu.VMEM(s, f)
    return pl.pallas_call(rs_col_kernel, out_shape=jax.ShapeDtypeStruct((S,512), f), in_specs=[VM], out_specs=VM,
        scratch_shapes=[V(2,4,S,256), V(2,2,4,S,256), V(2,4,S,256), V(2,2,4,S,256), V(2,4,S,256), V(2,4,S,256),
            V(2,S,256), V(2,2,S,256), V(2,S,256), V(2,2,S,256), V(2,S,256), V(2,S,256), V(2,S,256),
            pltpu.SemaphoreType.DMA((4,6)), pltpu.SemaphoreType.DMA((4,6)), pltpu.SemaphoreType.DMA((2,)), pltpu.SemaphoreType.DMA((2,))],
        compiler_params=pltpu.CompilerParams(collective_id=cid, has_side_effects=True, vmem_limit_bytes=56*2**20), name="rs_col")(p.reshape(4,2,4,S,512))

class RingAG:
    def __init__(self, part, me, devp, devm, ssem, rsem):
        up = lax.rem(me+1, 4); dn = lax.rem(me+3, 4)
        far = lax.rem(me+2, 4)
        self.s = [rc(part(me,0), part(me,0), ssem.at[0], rsem.at[0], devp),
                  rc(part(me,1), part(me,1), ssem.at[1], rsem.at[1], devm),
                  rc(part(me,1), part(me,1), ssem.at[2], rsem.at[2], devp),
                  rc(part(me,0), part(me,0), ssem.at[3], rsem.at[3], devm),
                  rc(part(dn,0), part(dn,0), ssem.at[4], rsem.at[4], devp),
                  rc(part(up,1), part(up,1), ssem.at[5], rsem.at[5], devm)]
        self.r = [rc(part(dn,0), part(dn,0), ssem.at[0], rsem.at[0], devp),
                  rc(part(up,1), part(up,1), ssem.at[1], rsem.at[1], devm),
                  rc(part(dn,1), part(dn,1), ssem.at[2], rsem.at[2], devp),
                  rc(part(up,0), part(up,0), ssem.at[3], rsem.at[3], devm),
                  rc(part(far,0), part(far,0), ssem.at[4], rsem.at[4], devp),
                  rc(part(far,1), part(far,1), ssem.at[5], rsem.at[5], devm)]
    def start(self):
        for i in range(4): self.s[i].start()
    def forward(self):
        self.r[0].wait_recv(); self.s[4].start()
        self.r[1].wait_recv(); self.s[5].start()
    def finish(self):
        for i in (2,3,4,5): self.r[i].wait_recv()
    def drain(self):
        for i in range(6): self.s[i].wait_send()

def ag_col_kernel(p, o, ss, rs, sx, rx):
    r, y, x, z, dev = place()
    yp, ym = dev(lax.rem(y+1,4),x,z), dev(lax.rem(y+3,4),x,z)
    zp, zm = dev(y,x,lax.rem(z+1,4)), dev(y,x,lax.rem(z+3,4))
    xd = dev(y,1-x,z)
    o[y,x,z] = p[...]
    barrier([yp, ym, zp, zm, xd])
    cx = rc(o.at[y,x,z], o.at[y,x,z], sx.at[0], rx.at[0], xd)
    cxr = rc(o.at[y,1-x,z], o.at[y,1-x,z], sx.at[0], rx.at[0], xd)
    cx.start()
    A = pl.ds(0,256); Bc = pl.ds(256,256)
    cxr.wait_recv()
    a1 = RingAG(lambda k,h: o.at[y,h,k,:,A], z, zp, zm, ss.at[0], rs.at[0])
    b1 = RingAG(lambda k,h: o.at[k,h,z,:,Bc], y, yp, ym, ss.at[1], rs.at[1])
    a1.start(); b1.start()
    a1.forward(); b1.forward()
    a1.finish()
    a2 = RingAG(lambda k,h: o.at[k,h,:,:,A], y, yp, ym, ss.at[2], rs.at[2])
    a2.start()
    b1.finish()
    b2 = RingAG(lambda k,h: o.at[:,h,k,:,Bc], z, zp, zm, ss.at[3], rs.at[3])
    b2.start()
    a2.forward(); b2.forward()
    a2.finish(); b2.finish()
    for t in (a1,b1,a2,b2): t.drain()
    cx.wait_send()

def ag_col(p, cid=2):
    S = 64
    o = pl.pallas_call(ag_col_kernel, out_shape=jax.ShapeDtypeStruct((4,2,4,S,512), jnp.float32), in_specs=[VM], out_specs=VM,
        scratch_shapes=[pltpu.SemaphoreType.DMA((4,6)), pltpu.SemaphoreType.DMA((4,6)), pltpu.SemaphoreType.DMA((1,)), pltpu.SemaphoreType.DMA((1,))],
        compiler_params=pltpu.CompilerParams(collective_id=cid, has_side_effects=True, vmem_limit_bytes=56*2**20), name="ag_col")(p)
    return o.reshape(32*S, 512)

def rs_row_kernel(p, o, rec1, q, rec2, s1, r1, s2, r2):
    r = lax.axis_index("row"); c = lax.axis_index("col")
    h = lax.div(r,2); k = lax.rem(r,2)
    other = (h*2 + 1-k, c); far = ((1-h)*2 + k, c)
    barrier([other, far])
    cs = [rc(p.at[1-h, 1-k], rec1.at[0], s1.at[0], r1.at[0], other), rc(p.at[h, 1-k], rec1.at[1], s1.at[1], r1.at[1], other)]
    for t in cs: t.start()
    cs[0].wait_recv()
    q[...] = p[1-h, k] + rec1[0]
    c2 = rc(q, rec2, s2.at[0], r2.at[0], far); c2.start()
    cs[1].wait_recv()
    o[...] = p[h, k] + rec1[1]
    c2.wait_recv()
    o[...] = o[...] + rec2[...]
    for t in cs: t.wait_send()
    c2.wait_send()

def rs_row(p, cid=3):
    n = p.shape[0]//4
    V = lambda *s: pltpu.VMEM(s, jnp.float32)
    D = pltpu.SemaphoreType.DMA
    return pl.pallas_call(rs_row_kernel, out_shape=jax.ShapeDtypeStruct((n,512), jnp.float32), in_specs=[VM], out_specs=VM,
        scratch_shapes=[V(2,n,512), V(n,512), V(n,512), D((2,)), D((2,)), D((1,)), D((1,))],
        compiler_params=pltpu.CompilerParams(collective_id=cid, has_side_effects=True, vmem_limit_bytes=56*2**20), name="rs_row")(p.reshape(2,2,n,512))

def ag_row_kernel(p, o, s1, r1, s2, r2):
    r = lax.axis_index("row"); c = lax.axis_index("col")
    h = lax.div(r,2); k = lax.rem(r,2)
    other = (h*2 + 1-k, c); far = ((1-h)*2 + k, c)
    o[h, k] = p[...]
    barrier([other, far])
    cf = rc(o.at[h,k], o.at[h,k], s1.at[0], r1.at[0], far)
    cfr = rc(o.at[1-h,k], o.at[1-h,k], s1.at[0], r1.at[0], far)
    cf.start()
    co = rc(o.at[h,k], o.at[h,k], s2.at[0], r2.at[0], other)
    cor = rc(o.at[h,1-k], o.at[h,1-k], s2.at[0], r2.at[0], other)
    co.start()
    cfr.wait_recv()
    co2 = rc(o.at[1-h,k], o.at[1-h,k], s2.at[1], r2.at[1], other)
    co2r = rc(o.at[1-h,1-k], o.at[1-h,1-k], s2.at[1], r2.at[1], other)
    co2.start()
    cor.wait_recv(); co2r.wait_recv()
    cf.wait_send(); co.wait_send(); co2.wait_send()

def ag_row(p, cid=4):
    n = p.shape[0]
    D = pltpu.SemaphoreType.DMA
    o = pl.pallas_call(ag_row_kernel, out_shape=jax.ShapeDtypeStruct((2,2,n,512), jnp.float32), in_specs=[VM], out_specs=VM,
        scratch_shapes=[D((1,)), D((1,)), D((2,)), D((2,))],
        compiler_params=pltpu.CompilerParams(collective_id=cid, has_side_effects=True, vmem_limit_bytes=56*2**20), name="ag_row")(p)
    return o.reshape(4*n, 512)
HI = lax.Precision.HIGHEST
PAIRS = [(i, k) for i in range(4) for k in range(i, 4)]
GROUPS = [(0, 2, "zyx"), (2, 2, "yxz"), (4, 1, "xzy")]

def gram_kernel(s, o, g, crec, *rest):
    bufs, (ssc, rsc, ss, rs) = rest[:-4], rest[-4:]
    r = lax.axis_index("row"); c = lax.axis_index("col")
    xh = lax.div(r, 2); k = lax.rem(r, 2)
    y = lax.div(c, 8); xl = lax.rem(lax.div(c, 4), 2); z = lax.rem(c, 4)
    x = xh*2 + xl
    at = {"x": x, "y": y, "z": z}
    def dev(q):
        return (lax.div(q["x"], 2)*2 + k, q["y"]*8 + lax.rem(q["x"], 2)*4 + q["z"])
    def peer(ax, d):
        q = dict(at); q[ax] = lax.rem(at[ax]+d, 4)
        return q[ax], dev(q)
    other = (xh*2 + 1-k, c)
    barrier([other] + [peer(ax, d)[1] for ax in "xyz" for d in (1,2,3)])
    n = 0
    for i in range(4):
        w = jnp.einsum("ni,nk->ik", s[:, i*128:(i+1)*128], s[:, i*128:], precision=HI, preferred_element_type=jnp.float32)
        for j in range(i, 4):
            g[n//5, n%5] = w[:, (j-i)*128:(j-i+1)*128]
            n += 1
    cc = rc(g.at[1-k], crec, ssc.at[0], rsc.at[0], other)
    cc.start()
    cc.wait_recv()
    g[k] = g[k] + crec[...]
    sends = []
    def exchange(src, buf, ax, sem):
        me = at[ax]
        cs = []
        for d in (1, 3, 2):
            to, dv = peer(ax, d)
            t = rc(src(to), buf.at[me], ss.at[sem, d], rs.at[sem, me], dv)
            t.start(); cs.append(t)
        sends.extend(cs)
        def done():
            for d in (1, 3, 2):
                fr, dv = peer(ax, d)
                rc(src(fr), buf.at[fr], ss.at[sem, d], rs.at[sem, fr], dv).wait_recv()
        return done
    def gather(view, ax, sem):
        me = at[ax]
        cs = []
        for d in (1, 3, 2):
            to, dv = peer(ax, d)
            t = rc(view(me), view(me), ss.at[sem, d], rs.at[sem, me], dv)
            t.start(); cs.append(t)
        sends.extend(cs)
        def done():
            for d in (1, 3, 2):
                fr, dv = peer(ax, d)
                rc(view(fr), view(fr), ss.at[sem, d], rs.at[sem, fr], dv).wait_recv()
        return done
    G3 = range(3)

    b1 = [bufs[3*i] for i in G3]; b2 = [bufs[3*i+1] for i in G3]; b3 = [bufs[3*i+2] for i in G3]
    f = []
    for i, (b0, nb, od) in enumerate(GROUPS):
        f.append(exchange(lambda q, b0=b0, nb=nb: g.at[k, pl.ds(b0, nb), pl.ds(pl.multiple_of(q*32, 32), 32)], b1[i], od[0], i*5))
    for i, (b0, nb, od) in enumerate(GROUPS):
        b1[i][at[od[0]]] = g[k, b0:b0+nb, pl.ds(pl.multiple_of(at[od[0]]*32, 32), 32)]
    f2 = []
    for i, (b0, nb, od) in enumerate(GROUPS):
        f[i]()
        b1[i][4] = (b1[i][0] + b1[i][1]) + (b1[i][2] + b1[i][3])
        f2.append(exchange(lambda q, i=i: b1[i].at[4, :, pl.ds(pl.multiple_of(q*8, 8), 8)], b2[i], od[1], i*5+1))
        b2[i][at[od[1]]] = b1[i][4, :, pl.ds(pl.multiple_of(at[od[1]]*8, 8), 8)]
    f3 = []
    for i, (b0, nb, od) in enumerate(GROUPS):
        f2[i]()
        b3[i][at[od[2]]] = (b2[i][0] + b2[i][1]) + (b2[i][2] + b2[i][3])
        f3.append(gather(lambda q, i=i: b3[i].at[q], od[2], i*5+2))
    f4 = []
    for i, (b0, nb, od) in enumerate(GROUPS):
        f3[i]()
        rows = lambda q, i=i, b0=b0, nb=nb, od=od: o.at[k, pl.ds(b0, nb), pl.ds(pl.multiple_of(at[od[0]]*32 + q*8, 8), 8)]
        rows(at[od[1]])[...] = (b3[i][0] + b3[i][1]) + (b3[i][2] + b3[i][3])
        f4.append(gather(rows, od[1], i*5+3))
    f5 = []
    for i, (b0, nb, od) in enumerate(GROUPS):
        f4[i]()
        f5.append(gather(lambda q, b0=b0, nb=nb: o.at[k, pl.ds(b0, nb), pl.ds(pl.multiple_of(q*32, 32), 32)], od[0], i*5+4))
    for t in f5: t()
    co = rc(o.at[k], o.at[k], ssc.at[1], rsc.at[1], other)
    co.start()
    rc(o.at[1-k], o.at[1-k], ssc.at[1], rsc.at[1], other).wait_recv()
    for t in sends: t.wait_send()
    cc.wait_send(); co.wait_send()

def gram_blocks(s, cid):
    V = lambda *sh: pltpu.VMEM(sh, jnp.float32)
    D = pltpu.SemaphoreType.DMA
    bufs = []
    for b0, nb, od in GROUPS:
        bufs += [V(5, nb, 32, 128), V(4, nb, 8, 128), V(4, nb, 8, 128)]
    return pl.pallas_call(gram_kernel, out_shape=jax.ShapeDtypeStruct((2,5,128,128), jnp.float32), in_specs=[VM], out_specs=VM,
        scratch_shapes=[V(2,5,128,128), V(5,128,128)] + bufs + [D((2,)), D((2,)), D((15,4)), D((15,4))],
        compiler_params=pltpu.CompilerParams(collective_id=cid, has_side_effects=True, vmem_limit_bytes=56*2**20), name="gram")(s)
HI = lax.Precision.HIGHEST
B = 128

def mm(a, b):
    return jnp.dot(a, b, precision=HI, preferred_element_type=jnp.float32)

def leaf_inverse(a):
    n = B // 8
    lane = lax.broadcasted_iota(jnp.int32, (1, B), 1)
    sub = lax.broadcasted_iota(jnp.int32, (8, B), 0)
    lane8 = lax.broadcasted_iota(jnp.int32, (8, B), 1)
    ch = [a[8*t:8*t+8, :] for t in range(n)]
    drow = jnp.zeros((8, B), jnp.float32)
    for t in range(n):
        drow = drow + jnp.where(lane8 == sub + 8*t, ch[t], 0.0)
    srow = lax.rsqrt(jnp.sum(drow, axis=0, keepdims=True))
    srow8 = jnp.broadcast_to(srow, (8, B))
    for t in range(n):
        scol = jnp.sum(jnp.where(lane8 == sub + 8*t, srow8, 0.0), axis=1, keepdims=True)
        ch[t] = ch[t] * srow8 * scol
    for j in range(0, B, 4):
        t0, s = divmod(j, 8)
        c = [jnp.broadcast_to(ch[t0][:, j+b:j+b+1], (8, B)) for b in range(4)]
        pv = lambda i, k: c[k][s+i:s+i+1]
        piv = [lane == j+b for b in range(4)]
        inpiv = (lane >= j) & (lane < j+4)
        R = [jnp.where(piv[b], 1.0, jnp.where(inpiv, 0.0, ch[t0][s+b:s+b+1, :])) for b in range(4)]
        p, q, d = pv(0, 0), pv(1, 0), pv(1, 1)
        det = p*d - q*q
        idet = 1.0 / det
        ip, iq, iD = d*idet, -q*idet, p*idet
        t00 = pv(2,0)*ip + pv(2,1)*iq; t01 = pv(2,0)*iq + pv(2,1)*iD
        t10 = pv(3,0)*ip + pv(3,1)*iq; t11 = pv(3,0)*iq + pv(3,1)*iD
        s00 = pv(2,2) - (t00*pv(2,0) + t01*pv(2,1))
        s10 = pv(3,2) - (t10*pv(2,0) + t11*pv(2,1))
        s11 = pv(3,3) - (t10*pv(3,0) + t11*pv(3,1))
        dets = s00*s11 - s10*s10
        idets = 1.0 / dets
        v0 = R[2] - (t00*R[0] + t01*R[1])
        v1 = R[3] - (t10*R[0] + t11*R[1])
        w2 = (s11*v0 - s10*v1) * idets
        w3 = (s00*v1 - s10*v0) * idets
        w0 = (ip*R[0] + iq*R[1]) - (t00*w2 + t10*w3)
        w1 = (iq*R[0] + iD*R[1]) - (t01*w2 + t11*w3)
        W = [jnp.broadcast_to(w, (8, B)) for w in (w0, w1, w2, w3)]
        ipp = 1.0 / p; iss = 1.0 / s00
        F = [R[0]*lax.rsqrt(p), (R[1] - (q*ipp)*R[0])*lax.rsqrt(det*ipp), v0*lax.rsqrt(s00), (v1 - (s10*iss)*v0)*lax.rsqrt(dets*iss)]
        inpiv8 = (lane8 >= j) & (lane8 < j+4)
        for t in range(t0, n):
            if t == t0:
                m = [jnp.where(sub > s+3, c[b], 0.0) for b in range(4)]
            else:
                m = [jnp.broadcast_to(ch[t][:, j+b:j+b+1], (8, B)) for b in range(4)]
            u = (m[0]*W[0] + m[1]*W[1]) + (m[2]*W[2] + m[3]*W[3])
            ch[t] = jnp.where(inpiv8, 0.0, ch[t]) - u
            if t == t0:
                for b in range(4):
                    ch[t] = jnp.where(sub == s+b, jnp.broadcast_to(jnp.where(lane <= j+b, F[b], 0.0), (8, B)), ch[t])

    return jnp.concatenate([x * srow8 for x in ch], 0)

def chol_kernel(g_ref, x_ref):
    n = 0
    for i in range(4):
        for k in range(4):
            if k >= i:
                x_ref[i*B:(i+1)*B, k*B:(k+1)*B] = g_ref[n]
                n += 1
            else:
                x_ref[i*B:(i+1)*B, k*B:(k+1)*B] = jnp.zeros((B, B), jnp.float32)
    for J in range(4):
        lo, hi = J*B, (J+1)*B
        x = leaf_inverse(x_ref[lo:hi, lo:hi])
        x_ref[lo:hi, lo:hi] = x
        if J > 0:
            x_ref[lo:hi, 0:lo] = mm(x, x_ref[lo:hi, 0:lo])
        if J < 3:
            right = mm(x, x_ref[lo:hi, hi:])
            rt = right.T
            x_ref[lo:hi, hi:] = right
            x_ref[hi:, hi:] = x_ref[hi:, hi:] - mm(rt, right)
            left = mm(rt, x_ref[lo:hi, 0:hi])
            if J > 0:
                x_ref[hi:, 0:lo] = x_ref[hi:, 0:lo] - left[:, 0:lo]
            x_ref[hi:, lo:hi] = -left[:, lo:hi]
            x_ref[lo:hi, hi:] = jnp.zeros_like(right)

def chol_inverse(g):
    return pl.pallas_call(chol_kernel, out_shape=jax.ShapeDtypeStruct((4*B, 4*B), jnp.float32),
        in_specs=[pl.BlockSpec(memory_space=pltpu.VMEM)], out_specs=pl.BlockSpec(memory_space=pltpu.VMEM),
        compiler_params=pltpu.CompilerParams(vmem_limit_bytes=48*2**20), name="chol")(g)

def chol_load(g, x_ref):
    n = 0
    for i in range(4):
        for k in range(4):
            if k >= i:
                x_ref[i*B:(i+1)*B, k*B:(k+1)*B] = g[n]
                n += 1
            else:
                x_ref[i*B:(i+1)*B, k*B:(k+1)*B] = jnp.zeros((B, B), jnp.float32)

def chol_steps(g, x_ref):
    chol_load(g, x_ref)
    for J in range(4):
        lo, hi = J*B, (J+1)*B
        x = leaf_inverse(x_ref[lo:hi, lo:hi])
        x_ref[lo:hi, lo:hi] = x
        if J > 0:
            x_ref[lo:hi, 0:lo] = mm(x, x_ref[lo:hi, 0:lo])
        if J < 3:
            right = mm(x, x_ref[lo:hi, hi:])
            rt = right.T
            x_ref[lo:hi, hi:] = right
            x_ref[hi:, hi:] = x_ref[hi:, hi:] - mm(rt, right)
            left = mm(rt, x_ref[lo:hi, 0:hi])
            if J > 0:
                x_ref[hi:, 0:lo] = x_ref[hi:, 0:lo] - left[:, 0:lo]
            x_ref[hi:, lo:hi] = -left[:, lo:hi]
            x_ref[lo:hi, hi:] = jnp.zeros_like(right)
        yield

def run(gen):
    for _ in gen:
        pass

def alternate(first, *others):
    gens = [first, *others]
    while gens:
        for t in list(gens):
            try:
                next(t)
            except StopIteration:
                gens.remove(t)

def mesh_place():
    r = lax.axis_index("row"); c = lax.axis_index("col")
    q = {"xh": lax.div(r, 2), "core": lax.rem(r, 2), "y": lax.div(c, 8), "xl": lax.rem(lax.div(c, 4), 2), "z": lax.rem(c, 4)}
    q["x"] = q["xh"]*2 + q["xl"]
    return r, c, q

def col_neighbours(r, q):
    def dev(y, x, z):
        return (r, y*8 + x*4 + z)
    y, x, z = q["y"], q["xl"], q["z"]
    return {"yp": dev(lax.rem(y+1,4),x,z), "ym": dev(lax.rem(y+3,4),x,z), "zp": dev(y,x,lax.rem(z+1,4)), "zm": dev(y,x,lax.rem(z+3,4)), "xd": dev(y,1-x,z)}

def row_neighbours(c, q):
    h, k = q["xh"], q["core"]
    return {"other": (h*2 + 1-k, c), "far": ((1-h)*2 + k, c)}

def axis_peer(q, ax, d):
    t = dict(q); t[ax] = lax.rem(q[ax]+d, 4)
    return t[ax], (lax.div(t["x"], 2)*2 + t["core"], t["y"]*8 + lax.rem(t["x"], 2)*4 + t["z"])

def gram_devices(c, q):
    return [row_neighbours(c, q)["other"]] + [axis_peer(q, ax, d)[1] for ax in "xyz" for d in (1, 2, 3)]

def gram_scratch():
    V = lambda *sh: pltpu.VMEM(sh, jnp.float32)
    D = pltpu.SemaphoreType.DMA
    bufs = [V(2,5,128,128), V(5,128,128)]
    for b0, nb, od in GROUPS:
        bufs += [V(5, nb, 32, 128), V(4, nb, 8, 128), V(4, nb, 8, 128)]
    return bufs + [D((2,)), D((2,)), D((15,4)), D((15,4))]
NGRAM = 15

def gram_steps(s, o, c, q, scr):
    g, crec, bufs, (ssc, rsc, ss, rs) = scr[0], scr[1], scr[2:11], scr[11:]
    k = q["core"]; at = q
    other = row_neighbours(c, q)["other"]
    n = 0
    for i in range(4):
        w = jnp.einsum("ni,nk->ik", s[:, i*128:(i+1)*128], s[:, i*128:], precision=HI, preferred_element_type=jnp.float32)
        for j in range(i, 4):
            g[n//5, n%5] = w[:, (j-i)*128:(j-i+1)*128]
            n += 1
    cc = rc(g.at[1-k], crec, ssc.at[0], rsc.at[0], other)
    cc.start()
    yield
    cc.wait_recv()
    g[k] = g[k] + crec[...]
    sends = []
    def exchange(src, buf, ax, sem):
        me = at[ax]
        for d in (1, 3, 2):
            to, dv = axis_peer(q, ax, d)
            t = rc(src(to), buf.at[me], ss.at[sem, d], rs.at[sem, me], dv)
            t.start(); sends.append(t)
        def done():
            for d in (1, 3, 2):
                fr, dv = axis_peer(q, ax, d)
                rc(src(fr), buf.at[fr], ss.at[sem, d], rs.at[sem, fr], dv).wait_recv()
        return done
    def gather(view, ax, sem):
        me = at[ax]
        for d in (1, 3, 2):
            to, dv = axis_peer(q, ax, d)
            t = rc(view(me), view(me), ss.at[sem, d], rs.at[sem, me], dv)
            t.start(); sends.append(t)
        def done():
            for d in (1, 3, 2):
                fr, dv = axis_peer(q, ax, d)
                rc(view(fr), view(fr), ss.at[sem, d], rs.at[sem, fr], dv).wait_recv()
        return done
    b1 = [bufs[3*i] for i in range(3)]; b2 = [bufs[3*i+1] for i in range(3)]; b3 = [bufs[3*i+2] for i in range(3)]
    m32 = lambda i: pl.ds(pl.multiple_of(i*32, 32), 32)
    m8 = lambda i: pl.ds(pl.multiple_of(i*8, 8), 8)
    f = []
    for i, (b0, nb, od) in enumerate(GROUPS):
        f.append(exchange(lambda t, b0=b0, nb=nb: g.at[k, pl.ds(b0, nb), m32(t)], b1[i], od[0], i*5))
    for i, (b0, nb, od) in enumerate(GROUPS):
        b1[i][at[od[0]]] = g[k, b0:b0+nb, m32(at[od[0]])]
    yield
    f2 = []
    for i, (b0, nb, od) in enumerate(GROUPS):
        f[i]()
        b1[i][4] = (b1[i][0] + b1[i][1]) + (b1[i][2] + b1[i][3])
        f2.append(exchange(lambda t, i=i: b1[i].at[4, :, m8(t)], b2[i], od[1], i*5+1))
        b2[i][at[od[1]]] = b1[i][4, :, m8(at[od[1]])]
    yield
    f3 = []
    for i, (b0, nb, od) in enumerate(GROUPS):
        f2[i]()
        b3[i][at[od[2]]] = (b2[i][0] + b2[i][1]) + (b2[i][2] + b2[i][3])
        f3.append(gather(lambda t, i=i: b3[i].at[t], od[2], i*5+2))
    yield
    f4 = []
    for i, (b0, nb, od) in enumerate(GROUPS):
        f3[i]()
        rows = lambda t, b0=b0, nb=nb, od=od: o.at[k, pl.ds(b0, nb), pl.ds(pl.multiple_of(at[od[0]]*32 + t*8, 8), 8)]
        rows(at[od[1]])[...] = (b3[i][0] + b3[i][1]) + (b3[i][2] + b3[i][3])
        f4.append(gather(rows, od[1], i*5+3))
    yield
    f5 = []
    for i, (b0, nb, od) in enumerate(GROUPS):
        f4[i]()
        f5.append(gather(lambda t, b0=b0, nb=nb: o.at[k, pl.ds(b0, nb), m32(t)], od[0], i*5+4))
    yield
    for t in f5: t()
    co = rc(o.at[k], o.at[k], ssc.at[1], rsc.at[1], other)
    co.start()
    yield
    rc(o.at[1-k], o.at[1-k], ssc.at[1], rsc.at[1], other).wait_recv()
    for t in sends: t.wait_send()
    cc.wait_send(); co.wait_send()

A = pl.ds(0, 256); Bc = pl.ds(256, 256)

def rs_scratch():
    S = 64
    V = lambda *s: pltpu.VMEM(s, jnp.float32)
    D = pltpu.SemaphoreType.DMA
    return [V(2,4,S,256), V(2,2,4,S,256), V(2,4,S,256), V(2,2,4,S,256), V(2,4,S,256), V(2,4,S,256),
            V(2,S,256), V(2,2,S,256), V(2,S,256), V(2,2,S,256), V(2,S,256), V(2,S,256), V(2,S,256),
            D((4,6)), D((4,6)), D((2,)), D((2,))]

def rs_steps(p, o, q, nb, scr):
    relA, finA, relB, finB, qa, qb, relA2, finA2, relB2, finB2, ra, rb, recx, ss, rs, sx, rx = scr
    y, x, z = q["y"], q["xl"], q["z"]
    yp, ym, zp, zm, xd = nb["yp"], nb["ym"], nb["zp"], nb["zm"], nb["xd"]
    a1 = RingRS(lambda k,h: p.at[k,h,:,:,A], y, yp, ym, relA, finA, ss.at[0], rs.at[0])
    b1 = RingRS(lambda k,h: p.at[:,h,k,:,Bc], z, zp, zm, relB, finB, ss.at[1], rs.at[1])
    a1.start(); b1.start()
    yield
    a1.forward(); b1.forward()
    yield
    a1.finish(qa)
    a2 = RingRS(lambda k,h: qa.at[h,k], z, zp, zm, relA2, finA2, ss.at[2], rs.at[2])
    a2.start()
    b1.finish(qb)
    b2 = RingRS(lambda k,h: qb.at[h,k], y, yp, ym, relB2, finB2, ss.at[3], rs.at[3])
    b2.start()
    a2.forward(); b2.forward()
    yield
    a2.finish(ra)
    cxa = rc(ra.at[1-x], recx.at[0], sx.at[0], rx.at[0], xd); cxa.start()
    b2.finish(rb)
    cxb = rc(rb.at[1-x], recx.at[1], sx.at[1], rx.at[1], xd); cxb.start()
    cxa.wait_recv()
    o[:, 0:256] = ra[x] + recx[0]
    cxb.wait_recv()
    o[:, 256:512] = rb[x] + recx[1]
    for t in (a1, b1, a2, b2): t.drain()
    cxa.wait_send(); cxb.wait_send()

def ag_scratch():
    D = pltpu.SemaphoreType.DMA
    return [D((4,6)), D((4,6)), D((1,)), D((1,))]

def ag_steps(o, q, nb, scr):
    ss, rs, sx, rx = scr
    y, x, z = q["y"], q["xl"], q["z"]
    yp, ym, zp, zm, xd = nb["yp"], nb["ym"], nb["zp"], nb["zm"], nb["xd"]
    cx = rc(o.at[y,x,z], o.at[y,x,z], sx.at[0], rx.at[0], xd)
    cxr = rc(o.at[y,1-x,z], o.at[y,1-x,z], sx.at[0], rx.at[0], xd)
    cx.start()
    yield
    cxr.wait_recv()
    a1 = RingAG(lambda k,h: o.at[y,h,k,:,A], z, zp, zm, ss.at[0], rs.at[0])
    b1 = RingAG(lambda k,h: o.at[k,h,z,:,Bc], y, yp, ym, ss.at[1], rs.at[1])
    a1.start(); b1.start()
    yield
    a1.forward(); b1.forward()
    yield
    a1.finish()
    a2 = RingAG(lambda k,h: o.at[k,h,:,:,A], y, yp, ym, ss.at[2], rs.at[2])
    a2.start()
    b1.finish()
    b2 = RingAG(lambda k,h: o.at[:,h,k,:,Bc], z, zp, zm, ss.at[3], rs.at[3])
    b2.start()
    yield
    a2.forward(); b2.forward()
    yield
    a2.finish(); b2.finish()
    for t in (a1,b1,a2,b2): t.drain()
    cx.wait_send()

def row_rs_scratch(n):
    V = lambda *s: pltpu.VMEM(s, jnp.float32)
    D = pltpu.SemaphoreType.DMA
    return [V(2,n,512), V(n,512), V(n,512), D((2,)), D((2,)), D((1,)), D((1,))]

def row_rs_steps(p, o, q, nb, scr):
    rec1, qf, rec2, s1, r1, s2, r2 = scr
    h, k = q["xh"], q["core"]
    cs = [rc(p.at[1-h, 1-k], rec1.at[0], s1.at[0], r1.at[0], nb["other"]), rc(p.at[h, 1-k], rec1.at[1], s1.at[1], r1.at[1], nb["other"])]
    for t in cs: t.start()
    cs[0].wait_recv()
    qf[...] = p[1-h, k] + rec1[0]
    c2 = rc(qf, rec2, s2.at[0], r2.at[0], nb["far"]); c2.start()
    cs[1].wait_recv()
    o[...] = p[h, k] + rec1[1]
    yield
    c2.wait_recv()
    o[...] = o[...] + rec2[...]
    for t in cs: t.wait_send()
    c2.wait_send()

def row_ag_scratch():
    D = pltpu.SemaphoreType.DMA
    return [D((1,)), D((1,)), D((2,)), D((2,))]

def row_ag_steps(o, q, nb, scr):
    s1, r1, s2, r2 = scr
    h, k = q["xh"], q["core"]
    cf = rc(o.at[h,k], o.at[h,k], s1.at[0], r1.at[0], nb["far"])
    cfr = rc(o.at[1-h,k], o.at[1-h,k], s1.at[0], r1.at[0], nb["far"])
    cf.start()
    co = rc(o.at[h,k], o.at[h,k], s2.at[0], r2.at[0], nb["other"])
    cor = rc(o.at[h,1-k], o.at[h,1-k], s2.at[0], r2.at[0], nb["other"])
    co.start()
    yield
    cor.wait_recv()
    yield
    cfr.wait_recv()
    co2 = rc(o.at[1-h,k], o.at[1-h,k], s2.at[1], r2.at[1], nb["other"])
    co2r = rc(o.at[1-h,1-k], o.at[1-h,1-k], s2.at[1], r2.at[1], nb["other"])
    co2.start()
    yield
    co2r.wait_recv()
    cf.wait_send(); co.wait_send(); co2.wait_send()


def call(kernel, name, cid, outs, scratch, *args):
    return pl.pallas_call(kernel, out_shape=[jax.ShapeDtypeStruct(s, jnp.float32) for s in outs],
        in_specs=[VM]*len(args), out_specs=[VM]*len(outs), scratch_shapes=scratch,
        compiler_params=pltpu.CompilerParams(collective_id=cid, has_side_effects=True, vmem_limit_bytes=60*2**20), name=name)(*args)

def gather_gram_kernel(p, o, gb, *scr):
    r, c, q = mesh_place()
    nb = col_neighbours(r, q)
    o[q["y"], q["xl"], q["z"]] = p[...]
    barrier(list(nb.values()) + gram_devices(c, q))
    alternate(ag_steps(o, q, nb, scr[NGRAM:]), gram_steps(p, gb, c, q, scr[:NGRAM]))

def gather_gram(own):
    o, g = call(gather_gram_kernel, "gather_gram", 1, [(4,2,4,64,512), (2,5,B,B)], gram_scratch() + ag_scratch(), own)
    return o.reshape(2048, 512), g

def row_sum_chol_kernel(p, g, o, x, *scr):
    r, c, q = mesh_place()
    nb = row_neighbours(c, q)
    barrier(list(nb.values()))
    alternate(row_rs_steps(p, o, q, nb, scr), chol_steps_once(g, x))

def chol_steps_once(g, x):
    run(chol_steps(g, x))
    yield

def row_sum_chol(w, g):
    n = w.shape[0]//4
    return call(row_sum_chol_kernel, "row_sum_chol", 2, [(n, 512), (512, 512)], row_rs_scratch(n), w.reshape(2,2,n,512), g.reshape(10,B,B))

def apply_t(rows, x):
    return lax.dot_general(rows, x, (((1,), (1,)), ((), ())), precision=HI, preferred_element_type=jnp.float32)

def norm_gather_kernel(p, x, o, gb, own, *scr):
    r, c, q = mesh_place()
    nb = row_neighbours(c, q)
    own[...] = apply_t(p[...], x[...])
    o[q["xh"], q["core"]] = own[...]
    barrier([nb["far"]] + gram_devices(c, q))
    ag = row_ag_steps(o, q, nb, scr[NGRAM:])
    next(ag)
    run(gram_steps(own, gb, c, q, scr[:NGRAM]))
    run(ag)

def norm_gather(raw, x):
    n = raw.shape[0]
    o, g = call(norm_gather_kernel, "norm_gather", 3, [(2,2,n,512), (2,5,B,B)], [pltpu.VMEM((n,512), jnp.float32)] + gram_scratch() + row_ag_scratch(), raw, x)
    return o.reshape(4*n, 512), g

def col_sum_kernel(p, o, *scr):
    r, c, q = mesh_place()
    nb = col_neighbours(r, q)
    barrier(list(nb.values()))
    run(rs_steps(p, o, q, nb, scr))

def col_sum(p):
    return call(col_sum_kernel, "col_sum", 4, [(64,512)], rs_scratch(), p.reshape(4,2,4,64,512))[0]

def col_sum_chol_kernel(p, g, o, x, *scr):
    r, c, q = mesh_place()
    nb = col_neighbours(r, q)
    barrier(list(nb.values()))
    rsg = rs_steps(p, o, q, nb, scr); ch = chol_steps(g, x)
    next(rsg); next(ch)
    next(rsg); next(ch); next(ch)
    next(rsg); next(ch)
    run(rsg); run(ch)

def col_sum_chol(p, g):
    return call(col_sum_chol_kernel, "col_sum_chol", 5, [(64,512), (512,512)], rs_scratch(), p.reshape(4,2,4,64,512), g.reshape(10,B,B))

def last_kernel(p, x2, o, own, gb, x3, *scr):
    r, c, q = mesh_place()
    own[...] = apply_t(p[...], x2[...])
    barrier(gram_devices(c, q))
    run(gram_steps(own, gb, c, q, scr))
    run(chol_steps(Blocks(gb), x3))
    o[...] = SCALE * apply_t(own[...], x3[...])

class Blocks:
    def __init__(self, ref): self.ref = ref
    def __getitem__(self, n): return self.ref[n//5, n%5]

SCALE = float(8192.0 ** 0.5)

def last(raw, x2):
    V = lambda *s: pltpu.VMEM(s, jnp.float32)
    return call(last_kernel, "last", 6, [(64,512)], [V(64,512), V(2,5,B,B), V(512,512)] + gram_scratch(), raw, x2)[0]
DEEP = 1664
bf16 = jnp.bfloat16

def dot32(a, b):
    return jnp.dot(a, b, preferred_element_type=jnp.float32)

def dot3(ah, al, bh, bl):
    return dot32(ah, bh) + (dot32(ah, bl) + dot32(al, bh))

def split(v):
    h = v.astype(bf16)
    return h, (v - h.astype(jnp.float32)).astype(bf16)

class RS2:
    def __init__(self, p, o, q, nb, scr):
        (self.relA, self.finA, self.relB, self.finB, self.qa, self.qb, self.relA2, self.finA2, self.relB2, self.finB2,
         self.ra, self.rb, self.recx, self.ss, self.rs, self.sx, self.rx) = scr
        self.p, self.o, self.q, self.nb = p, o, q, nb
        y, x, z = q["y"], q["xl"], q["z"]
        self.a1 = RingRS(lambda k,h: p.at[k,h,:,:,A], y, nb["yp"], nb["ym"], self.relA, self.finA, self.ss.at[0], self.rs.at[0])
        self.b1 = RingRS(lambda k,h: p.at[:,h,k,:,Bc], z, nb["zp"], nb["zm"], self.relB, self.finB, self.ss.at[1], self.rs.at[1])
        self.a2 = RingRS(lambda k,h: self.qa.at[h,k], z, nb["zp"], nb["zm"], self.relA2, self.finA2, self.ss.at[2], self.rs.at[2])
        self.b2 = RingRS(lambda k,h: self.qb.at[h,k], y, nb["yp"], nb["ym"], self.relB2, self.finB2, self.ss.at[3], self.rs.at[3])
    def second(self):
        self.a1.finish(self.qa); self.a2.start()
        self.b1.finish(self.qb); self.b2.start()
    def second_forward(self):
        self.a2.forward(); self.b2.forward()
    def third(self):
        x = self.q["xl"]
        self.a2.finish(self.ra)
        self.cxa = rc(self.ra.at[1-x], self.recx.at[0], self.sx.at[0], self.rx.at[0], self.nb["xd"]); self.cxa.start()
        self.b2.finish(self.rb)
        self.cxb = rc(self.rb.at[1-x], self.recx.at[1], self.sx.at[1], self.rx.at[1], self.nb["xd"]); self.cxb.start()
    def end(self):
        x = self.q["xl"]
        self.cxa.wait_recv()
        self.o[:, 0:256] = self.ra[x] + self.recx[0]
        self.cxb.wait_recv()
        self.o[:, 256:512] = self.rb[x] + self.recx[1]
        for t in (self.a1, self.b1, self.a2, self.b2): t.drain()
        self.cxa.wait_send(); self.cxb.wait_send()

def start_relay(t):
    t.c[0].start(); t.c[1].start()

def start_direct(t):
    t.c[2].start(); t.c[3].start()

def split_rows(av, bv, k):
    def body(i, _):
        xx = lax.div(i, 4); zz = lax.rem(i, 4)
        for t in range(4):
            rows = pl.ds(16*t, 16)
            d = av[k, xx, zz, rows, :].astype(jnp.float32) - bv[k, xx, zz, rows, :].astype(jnp.float32)
            h, l = split(d)
            av[k, xx, zz, rows, :] = h
            bv[k, xx, zz, rows, :] = l
        return 0
    lax.fori_loop(0, 8, body, 0)

def load_start(a, b, av, bv, sem, order):
    cs = []
    for i, k in enumerate(order):
        ca = pltpu.make_async_copy(a.at[k], av.at[k], sem.at[0, i]); cb = pltpu.make_async_copy(b.at[k], bv.at[k], sem.at[1, i])
        ca.start(); cb.start()
        cs.append((ca, cb))
    return cs

def products(x, av, bv, xh, xl, p, loads, order, q, rs):
    y, z = q["y"], q["z"]
    far = lambda v: lax.rem(v+2, 4)
    up = lambda v: lax.rem(v+1, 4)
    dn = lambda v: lax.rem(v+3, 4)
    h, l = split(x[...])
    xh[...] = h
    xl[...] = l
    def blockA(k):
        w = dot3(av[k].reshape(512, DEEP), bv[k].reshape(512, DEEP), xh[:, 0:256], xl[:, 0:256])
        p[k, :, :, :, 0:256] = w.reshape(2, 4, 64, 256)
    def blockB(k):
        w = dot3(av[:, :, k].reshape(512, DEEP), bv[:, :, k].reshape(512, DEEP), xh[:, 256:512], xl[:, 256:512])
        p[:, :, k, :, 256:512] = w.reshape(4, 2, 64, 256)
    for i, k in enumerate(order):
        loads[i][0].wait(); loads[i][1].wait()
        split_rows(av, bv, k)
        if i == 0:
            blockA(far(y))
            start_relay(rs.a1)
    blockB(far(z)); start_relay(rs.b1)
    blockA(up(y)); blockA(dn(y)); start_direct(rs.a1)
    blockB(up(z)); blockB(dn(z)); start_direct(rs.b1)
    rs.a1.forward(); rs.b1.forward()
    blockA(y); blockB(z)

def row_order(q):
    y = q["y"]
    return [lax.rem(y+d, 4) for d in (2, 1, 3, 0)]

def transposes(av, bv, th, tl, y):
    def body(z, _):
        cols = pl.ds(pl.multiple_of((y*4 + z)*128, 128), 128)
        for n in range(13):
            lanes = slice(n*128, n*128+128)
            d = av[y, :, z, :, lanes].reshape(128, 128).astype(jnp.float32) + bv[y, :, z, :, lanes].reshape(128, 128).astype(jnp.float32)
            h, l = split(d.T)
            th[lanes, cols] = h
            tl[lanes, cols] = l
        return 0
    lax.fori_loop(0, 4, body, 0)

def sketch_kernel(a, b, x, o, th_o, tl_o, av, bv, xh, xl, p, th, tl, lsem, osem, *scr):
    r, c, q = mesh_place()
    order = row_order(q)
    loads = load_start(a, b, av, bv, lsem, order)
    nb = col_neighbours(r, q)
    barrier(list(nb.values()))
    rs = RS2(p, o, q, nb, scr)
    products(x, av, bv, xh, xl, p, loads, order, q, rs)
    for y in range(3): transposes(av, bv, th, tl, y)
    rs.second()
    transposes(av, bv, th, tl, 3)
    outs = [pltpu.make_async_copy(th, th_o, osem.at[0]), pltpu.make_async_copy(tl, tl_o, osem.at[1])]
    for t in outs: t.start()
    rs.second_forward()
    rs.third()
    rs.end()
    for t in outs: t.wait()

def vm(shape, dt=jnp.float32):
    return pltpu.VMEM(shape, dt)

def product_scratch():
    D = pltpu.SemaphoreType.DMA
    return [vm((4,2,4,64,DEEP), bf16), vm((4,2,4,64,DEEP), bf16), vm((DEEP,512), bf16), vm((DEEP,512), bf16), vm((4,2,4,64,512))]

ANY = pl.BlockSpec(memory_space=pl.ANY)

def call2(kernel, name, cid, ins, outs, scratch, *args):
    return pl.pallas_call(kernel, out_shape=[jax.ShapeDtypeStruct(s, d) for s, d, _ in outs],
        in_specs=list(ins), out_specs=[s for _, _, s in outs], scratch_shapes=scratch,
        compiler_params=pltpu.CompilerParams(collective_id=cid, has_side_effects=True, vmem_limit_bytes=62*2**20), name=name)(*args)

F = jnp.float32

def sketch_sum(a, b, x):
    D = pltpu.SemaphoreType.DMA
    return call2(sketch_kernel, "sketch_sum", 7, (ANY, ANY, VM), [((64,512), F, VM), ((DEEP,2048), bf16, ANY), ((DEEP,2048), bf16, ANY)],
        product_scratch() + [vm((DEEP,2048), bf16), vm((DEEP,2048), bf16), D((2,4)), D((2,))] + rs_scratch(), a, b, x)

def resketch_kernel(a, b, x, g, o, xi, av, bv, xh, xl, p, lsem, *scr):
    r, c, q = mesh_place()
    order = row_order(q)
    loads = load_start(a, b, av, bv, lsem, order)
    nb = col_neighbours(r, q)
    barrier(list(nb.values()))
    rs = RS2(p, o, q, nb, scr)
    products(x, av, bv, xh, xl, p, loads, order, q, rs)
    ch = chol_steps(Blocks(g), xi)
    next(ch)
    rs.second()
    next(ch)
    rs.second_forward()
    next(ch)
    rs.third()
    run(ch)
    rs.end()

def resketch_sum(a, b, x, g):
    D = pltpu.SemaphoreType.DMA
    return call2(resketch_kernel, "resketch_sum", 8, (ANY, ANY, VM, VM), [((64,512), F, VM), ((512,512), F, VM)],
        product_scratch() + [D((2,4))] + rs_scratch(), a, b, x, g)

class AG2:
    def __init__(self, o, q, nb, scr):
        self.o, self.q, self.nb = o, q, nb
        ss, rs, sx, rx = scr
        y, x, z = q["y"], q["xl"], q["z"]
        yp, ym, zp, zm, xd = nb["yp"], nb["ym"], nb["zp"], nb["zm"], nb["xd"]
        self.cx = rc(o.at[y,z,x], o.at[y,z,x], sx.at[0], rx.at[0], xd)
        self.cxr = rc(o.at[y,z,1-x], o.at[y,z,1-x], sx.at[0], rx.at[0], xd)
        self.a1 = RingAG(lambda k,h: o.at[y,k,h,:,A], z, zp, zm, ss.at[0], rs.at[0])
        self.b1 = RingAG(lambda k,h: o.at[k,z,h,:,Bc], y, yp, ym, ss.at[1], rs.at[1])
        self.a2 = RingAG(lambda k,h: o.at[k,:,h,:,A], y, yp, ym, ss.at[2], rs.at[2])
        self.b2 = RingAG(lambda k,h: o.at[:,k,h,:,Bc], z, zp, zm, ss.at[3], rs.at[3])
    def first(self):
        self.cx.start()
    def second(self):
        self.cxr.wait_recv()
        self.a1.start(); self.b1.start()
    def second_forward(self):
        self.a1.forward(); self.b1.forward()
    def third(self):
        self.a1.finish(); self.a2.start()
        self.b1.finish(); self.b2.start()
    def third_forward(self):
        self.a2.forward(); self.b2.forward()
    def near(self, t):
        t.r[2].wait_recv(); t.r[3].wait_recv()
    def far(self, t):
        t.r[4].wait_recv(); t.r[5].wait_recv()
    def drain(self):
        for t in (self.a1, self.b1, self.a2, self.b2): t.drain()
        self.cx.wait_send()

def cosketch_kernel(own, th_i, tl_i, w, gb, o, th, tl, lsem, *scr):
    r, c, q = mesh_place()
    ct = [pltpu.make_async_copy(th_i, th, lsem.at[0]), pltpu.make_async_copy(tl_i, tl, lsem.at[1])]
    for t in ct: t.start()
    nb = col_neighbours(r, q)
    y, z = q["y"], q["z"]
    o[y, z, q["xl"]] = own[...]
    barrier(list(nb.values()) + gram_devices(c, q))
    ag = AG2(o, q, nb, scr[NGRAM:])
    gr = gram_steps(own, gb, c, q, scr[:NGRAM])
    def blockA(k, first=False):
        cols = pl.ds(pl.multiple_of(k*512, 512), 512)
        sh, sl = split(o[k, :, :, :, 0:256].reshape(512, 256))
        v = dot3(th[:, cols], tl[:, cols], sh, sl)
        w[:, 0:256] = v if first else w[:, 0:256] + v
    def blockB(k, first=False):
        cols = [pl.ds(pl.multiple_of((i*4 + k)*128, 128), 128) for i in range(4)]
        sh, sl = split(o[:, k, :, :, 256:512].reshape(512, 256))
        v = dot3(jnp.concatenate([th[:, t] for t in cols], 1), jnp.concatenate([tl[:, t] for t in cols], 1), sh, sl)
        w[:, 256:512] = v if first else w[:, 256:512] + v
    up = lambda v: lax.rem(v+1, 4)
    dn = lambda v: lax.rem(v+3, 4)
    ag.first(); next(gr)
    ag.second(); next(gr)
    ag.second_forward(); next(gr)
    ag.third(); next(gr)
    for t in ct: t.wait()
    blockA(y, True); next(gr)
    blockB(z, True)
    ag.third_forward(); next(gr); next(gr)
    ag.near(ag.a2); blockA(up(y)); blockA(dn(y))
    run(gr)
    ag.near(ag.b2); blockB(up(z)); blockB(dn(z))
    ag.far(ag.a2); blockA(lax.rem(y+2, 4))
    ag.far(ag.b2); blockB(lax.rem(z+2, 4))
    ag.drain()

def cosketch(own, th, tl):
    D = pltpu.SemaphoreType.DMA
    return call2(cosketch_kernel, "cosketch", 9, (VM, ANY, ANY), [((DEEP,512), F, VM), ((2,5,B,B), F, VM)],
        [vm((4,4,2,64,512)), vm((DEEP,2048), bf16), vm((DEEP,2048), bf16), D((2,))] + gram_scratch() + ag_scratch(), own, th, tl)
def shards(adjusted_weight, base_weight, test_matrix):
    rows = (4, 2, 4, 64, DEEP)
    a, b = adjusted_weight.reshape(rows), base_weight.reshape(rows)
    own, th, tl = sketch_sum(a, b, test_matrix)
    w, g1 = cosketch(own, th, tl)
    raw, x1 = row_sum_chol(w, g1)
    co, g2 = norm_gather(raw, x1)
    raw, x2 = resketch_sum(a, b, co, g2)
    return last(raw, x2)


def solution(mesh):
    return jax.shard_map(
        shards,
        mesh=mesh,
        in_specs=(P("row", "col"), P("row", "col"), P("col", None)),
        out_specs=P(("row", "col"), None),
        check_vma=False,
    )
```

```python
import jax
import jax.numpy as jnp
from jax import lax
from jax.experimental import pallas as pl
from jax.experimental.pallas import tpu as pltpu
from jax.sharding import PartitionSpec as P

MESH = pl.DeviceIdType.MESH
VM = pl.BlockSpec(memory_space=pltpu.VMEM)

def place():
    r = lax.axis_index("row"); c = lax.axis_index("col")
    y = lax.div(c, 8); x = lax.rem(lax.div(c, 4), 2); z = lax.rem(c, 4)
    def dev(yy, xx, zz):
        return (r, yy*8 + xx*4 + zz)
    return r, y, x, z, dev

def barrier(devs):
    sem = pltpu.get_barrier_semaphore()
    for d in devs:
        pl.semaphore_signal(sem, inc=1, device_id=d, device_id_type=MESH)
    pl.semaphore_wait(sem, len(devs))

def rc(src, dst, ssem, rsem, dev):
    return pltpu.make_async_remote_copy(src_ref=src, dst_ref=dst, send_sem=ssem, recv_sem=rsem, device_id=dev, device_id_type=MESH)

class RingRS:
    def __init__(self, part, me, devp, devm, relay, fin, ssem, rsem):
        self.part, self.me, self.devp, self.devm, self.relay, self.fin = part, me, devp, devm, relay, fin
        up = lax.rem(me+1, 4); dn = lax.rem(me+3, 4); far = lax.rem(me+2, 4)
        self.up, self.dn = up, dn
        self.c = [
            rc(part(far, 0), relay.at[0], ssem.at[0], rsem.at[0], devp),
            rc(part(far, 1), relay.at[1], ssem.at[1], rsem.at[1], devm),
            rc(part(up, 1), fin.at[0, 1], ssem.at[2], rsem.at[2], devp),
            rc(part(dn, 0), fin.at[1, 0], ssem.at[3], rsem.at[3], devm),
            rc(relay.at[0], fin.at[0, 0], ssem.at[4], rsem.at[4], devp),
            rc(relay.at[1], fin.at[1, 1], ssem.at[5], rsem.at[5], devm),
        ]
    def start(self):
        for i in range(4): self.c[i].start()
    def forward(self):
        self.c[0].wait_recv()
        self.relay[0] = self.relay[0] + self.part(self.up, 0)[...]
        self.c[4].start()
        self.c[1].wait_recv()
        self.relay[1] = self.relay[1] + self.part(self.dn, 1)[...]
        self.c[5].start()
    def finish(self, out):
        for i in (2, 3, 4, 5): self.c[i].wait_recv()
        for h in range(2):
            out[h] = self.part(self.me, h)[...] + self.fin[0, h] + self.fin[1, h]
    def drain(self):
        for i in range(6): self.c[i].wait_send()

def rs_col_kernel(p, o, relA, finA, relB, finB, qa, qb, relA2, finA2, relB2, finB2, ra, rb, recx, ss, rs, sx, rx):
    r, y, x, z, dev = place()
    yp, ym = dev(lax.rem(y+1,4),x,z), dev(lax.rem(y+3,4),x,z)
    zp, zm = dev(y,x,lax.rem(z+1,4)), dev(y,x,lax.rem(z+3,4))
    xd = dev(y,1-x,z)
    barrier([yp, ym, zp, zm, xd])
    A = pl.ds(0,256); Bc = pl.ds(256,256)
    a1 = RingRS(lambda k,h: p.at[k,h,:,:,A], y, yp, ym, relA, finA, ss.at[0], rs.at[0])
    b1 = RingRS(lambda k,h: p.at[:,h,k,:,Bc], z, zp, zm, relB, finB, ss.at[1], rs.at[1])
    a1.start(); b1.start(); a1.forward(); b1.forward()
    a1.finish(qa)
    a2 = RingRS(lambda k,h: qa.at[h,k], z, zp, zm, relA2, finA2, ss.at[2], rs.at[2])
    a2.start()
    b1.finish(qb)
    b2 = RingRS(lambda k,h: qb.at[h,k], y, yp, ym, relB2, finB2, ss.at[3], rs.at[3])
    b2.start()
    a2.forward(); b2.forward()
    a2.finish(ra)
    cxa = rc(ra.at[1-x], recx.at[0], sx.at[0], rx.at[0], xd); cxa.start()
    b2.finish(rb)
    cxb = rc(rb.at[1-x], recx.at[1], sx.at[1], rx.at[1], xd); cxb.start()
    cxa.wait_recv()
    o[:, 0:256] = ra[x] + recx[0]
    cxb.wait_recv()
    o[:, 256:512] = rb[x] + recx[1]
    for t in (a1, b1, a2, b2): t.drain()
    cxa.wait_send(); cxb.wait_send()

def rs_col(p, cid=1):
    S = 64
    f = jnp.float32
    V = lambda *s: pltpu.VMEM(s, f)
    return pl.pallas_call(rs_col_kernel, out_shape=jax.ShapeDtypeStruct((S,512), f), in_specs=[VM], out_specs=VM,
        scratch_shapes=[V(2,4,S,256), V(2,2,4,S,256), V(2,4,S,256), V(2,2,4,S,256), V(2,4,S,256), V(2,4,S,256),
            V(2,S,256), V(2,2,S,256), V(2,S,256), V(2,2,S,256), V(2,S,256), V(2,S,256), V(2,S,256),
            pltpu.SemaphoreType.DMA((4,6)), pltpu.SemaphoreType.DMA((4,6)), pltpu.SemaphoreType.DMA((2,)), pltpu.SemaphoreType.DMA((2,))],
        compiler_params=pltpu.CompilerParams(collective_id=cid, has_side_effects=True, vmem_limit_bytes=56*2**20), name="rs_col")(p.reshape(4,2,4,S,512))

class RingAG:
    def __init__(self, part, me, devp, devm, ssem, rsem):
        up = lax.rem(me+1, 4); dn = lax.rem(me+3, 4)
        far = lax.rem(me+2, 4)
        self.s = [rc(part(me,0), part(me,0), ssem.at[0], rsem.at[0], devp),
                  rc(part(me,1), part(me,1), ssem.at[1], rsem.at[1], devm),
                  rc(part(me,1), part(me,1), ssem.at[2], rsem.at[2], devp),
                  rc(part(me,0), part(me,0), ssem.at[3], rsem.at[3], devm),
                  rc(part(dn,0), part(dn,0), ssem.at[4], rsem.at[4], devp),
                  rc(part(up,1), part(up,1), ssem.at[5], rsem.at[5], devm)]
        self.r = [rc(part(dn,0), part(dn,0), ssem.at[0], rsem.at[0], devp),
                  rc(part(up,1), part(up,1), ssem.at[1], rsem.at[1], devm),
                  rc(part(dn,1), part(dn,1), ssem.at[2], rsem.at[2], devp),
                  rc(part(up,0), part(up,0), ssem.at[3], rsem.at[3], devm),
                  rc(part(far,0), part(far,0), ssem.at[4], rsem.at[4], devp),
                  rc(part(far,1), part(far,1), ssem.at[5], rsem.at[5], devm)]
    def start(self):
        for i in range(4): self.s[i].start()
    def forward(self):
        self.r[0].wait_recv(); self.s[4].start()
        self.r[1].wait_recv(); self.s[5].start()
    def finish(self):
        for i in (2,3,4,5): self.r[i].wait_recv()
    def drain(self):
        for i in range(6): self.s[i].wait_send()

def ag_col_kernel(p, o, ss, rs, sx, rx):
    r, y, x, z, dev = place()
    yp, ym = dev(lax.rem(y+1,4),x,z), dev(lax.rem(y+3,4),x,z)
    zp, zm = dev(y,x,lax.rem(z+1,4)), dev(y,x,lax.rem(z+3,4))
    xd = dev(y,1-x,z)
    o[y,x,z] = p[...]
    barrier([yp, ym, zp, zm, xd])
    cx = rc(o.at[y,x,z], o.at[y,x,z], sx.at[0], rx.at[0], xd)
    cxr = rc(o.at[y,1-x,z], o.at[y,1-x,z], sx.at[0], rx.at[0], xd)
    cx.start()
    A = pl.ds(0,256); Bc = pl.ds(256,256)
    cxr.wait_recv()
    a1 = RingAG(lambda k,h: o.at[y,h,k,:,A], z, zp, zm, ss.at[0], rs.at[0])
    b1 = RingAG(lambda k,h: o.at[k,h,z,:,Bc], y, yp, ym, ss.at[1], rs.at[1])
    a1.start(); b1.start()
    a1.forward(); b1.forward()
    a1.finish()
    a2 = RingAG(lambda k,h: o.at[k,h,:,:,A], y, yp, ym, ss.at[2], rs.at[2])
    a2.start()
    b1.finish()
    b2 = RingAG(lambda k,h: o.at[:,h,k,:,Bc], z, zp, zm, ss.at[3], rs.at[3])
    b2.start()
    a2.forward(); b2.forward()
    a2.finish(); b2.finish()
    for t in (a1,b1,a2,b2): t.drain()
    cx.wait_send()

def ag_col(p, cid=2):
    S = 64
    o = pl.pallas_call(ag_col_kernel, out_shape=jax.ShapeDtypeStruct((4,2,4,S,512), jnp.float32), in_specs=[VM], out_specs=VM,
        scratch_shapes=[pltpu.SemaphoreType.DMA((4,6)), pltpu.SemaphoreType.DMA((4,6)), pltpu.SemaphoreType.DMA((1,)), pltpu.SemaphoreType.DMA((1,))],
        compiler_params=pltpu.CompilerParams(collective_id=cid, has_side_effects=True, vmem_limit_bytes=56*2**20), name="ag_col")(p)
    return o.reshape(32*S, 512)

def rs_row_kernel(p, o, rec1, q, rec2, s1, r1, s2, r2):
    r = lax.axis_index("row"); c = lax.axis_index("col")
    h = lax.div(r,2); k = lax.rem(r,2)
    other = (h*2 + 1-k, c); far = ((1-h)*2 + k, c)
    barrier([other, far])
    cs = [rc(p.at[1-h, 1-k], rec1.at[0], s1.at[0], r1.at[0], other), rc(p.at[h, 1-k], rec1.at[1], s1.at[1], r1.at[1], other)]
    for t in cs: t.start()
    cs[0].wait_recv()
    q[...] = p[1-h, k] + rec1[0]
    c2 = rc(q, rec2, s2.at[0], r2.at[0], far); c2.start()
    cs[1].wait_recv()
    o[...] = p[h, k] + rec1[1]
    c2.wait_recv()
    o[...] = o[...] + rec2[...]
    for t in cs: t.wait_send()
    c2.wait_send()

def rs_row(p, cid=3):
    n = p.shape[0]//4
    V = lambda *s: pltpu.VMEM(s, jnp.float32)
    D = pltpu.SemaphoreType.DMA
    return pl.pallas_call(rs_row_kernel, out_shape=jax.ShapeDtypeStruct((n,512), jnp.float32), in_specs=[VM], out_specs=VM,
        scratch_shapes=[V(2,n,512), V(n,512), V(n,512), D((2,)), D((2,)), D((1,)), D((1,))],
        compiler_params=pltpu.CompilerParams(collective_id=cid, has_side_effects=True, vmem_limit_bytes=56*2**20), name="rs_row")(p.reshape(2,2,n,512))

def ag_row_kernel(p, o, s1, r1, s2, r2):
    r = lax.axis_index("row"); c = lax.axis_index("col")
    h = lax.div(r,2); k = lax.rem(r,2)
    other = (h*2 + 1-k, c); far = ((1-h)*2 + k, c)
    o[h, k] = p[...]
    barrier([other, far])
    cf = rc(o.at[h,k], o.at[h,k], s1.at[0], r1.at[0], far)
    cfr = rc(o.at[1-h,k], o.at[1-h,k], s1.at[0], r1.at[0], far)
    cf.start()
    co = rc(o.at[h,k], o.at[h,k], s2.at[0], r2.at[0], other)
    cor = rc(o.at[h,1-k], o.at[h,1-k], s2.at[0], r2.at[0], other)
    co.start()
    cfr.wait_recv()
    co2 = rc(o.at[1-h,k], o.at[1-h,k], s2.at[1], r2.at[1], other)
    co2r = rc(o.at[1-h,1-k], o.at[1-h,1-k], s2.at[1], r2.at[1], other)
    co2.start()
    cor.wait_recv(); co2r.wait_recv()
    cf.wait_send(); co.wait_send(); co2.wait_send()

def ag_row(p, cid=4):
    n = p.shape[0]
    D = pltpu.SemaphoreType.DMA
    o = pl.pallas_call(ag_row_kernel, out_shape=jax.ShapeDtypeStruct((2,2,n,512), jnp.float32), in_specs=[VM], out_specs=VM,
        scratch_shapes=[D((1,)), D((1,)), D((2,)), D((2,))],
        compiler_params=pltpu.CompilerParams(collective_id=cid, has_side_effects=True, vmem_limit_bytes=56*2**20), name="ag_row")(p)
    return o.reshape(4*n, 512)
HI = lax.Precision.HIGHEST
PAIRS = [(i, k) for i in range(4) for k in range(i, 4)]
GROUPS = [(0, 2, "zyx"), (2, 2, "yxz"), (4, 1, "xzy")]

def gram_kernel(s, o, g, crec, *rest):
    bufs, (ssc, rsc, ss, rs) = rest[:-4], rest[-4:]
    r = lax.axis_index("row"); c = lax.axis_index("col")
    xh = lax.div(r, 2); k = lax.rem(r, 2)
    y = lax.div(c, 8); xl = lax.rem(lax.div(c, 4), 2); z = lax.rem(c, 4)
    x = xh*2 + xl
    at = {"x": x, "y": y, "z": z}
    def dev(q):
        return (lax.div(q["x"], 2)*2 + k, q["y"]*8 + lax.rem(q["x"], 2)*4 + q["z"])
    def peer(ax, d):
        q = dict(at); q[ax] = lax.rem(at[ax]+d, 4)
        return q[ax], dev(q)
    other = (xh*2 + 1-k, c)
    barrier([other] + [peer(ax, d)[1] for ax in "xyz" for d in (1,2,3)])
    n = 0
    for i in range(4):
        w = jnp.einsum("ni,nk->ik", s[:, i*128:(i+1)*128], s[:, i*128:], precision=HI, preferred_element_type=jnp.float32)
        for j in range(i, 4):
            g[n//5, n%5] = w[:, (j-i)*128:(j-i+1)*128]
            n += 1
    cc = rc(g.at[1-k], crec, ssc.at[0], rsc.at[0], other)
    cc.start()
    cc.wait_recv()
    g[k] = g[k] + crec[...]
    sends = []
    def exchange(src, buf, ax, sem):
        me = at[ax]
        cs = []
        for d in (1, 3, 2):
            to, dv = peer(ax, d)
            t = rc(src(to), buf.at[me], ss.at[sem, d], rs.at[sem, me], dv)
            t.start(); cs.append(t)
        sends.extend(cs)
        def done():
            for d in (1, 3, 2):
                fr, dv = peer(ax, d)
                rc(src(fr), buf.at[fr], ss.at[sem, d], rs.at[sem, fr], dv).wait_recv()
        return done
    def gather(view, ax, sem):
        me = at[ax]
        cs = []
        for d in (1, 3, 2):
            to, dv = peer(ax, d)
            t = rc(view(me), view(me), ss.at[sem, d], rs.at[sem, me], dv)
            t.start(); cs.append(t)
        sends.extend(cs)
        def done():
            for d in (1, 3, 2):
                fr, dv = peer(ax, d)
                rc(view(fr), view(fr), ss.at[sem, d], rs.at[sem, fr], dv).wait_recv()
        return done
    G3 = range(3)

    b1 = [bufs[3*i] for i in G3]; b2 = [bufs[3*i+1] for i in G3]; b3 = [bufs[3*i+2] for i in G3]
    f = []
    for i, (b0, nb, od) in enumerate(GROUPS):
        f.append(exchange(lambda q, b0=b0, nb=nb: g.at[k, pl.ds(b0, nb), pl.ds(pl.multiple_of(q*32, 32), 32)], b1[i], od[0], i*5))
    for i, (b0, nb, od) in enumerate(GROUPS):
        b1[i][at[od[0]]] = g[k, b0:b0+nb, pl.ds(pl.multiple_of(at[od[0]]*32, 32), 32)]
    f2 = []
    for i, (b0, nb, od) in enumerate(GROUPS):
        f[i]()
        b1[i][4] = (b1[i][0] + b1[i][1]) + (b1[i][2] + b1[i][3])
        f2.append(exchange(lambda q, i=i: b1[i].at[4, :, pl.ds(pl.multiple_of(q*8, 8), 8)], b2[i], od[1], i*5+1))
        b2[i][at[od[1]]] = b1[i][4, :, pl.ds(pl.multiple_of(at[od[1]]*8, 8), 8)]
    f3 = []
    for i, (b0, nb, od) in enumerate(GROUPS):
        f2[i]()
        b3[i][at[od[2]]] = (b2[i][0] + b2[i][1]) + (b2[i][2] + b2[i][3])
        f3.append(gather(lambda q, i=i: b3[i].at[q], od[2], i*5+2))
    f4 = []
    for i, (b0, nb, od) in enumerate(GROUPS):
        f3[i]()
        rows = lambda q, i=i, b0=b0, nb=nb, od=od: o.at[k, pl.ds(b0, nb), pl.ds(pl.multiple_of(at[od[0]]*32 + q*8, 8), 8)]
        rows(at[od[1]])[...] = (b3[i][0] + b3[i][1]) + (b3[i][2] + b3[i][3])
        f4.append(gather(rows, od[1], i*5+3))
    f5 = []
    for i, (b0, nb, od) in enumerate(GROUPS):
        f4[i]()
        f5.append(gather(lambda q, b0=b0, nb=nb: o.at[k, pl.ds(b0, nb), pl.ds(pl.multiple_of(q*32, 32), 32)], od[0], i*5+4))
    for t in f5: t()
    co = rc(o.at[k], o.at[k], ssc.at[1], rsc.at[1], other)
    co.start()
    rc(o.at[1-k], o.at[1-k], ssc.at[1], rsc.at[1], other).wait_recv()
    for t in sends: t.wait_send()
    cc.wait_send(); co.wait_send()

def gram_blocks(s, cid):
    V = lambda *sh: pltpu.VMEM(sh, jnp.float32)
    D = pltpu.SemaphoreType.DMA
    bufs = []
    for b0, nb, od in GROUPS:
        bufs += [V(5, nb, 32, 128), V(4, nb, 8, 128), V(4, nb, 8, 128)]
    return pl.pallas_call(gram_kernel, out_shape=jax.ShapeDtypeStruct((2,5,128,128), jnp.float32), in_specs=[VM], out_specs=VM,
        scratch_shapes=[V(2,5,128,128), V(5,128,128)] + bufs + [D((2,)), D((2,)), D((15,4)), D((15,4))],
        compiler_params=pltpu.CompilerParams(collective_id=cid, has_side_effects=True, vmem_limit_bytes=56*2**20), name="gram")(s)
HI = lax.Precision.HIGHEST
B = 128

def mm(a, b):
    return jnp.dot(a, b, precision=HI, preferred_element_type=jnp.float32)

def leaf_inverse(a):
    n = B // 8
    lane = lax.broadcasted_iota(jnp.int32, (1, B), 1)
    sub = lax.broadcasted_iota(jnp.int32, (8, B), 0)
    lane8 = lax.broadcasted_iota(jnp.int32, (8, B), 1)
    ch = [a[8*t:8*t+8, :] for t in range(n)]
    drow = jnp.zeros((8, B), jnp.float32)
    for t in range(n):
        drow = drow + jnp.where(lane8 == sub + 8*t, ch[t], 0.0)
    srow = lax.rsqrt(jnp.sum(drow, axis=0, keepdims=True))
    srow8 = jnp.broadcast_to(srow, (8, B))
    for t in range(n):
        scol = jnp.sum(jnp.where(lane8 == sub + 8*t, srow8, 0.0), axis=1, keepdims=True)
        ch[t] = ch[t] * srow8 * scol
    for j in range(0, B, 4):
        t0, s = divmod(j, 8)
        c = [jnp.broadcast_to(ch[t0][:, j+b:j+b+1], (8, B)) for b in range(4)]
        pv = lambda i, k: c[k][s+i:s+i+1]
        piv = [lane == j+b for b in range(4)]
        inpiv = (lane >= j) & (lane < j+4)
        R = [jnp.where(piv[b], 1.0, jnp.where(inpiv, 0.0, ch[t0][s+b:s+b+1, :])) for b in range(4)]
        p, q, d = pv(0, 0), pv(1, 0), pv(1, 1)
        det = p*d - q*q
        idet = 1.0 / det
        ip, iq, iD = d*idet, -q*idet, p*idet
        t00 = pv(2,0)*ip + pv(2,1)*iq; t01 = pv(2,0)*iq + pv(2,1)*iD
        t10 = pv(3,0)*ip + pv(3,1)*iq; t11 = pv(3,0)*iq + pv(3,1)*iD
        s00 = pv(2,2) - (t00*pv(2,0) + t01*pv(2,1))
        s10 = pv(3,2) - (t10*pv(2,0) + t11*pv(2,1))
        s11 = pv(3,3) - (t10*pv(3,0) + t11*pv(3,1))
        dets = s00*s11 - s10*s10
        idets = 1.0 / dets
        v0 = R[2] - (t00*R[0] + t01*R[1])
        v1 = R[3] - (t10*R[0] + t11*R[1])
        w2 = (s11*v0 - s10*v1) * idets
        w3 = (s00*v1 - s10*v0) * idets
        w0 = (ip*R[0] + iq*R[1]) - (t00*w2 + t10*w3)
        w1 = (iq*R[0] + iD*R[1]) - (t01*w2 + t11*w3)
        W = [jnp.broadcast_to(w, (8, B)) for w in (w0, w1, w2, w3)]
        ipp = 1.0 / p; iss = 1.0 / s00
        F = [R[0]*lax.rsqrt(p), (R[1] - (q*ipp)*R[0])*lax.rsqrt(det*ipp), v0*lax.rsqrt(s00), (v1 - (s10*iss)*v0)*lax.rsqrt(dets*iss)]
        inpiv8 = (lane8 >= j) & (lane8 < j+4)
        for t in range(t0, n):
            if t == t0:
                m = [jnp.where(sub > s+3, c[b], 0.0) for b in range(4)]
            else:
                m = [jnp.broadcast_to(ch[t][:, j+b:j+b+1], (8, B)) for b in range(4)]
            u = (m[0]*W[0] + m[1]*W[1]) + (m[2]*W[2] + m[3]*W[3])
            ch[t] = jnp.where(inpiv8, 0.0, ch[t]) - u
            if t == t0:
                for b in range(4):
                    ch[t] = jnp.where(sub == s+b, jnp.broadcast_to(jnp.where(lane <= j+b, F[b], 0.0), (8, B)), ch[t])

    return jnp.concatenate([x * srow8 for x in ch], 0)

def chol_kernel(g_ref, x_ref):
    n = 0
    for i in range(4):
        for k in range(4):
            if k >= i:
                x_ref[i*B:(i+1)*B, k*B:(k+1)*B] = g_ref[n]
                n += 1
            else:
                x_ref[i*B:(i+1)*B, k*B:(k+1)*B] = jnp.zeros((B, B), jnp.float32)
    for J in range(4):
        lo, hi = J*B, (J+1)*B
        x = leaf_inverse(x_ref[lo:hi, lo:hi])
        x_ref[lo:hi, lo:hi] = x
        if J > 0:
            x_ref[lo:hi, 0:lo] = mm(x, x_ref[lo:hi, 0:lo])
        if J < 3:
            right = mm(x, x_ref[lo:hi, hi:])
            rt = right.T
            x_ref[lo:hi, hi:] = right
            x_ref[hi:, hi:] = x_ref[hi:, hi:] - mm(rt, right)
            left = mm(rt, x_ref[lo:hi, 0:hi])
            if J > 0:
                x_ref[hi:, 0:lo] = x_ref[hi:, 0:lo] - left[:, 0:lo]
            x_ref[hi:, lo:hi] = -left[:, lo:hi]
            x_ref[lo:hi, hi:] = jnp.zeros_like(right)

def chol_inverse(g):
    return pl.pallas_call(chol_kernel, out_shape=jax.ShapeDtypeStruct((4*B, 4*B), jnp.float32),
        in_specs=[pl.BlockSpec(memory_space=pltpu.VMEM)], out_specs=pl.BlockSpec(memory_space=pltpu.VMEM),
        compiler_params=pltpu.CompilerParams(vmem_limit_bytes=48*2**20), name="chol")(g)

def chol_load(g, x_ref):
    n = 0
    for i in range(4):
        for k in range(4):
            if k >= i:
                x_ref[i*B:(i+1)*B, k*B:(k+1)*B] = g[n]
                n += 1
            else:
                x_ref[i*B:(i+1)*B, k*B:(k+1)*B] = jnp.zeros((B, B), jnp.float32)

def chol_steps(g, x_ref):
    chol_load(g, x_ref)
    for J in range(4):
        lo, hi = J*B, (J+1)*B
        x = leaf_inverse(x_ref[lo:hi, lo:hi])
        x_ref[lo:hi, lo:hi] = x
        if J > 0:
            x_ref[lo:hi, 0:lo] = mm(x, x_ref[lo:hi, 0:lo])
        if J < 3:
            right = mm(x, x_ref[lo:hi, hi:])
            rt = right.T
            x_ref[lo:hi, hi:] = right
            x_ref[hi:, hi:] = x_ref[hi:, hi:] - mm(rt, right)
            left = mm(rt, x_ref[lo:hi, 0:hi])
            if J > 0:
                x_ref[hi:, 0:lo] = x_ref[hi:, 0:lo] - left[:, 0:lo]
            x_ref[hi:, lo:hi] = -left[:, lo:hi]
            x_ref[lo:hi, hi:] = jnp.zeros_like(right)
        yield

def run(gen):
    for _ in gen:
        pass

def alternate(first, *others):
    gens = [first, *others]
    while gens:
        for t in list(gens):
            try:
                next(t)
            except StopIteration:
                gens.remove(t)

def mesh_place():
    r = lax.axis_index("row"); c = lax.axis_index("col")
    q = {"xh": lax.div(r, 2), "core": lax.rem(r, 2), "y": lax.div(c, 8), "xl": lax.rem(lax.div(c, 4), 2), "z": lax.rem(c, 4)}
    q["x"] = q["xh"]*2 + q["xl"]
    return r, c, q

def col_neighbours(r, q):
    def dev(y, x, z):
        return (r, y*8 + x*4 + z)
    y, x, z = q["y"], q["xl"], q["z"]
    return {"yp": dev(lax.rem(y+1,4),x,z), "ym": dev(lax.rem(y+3,4),x,z), "zp": dev(y,x,lax.rem(z+1,4)), "zm": dev(y,x,lax.rem(z+3,4)), "xd": dev(y,1-x,z)}

def row_neighbours(c, q):
    h, k = q["xh"], q["core"]
    return {"other": (h*2 + 1-k, c), "far": ((1-h)*2 + k, c)}

def axis_peer(q, ax, d):
    t = dict(q); t[ax] = lax.rem(q[ax]+d, 4)
    return t[ax], (lax.div(t["x"], 2)*2 + t["core"], t["y"]*8 + lax.rem(t["x"], 2)*4 + t["z"])

def gram_devices(c, q):
    return [row_neighbours(c, q)["other"]] + [axis_peer(q, ax, d)[1] for ax in "xyz" for d in (1, 2, 3)]

def gram_scratch():
    V = lambda *sh: pltpu.VMEM(sh, jnp.float32)
    D = pltpu.SemaphoreType.DMA
    bufs = [V(2,5,128,128), V(5,128,128)]
    for b0, nb, od in GROUPS:
        bufs += [V(5, nb, 32, 128), V(4, nb, 8, 128), V(4, nb, 8, 128)]
    return bufs + [D((2,)), D((2,)), D((15,4)), D((15,4))]
NGRAM = 15


def gram_steps(s, o, c, q, scr, GROUPS=GROUPS):
    g, crec, bufs, (ssc, rsc, ss, rs) = scr[0], scr[1], scr[2:11], scr[11:]
    k = q["core"]; at = q
    other = row_neighbours(c, q)["other"]
    n = 0
    for i in range(4):
        w = jnp.einsum("ni,nk->ik", s[:, i*128:(i+1)*128], s[:, i*128:], precision=HI, preferred_element_type=jnp.float32)
        for j in range(i, 4):
            g[n//5, n%5] = w[:, (j-i)*128:(j-i+1)*128]
            n += 1
    cc = rc(g.at[1-k], crec, ssc.at[0], rsc.at[0], other)
    cc.start()
    yield
    cc.wait_recv()
    g[k] = g[k] + crec[...]
    sends = []
    def exchange(src, buf, ax, sem):
        me = at[ax]
        for d in (1, 3, 2):
            to, dv = axis_peer(q, ax, d)
            t = rc(src(to), buf.at[me], ss.at[sem, d], rs.at[sem, me], dv)
            t.start(); sends.append(t)
        def done():
            for d in (1, 3, 2):
                fr, dv = axis_peer(q, ax, d)
                rc(src(fr), buf.at[fr], ss.at[sem, d], rs.at[sem, fr], dv).wait_recv()
        return done
    def gather(view, ax, sem):
        me = at[ax]
        for d in (1, 3, 2):
            to, dv = axis_peer(q, ax, d)
            t = rc(view(me), view(me), ss.at[sem, d], rs.at[sem, me], dv)
            t.start(); sends.append(t)
        def done():
            for d in (1, 3, 2):
                fr, dv = axis_peer(q, ax, d)
                rc(view(fr), view(fr), ss.at[sem, d], rs.at[sem, fr], dv).wait_recv()
        return done
    b1 = [bufs[3*i] for i in range(3)]; b2 = [bufs[3*i+1] for i in range(3)]; b3 = [bufs[3*i+2] for i in range(3)]
    m32 = lambda i: pl.ds(pl.multiple_of(i*32, 32), 32)
    m8 = lambda i: pl.ds(pl.multiple_of(i*8, 8), 8)
    f = []
    for i, (b0, nb, od) in enumerate(GROUPS):
        f.append(exchange(lambda t, b0=b0, nb=nb: g.at[k, pl.ds(b0, nb), m32(t)], b1[i], od[0], i*5))
    for i, (b0, nb, od) in enumerate(GROUPS):
        b1[i][at[od[0]]] = g[k, b0:b0+nb, m32(at[od[0]])]
    yield
    f2 = []
    for i, (b0, nb, od) in enumerate(GROUPS):
        f[i]()
        b1[i][4] = (b1[i][0] + b1[i][1]) + (b1[i][2] + b1[i][3])
        f2.append(exchange(lambda t, i=i: b1[i].at[4, :, m8(t)], b2[i], od[1], i*5+1))
        b2[i][at[od[1]]] = b1[i][4, :, m8(at[od[1]])]
    yield
    f3 = []
    for i, (b0, nb, od) in enumerate(GROUPS):
        f2[i]()
        b3[i][at[od[2]]] = (b2[i][0] + b2[i][1]) + (b2[i][2] + b2[i][3])
        f3.append(gather(lambda t, i=i: b3[i].at[t], od[2], i*5+2))
    yield
    f4 = []
    for i, (b0, nb, od) in enumerate(GROUPS):
        f3[i]()
        rows = lambda t, b0=b0, nb=nb, od=od: o.at[k, pl.ds(b0, nb), pl.ds(pl.multiple_of(at[od[0]]*32 + t*8, 8), 8)]
        rows(at[od[1]])[...] = (b3[i][0] + b3[i][1]) + (b3[i][2] + b3[i][3])
        f4.append(gather(rows, od[1], i*5+3))
    yield
    f5 = []
    for i, (b0, nb, od) in enumerate(GROUPS):
        f4[i]()
        f5.append(gather(lambda t, b0=b0, nb=nb: o.at[k, pl.ds(b0, nb), m32(t)], od[0], i*5+4))
    yield
    for t in f5: t()
    co = rc(o.at[k], o.at[k], ssc.at[1], rsc.at[1], other)
    co.start()
    yield
    rc(o.at[1-k], o.at[1-k], ssc.at[1], rsc.at[1], other).wait_recv()
    for t in sends: t.wait_send()
    cc.wait_send(); co.wait_send()

A = pl.ds(0, 256); Bc = pl.ds(256, 256)

def rs_scratch():
    S = 64
    V = lambda *s: pltpu.VMEM(s, jnp.float32)
    D = pltpu.SemaphoreType.DMA
    return [V(2,4,S,256), V(2,2,4,S,256), V(2,4,S,256), V(2,2,4,S,256), V(2,4,S,256), V(2,4,S,256),
            V(2,S,256), V(2,2,S,256), V(2,S,256), V(2,2,S,256), V(2,S,256), V(2,S,256), V(2,S,256),
            D((4,6)), D((4,6)), D((2,)), D((2,))]

def rs_steps(p, o, q, nb, scr):
    relA, finA, relB, finB, qa, qb, relA2, finA2, relB2, finB2, ra, rb, recx, ss, rs, sx, rx = scr
    y, x, z = q["y"], q["xl"], q["z"]
    yp, ym, zp, zm, xd = nb["yp"], nb["ym"], nb["zp"], nb["zm"], nb["xd"]
    a1 = RingRS(lambda k,h: p.at[k,h,:,:,A], y, yp, ym, relA, finA, ss.at[0], rs.at[0])
    b1 = RingRS(lambda k,h: p.at[:,h,k,:,Bc], z, zp, zm, relB, finB, ss.at[1], rs.at[1])
    a1.start(); b1.start()
    yield
    a1.forward(); b1.forward()
    yield
    a1.finish(qa)
    a2 = RingRS(lambda k,h: qa.at[h,k], z, zp, zm, relA2, finA2, ss.at[2], rs.at[2])
    a2.start()
    b1.finish(qb)
    b2 = RingRS(lambda k,h: qb.at[h,k], y, yp, ym, relB2, finB2, ss.at[3], rs.at[3])
    b2.start()
    a2.forward(); b2.forward()
    yield
    a2.finish(ra)
    cxa = rc(ra.at[1-x], recx.at[0], sx.at[0], rx.at[0], xd); cxa.start()
    b2.finish(rb)
    cxb = rc(rb.at[1-x], recx.at[1], sx.at[1], rx.at[1], xd); cxb.start()
    cxa.wait_recv()
    o[:, 0:256] = ra[x] + recx[0]
    cxb.wait_recv()
    o[:, 256:512] = rb[x] + recx[1]
    for t in (a1, b1, a2, b2): t.drain()
    cxa.wait_send(); cxb.wait_send()

def ag_scratch():
    D = pltpu.SemaphoreType.DMA
    return [D((4,6)), D((4,6)), D((1,)), D((1,))]

def ag_steps(o, q, nb, scr):
    ss, rs, sx, rx = scr
    y, x, z = q["y"], q["xl"], q["z"]
    yp, ym, zp, zm, xd = nb["yp"], nb["ym"], nb["zp"], nb["zm"], nb["xd"]
    cx = rc(o.at[y,x,z], o.at[y,x,z], sx.at[0], rx.at[0], xd)
    cxr = rc(o.at[y,1-x,z], o.at[y,1-x,z], sx.at[0], rx.at[0], xd)
    cx.start()
    yield
    cxr.wait_recv()
    a1 = RingAG(lambda k,h: o.at[y,h,k,:,A], z, zp, zm, ss.at[0], rs.at[0])
    b1 = RingAG(lambda k,h: o.at[k,h,z,:,Bc], y, yp, ym, ss.at[1], rs.at[1])
    a1.start(); b1.start()
    yield
    a1.forward(); b1.forward()
    yield
    a1.finish()
    a2 = RingAG(lambda k,h: o.at[k,h,:,:,A], y, yp, ym, ss.at[2], rs.at[2])
    a2.start()
    b1.finish()
    b2 = RingAG(lambda k,h: o.at[:,h,k,:,Bc], z, zp, zm, ss.at[3], rs.at[3])
    b2.start()
    yield
    a2.forward(); b2.forward()
    yield
    a2.finish(); b2.finish()
    for t in (a1,b1,a2,b2): t.drain()
    cx.wait_send()

def row_rs_scratch(n):
    V = lambda *s: pltpu.VMEM(s, jnp.float32)
    D = pltpu.SemaphoreType.DMA
    return [V(2,n,512), V(n,512), V(n,512), D((2,)), D((2,)), D((1,)), D((1,))]

def row_rs_steps(p, o, q, nb, scr):
    rec1, qf, rec2, s1, r1, s2, r2 = scr
    h, k = q["xh"], q["core"]
    cs = [rc(p.at[1-h, 1-k], rec1.at[0], s1.at[0], r1.at[0], nb["other"]), rc(p.at[h, 1-k], rec1.at[1], s1.at[1], r1.at[1], nb["other"])]
    for t in cs: t.start()
    cs[0].wait_recv()
    qf[...] = p[1-h, k] + rec1[0]
    c2 = rc(qf, rec2, s2.at[0], r2.at[0], nb["far"]); c2.start()
    cs[1].wait_recv()
    o[...] = p[h, k] + rec1[1]
    yield
    c2.wait_recv()
    o[...] = o[...] + rec2[...]
    for t in cs: t.wait_send()
    c2.wait_send()

def row_ag_scratch():
    D = pltpu.SemaphoreType.DMA
    return [D((1,)), D((1,)), D((2,)), D((2,))]

def row_ag_steps(o, q, nb, scr):
    s1, r1, s2, r2 = scr
    h, k = q["xh"], q["core"]
    cf = rc(o.at[h,k], o.at[h,k], s1.at[0], r1.at[0], nb["far"])
    cfr = rc(o.at[1-h,k], o.at[1-h,k], s1.at[0], r1.at[0], nb["far"])
    cf.start()
    co = rc(o.at[h,k], o.at[h,k], s2.at[0], r2.at[0], nb["other"])
    cor = rc(o.at[h,1-k], o.at[h,1-k], s2.at[0], r2.at[0], nb["other"])
    co.start()
    yield
    cor.wait_recv()
    yield
    cfr.wait_recv()
    co2 = rc(o.at[1-h,k], o.at[1-h,k], s2.at[1], r2.at[1], nb["other"])
    co2r = rc(o.at[1-h,1-k], o.at[1-h,1-k], s2.at[1], r2.at[1], nb["other"])
    co2.start()
    yield
    co2r.wait_recv()
    cf.wait_send(); co.wait_send(); co2.wait_send()


def call(kernel, name, cid, outs, scratch, *args):
    return pl.pallas_call(kernel, out_shape=[jax.ShapeDtypeStruct(s, jnp.float32) for s in outs],
        in_specs=[VM]*len(args), out_specs=[VM]*len(outs), scratch_shapes=scratch,
        compiler_params=pltpu.CompilerParams(collective_id=cid, has_side_effects=True, vmem_limit_bytes=60*2**20), name=name)(*args)

def gather_gram_kernel(p, o, gb, *scr):
    r, c, q = mesh_place()
    nb = col_neighbours(r, q)
    o[q["y"], q["xl"], q["z"]] = p[...]
    barrier(list(nb.values()) + gram_devices(c, q))
    alternate(ag_steps(o, q, nb, scr[NGRAM:]), gram_steps(p, gb, c, q, scr[:NGRAM]))

def gather_gram(own):
    o, g = call(gather_gram_kernel, "gather_gram", 1, [(4,2,4,64,512), (2,5,B,B)], gram_scratch() + ag_scratch(), own)
    return o.reshape(2048, 512), g

def row_sum_chol_kernel(p, g, o, x, *scr):
    r, c, q = mesh_place()
    nb = row_neighbours(c, q)
    barrier(list(nb.values()))
    alternate(row_rs_steps(p, o, q, nb, scr), chol_steps_once(g, x))

def chol_steps_once(g, x):
    run(chol_steps(g, x))
    yield

def row_sum_chol(w, g):
    n = w.shape[0]//4
    return call(row_sum_chol_kernel, "row_sum_chol", 2, [(n, 512), (512, 512)], row_rs_scratch(n), w.reshape(2,2,n,512), g.reshape(10,B,B))

def apply_t(rows, x):
    return lax.dot_general(rows, x, (((1,), (1,)), ((), ())), precision=HI, preferred_element_type=jnp.float32)

def norm_gather_kernel(p, x, o, gb, own, *scr):
    r, c, q = mesh_place()
    nb = row_neighbours(c, q)
    own[...] = apply_t(p[...], x[...])
    o[q["xh"], q["core"]] = own[...]
    barrier([nb["far"]] + gram_devices(c, q))
    ag = row_ag_steps(o, q, nb, scr[NGRAM:])
    next(ag)
    run(gram_steps(own, gb, c, q, scr[:NGRAM]))
    run(ag)

def norm_gather(raw, x):
    n = raw.shape[0]
    o, g = call(norm_gather_kernel, "norm_gather", 3, [(2,2,n,512), (2,5,B,B)], [pltpu.VMEM((n,512), jnp.float32)] + gram_scratch() + row_ag_scratch(), raw, x)
    return o.reshape(4*n, 512), g

def col_sum_kernel(p, o, *scr):
    r, c, q = mesh_place()
    nb = col_neighbours(r, q)
    barrier(list(nb.values()))
    run(rs_steps(p, o, q, nb, scr))

def col_sum(p):
    return call(col_sum_kernel, "col_sum", 4, [(64,512)], rs_scratch(), p.reshape(4,2,4,64,512))[0]

def col_sum_chol_kernel(p, g, o, x, *scr):
    r, c, q = mesh_place()
    nb = col_neighbours(r, q)
    barrier(list(nb.values()))
    rsg = rs_steps(p, o, q, nb, scr); ch = chol_steps(g, x)
    next(rsg); next(ch)
    next(rsg); next(ch); next(ch)
    next(rsg); next(ch)
    run(rsg); run(ch)

def col_sum_chol(p, g):
    return call(col_sum_chol_kernel, "col_sum_chol", 5, [(64,512), (512,512)], rs_scratch(), p.reshape(4,2,4,64,512), g.reshape(10,B,B))

def last_kernel(p, x2, o, own, gb, x3, *scr):
    r, c, q = mesh_place()
    own[...] = apply_t(p[...], x2[...])
    barrier(gram_devices(c, q))
    run(gram_steps(own, gb, c, q, scr))
    run(chol_steps(Blocks(gb), x3))
    o[...] = SCALE * apply_t(own[...], x3[...])

class Blocks:
    def __init__(self, ref): self.ref = ref
    def __getitem__(self, n): return self.ref[n//5, n%5]

SCALE = float(8192.0 ** 0.5)

def last(raw, x2):
    V = lambda *s: pltpu.VMEM(s, jnp.float32)
    return call(last_kernel, "last", 6, [(64,512)], [V(64,512), V(2,5,B,B), V(512,512)] + gram_scratch(), raw, x2)[0]
DEEP = 1664
bf16 = jnp.bfloat16

def dot32(a, b):
    return jnp.dot(a, b, preferred_element_type=jnp.float32)

def dot3(ah, al, bh, bl):
    return dot32(ah, bh) + (dot32(ah, bl) + dot32(al, bh))

def split(v):
    h = v.astype(bf16)
    return h, (v - h.astype(jnp.float32)).astype(bf16)

class RS2:
    def __init__(self, p, o, q, nb, scr):
        (self.relA, self.finA, self.relB, self.finB, self.qa, self.qb, self.relA2, self.finA2, self.relB2, self.finB2,
         self.ra, self.rb, self.recx, self.ss, self.rs, self.sx, self.rx) = scr
        self.p, self.o, self.q, self.nb = p, o, q, nb
        y, x, z = q["y"], q["xl"], q["z"]
        self.a1 = RingRS(lambda k,h: p.at[k,h,:,:,A], y, nb["yp"], nb["ym"], self.relA, self.finA, self.ss.at[0], self.rs.at[0])
        self.b1 = RingRS(lambda k,h: p.at[:,h,k,:,Bc], z, nb["zp"], nb["zm"], self.relB, self.finB, self.ss.at[1], self.rs.at[1])
        self.a2 = RingRS(lambda k,h: self.qa.at[h,k], z, nb["zp"], nb["zm"], self.relA2, self.finA2, self.ss.at[2], self.rs.at[2])
        self.b2 = RingRS(lambda k,h: self.qb.at[h,k], y, nb["yp"], nb["ym"], self.relB2, self.finB2, self.ss.at[3], self.rs.at[3])
    def second(self):
        self.a1.finish(self.qa); self.a2.start()
        self.b1.finish(self.qb); self.b2.start()
    def second_forward(self):
        self.a2.forward(); self.b2.forward()
    def third(self):
        x = self.q["xl"]
        self.a2.finish(self.ra)
        self.cxa = rc(self.ra.at[1-x], self.recx.at[0], self.sx.at[0], self.rx.at[0], self.nb["xd"]); self.cxa.start()
        self.b2.finish(self.rb)
        self.cxb = rc(self.rb.at[1-x], self.recx.at[1], self.sx.at[1], self.rx.at[1], self.nb["xd"]); self.cxb.start()
    def end(self):
        x = self.q["xl"]
        self.cxa.wait_recv()
        self.o[:, 0:256] = self.ra[x] + self.recx[0]
        self.cxb.wait_recv()
        self.o[:, 256:512] = self.rb[x] + self.recx[1]
        for t in (self.a1, self.b1, self.a2, self.b2): t.drain()
        self.cxa.wait_send(); self.cxb.wait_send()

def start_relay(t):
    t.c[0].start(); t.c[1].start()

def start_direct(t):
    t.c[2].start(); t.c[3].start()

def split_rows(av, bv, k):
    def body(i, _):
        xx = lax.div(i, 4); zz = lax.rem(i, 4)
        for t in range(4):
            rows = pl.ds(16*t, 16)
            d = av[k, xx, zz, rows, :].astype(jnp.float32) - bv[k, xx, zz, rows, :].astype(jnp.float32)
            h, l = split(d)
            av[k, xx, zz, rows, :] = h
            bv[k, xx, zz, rows, :] = l
        return 0
    lax.fori_loop(0, 8, body, 0)

def load_start(a, b, av, bv, sem, order):
    cs = []
    for i, k in enumerate(order):
        ca = pltpu.make_async_copy(a.at[k], av.at[k], sem.at[0, i]); cb = pltpu.make_async_copy(b.at[k], bv.at[k], sem.at[1, i])
        ca.start(); cb.start()
        cs.append((ca, cb))
    return cs

def products(x, av, bv, xh, xl, p, loads, order, q, rs):
    y, z = q["y"], q["z"]
    far = lambda v: lax.rem(v+2, 4)
    up = lambda v: lax.rem(v+1, 4)
    dn = lambda v: lax.rem(v+3, 4)
    h, l = split(x[...])
    xh[...] = h
    xl[...] = l
    def blockA(k):
        w = dot3(av[k].reshape(512, DEEP), bv[k].reshape(512, DEEP), xh[:, 0:256], xl[:, 0:256])
        p[k, :, :, :, 0:256] = w.reshape(2, 4, 64, 256)
    def blockB(k):
        w = dot3(av[:, :, k].reshape(512, DEEP), bv[:, :, k].reshape(512, DEEP), xh[:, 256:512], xl[:, 256:512])
        p[:, :, k, :, 256:512] = w.reshape(4, 2, 64, 256)
    for i, k in enumerate(order):
        loads[i][0].wait(); loads[i][1].wait()
        split_rows(av, bv, k)
        if i == 0:
            blockA(far(y))
            start_relay(rs.a1)
    blockB(far(z)); start_relay(rs.b1)
    blockA(up(y)); blockA(dn(y)); start_direct(rs.a1)
    blockB(up(z)); blockB(dn(z)); start_direct(rs.b1)
    rs.a1.forward(); rs.b1.forward()
    blockA(y); blockB(z)

def row_order(q):
    y = q["y"]
    return [lax.rem(y+d, 4) for d in (2, 1, 3, 0)]

def transposes(av, bv, th, tl, y):
    def body(z, _):
        cols = pl.ds(pl.multiple_of((y*4 + z)*128, 128), 128)
        for n in range(13):
            lanes = slice(n*128, n*128+128)
            d = av[y, :, z, :, lanes].reshape(128, 128).astype(jnp.float32) + bv[y, :, z, :, lanes].reshape(128, 128).astype(jnp.float32)
            h, l = split(d.T)
            th[lanes, cols] = h
            tl[lanes, cols] = l
        return 0
    lax.fori_loop(0, 4, body, 0)

def sketch_kernel(a, b, x, o, th_o, tl_o, av, bv, xh, xl, p, th, tl, lsem, osem, *scr):
    r, c, q = mesh_place()
    order = row_order(q)
    loads = load_start(a, b, av, bv, lsem, order)
    nb = col_neighbours(r, q)
    barrier(list(nb.values()))
    rs = RS2(p, o, q, nb, scr)
    products(x, av, bv, xh, xl, p, loads, order, q, rs)
    for y in range(3): transposes(av, bv, th, tl, y)
    rs.second()
    transposes(av, bv, th, tl, 3)
    outs = [pltpu.make_async_copy(th, th_o, osem.at[0]), pltpu.make_async_copy(tl, tl_o, osem.at[1])]
    for t in outs: t.start()
    rs.second_forward()
    rs.third()
    rs.end()
    for t in outs: t.wait()

def vm(shape, dt=jnp.float32):
    return pltpu.VMEM(shape, dt)

def product_scratch():
    D = pltpu.SemaphoreType.DMA
    return [vm((4,2,4,64,DEEP), bf16), vm((4,2,4,64,DEEP), bf16), vm((DEEP,512), bf16), vm((DEEP,512), bf16), vm((4,2,4,64,512))]

ANY = pl.BlockSpec(memory_space=pl.ANY)

def call2(kernel, name, cid, ins, outs, scratch, *args):
    return pl.pallas_call(kernel, out_shape=[jax.ShapeDtypeStruct(s, d) for s, d, _ in outs],
        in_specs=list(ins), out_specs=[s for _, _, s in outs], scratch_shapes=scratch,
        compiler_params=pltpu.CompilerParams(collective_id=cid, has_side_effects=True, vmem_limit_bytes=62*2**20), name=name)(*args)

F = jnp.float32

def sketch_sum(a, b, x):
    D = pltpu.SemaphoreType.DMA
    return call2(sketch_kernel, "sketch_sum", 7, (ANY, ANY, VM), [((64,512), F, VM), ((DEEP,2048), bf16, ANY), ((DEEP,2048), bf16, ANY)],
        product_scratch() + [vm((DEEP,2048), bf16), vm((DEEP,2048), bf16), D((2,4)), D((2,))] + rs_scratch(), a, b, x)

def resketch_kernel(a, b, x, g, o, xi, av, bv, xh, xl, p, lsem, *scr):
    r, c, q = mesh_place()
    order = row_order(q)
    loads = load_start(a, b, av, bv, lsem, order)
    nb = col_neighbours(r, q)
    barrier(list(nb.values()))
    rs = RS2(p, o, q, nb, scr)
    products(x, av, bv, xh, xl, p, loads, order, q, rs)
    ch = chol_steps(Blocks(g), xi)
    next(ch)
    rs.second()
    next(ch)
    rs.second_forward()
    next(ch)
    rs.third()
    run(ch)
    rs.end()

def resketch_sum(a, b, x, g):
    D = pltpu.SemaphoreType.DMA
    return call2(resketch_kernel, "resketch_sum", 8, (ANY, ANY, VM, VM), [((64,512), F, VM), ((512,512), F, VM)],
        product_scratch() + [D((2,4))] + rs_scratch(), a, b, x, g)

class AG2:
    def __init__(self, o, q, nb, scr):
        self.o, self.q, self.nb = o, q, nb
        ss, rs, sx, rx = scr
        y, x, z = q["y"], q["xl"], q["z"]
        yp, ym, zp, zm, xd = nb["yp"], nb["ym"], nb["zp"], nb["zm"], nb["xd"]
        self.cx = rc(o.at[y,z,x], o.at[y,z,x], sx.at[0], rx.at[0], xd)
        self.cxr = rc(o.at[y,z,1-x], o.at[y,z,1-x], sx.at[0], rx.at[0], xd)
        self.a1 = RingAG(lambda k,h: o.at[y,k,h,:,A], z, zp, zm, ss.at[0], rs.at[0])
        self.b1 = RingAG(lambda k,h: o.at[k,z,h,:,Bc], y, yp, ym, ss.at[1], rs.at[1])
        self.a2 = RingAG(lambda k,h: o.at[k,:,h,:,A], y, yp, ym, ss.at[2], rs.at[2])
        self.b2 = RingAG(lambda k,h: o.at[:,k,h,:,Bc], z, zp, zm, ss.at[3], rs.at[3])
    def first(self):
        self.cx.start()
    def second(self):
        self.cxr.wait_recv()
        self.a1.start(); self.b1.start()
    def second_forward(self):
        self.a1.forward(); self.b1.forward()
    def third(self):
        self.a1.finish(); self.a2.start()
        self.b1.finish(); self.b2.start()
    def third_forward(self):
        self.a2.forward(); self.b2.forward()
    def near(self, t):
        t.r[2].wait_recv(); t.r[3].wait_recv()
    def far(self, t):
        t.r[4].wait_recv(); t.r[5].wait_recv()
    def drain(self):
        for t in (self.a1, self.b1, self.a2, self.b2): t.drain()
        self.cx.wait_send()

def cosketch_kernel(own, th_i, tl_i, w, gb, o, th, tl, lsem, *scr):
    r, c, q = mesh_place()
    ct = [pltpu.make_async_copy(th_i, th, lsem.at[0]), pltpu.make_async_copy(tl_i, tl, lsem.at[1])]
    for t in ct: t.start()
    nb = col_neighbours(r, q)
    y, z = q["y"], q["z"]
    o[y, z, q["xl"]] = own[...]
    barrier(list(nb.values()) + gram_devices(c, q))
    ag = AG2(o, q, nb, scr[NGRAM:])
    gr = gram_steps(own, gb, c, q, scr[:NGRAM])
    def blockA(k, first=False):
        cols = pl.ds(pl.multiple_of(k*512, 512), 512)
        sh, sl = split(o[k, :, :, :, 0:256].reshape(512, 256))
        v = dot3(th[:, cols], tl[:, cols], sh, sl)
        w[:, 0:256] = v if first else w[:, 0:256] + v
    def blockB(k, first=False):
        cols = [pl.ds(pl.multiple_of((i*4 + k)*128, 128), 128) for i in range(4)]
        sh, sl = split(o[:, k, :, :, 256:512].reshape(512, 256))
        v = dot3(jnp.concatenate([th[:, t] for t in cols], 1), jnp.concatenate([tl[:, t] for t in cols], 1), sh, sl)
        w[:, 256:512] = v if first else w[:, 256:512] + v
    up = lambda v: lax.rem(v+1, 4)
    dn = lambda v: lax.rem(v+3, 4)
    ag.first(); next(gr)
    ag.second(); next(gr)
    ag.second_forward(); next(gr)
    ag.third(); next(gr)
    for t in ct: t.wait()
    blockA(y, True); next(gr)
    blockB(z, True)
    ag.third_forward(); next(gr); next(gr)
    ag.near(ag.a2); blockA(up(y)); blockA(dn(y))
    run(gr)
    ag.near(ag.b2); blockB(up(z)); blockB(dn(z))
    ag.far(ag.a2); blockA(lax.rem(y+2, 4))
    ag.far(ag.b2); blockB(lax.rem(z+2, 4))
    ag.drain()

def cosketch(own, th, tl):
    D = pltpu.SemaphoreType.DMA
    return call2(cosketch_kernel, "cosketch", 9, (VM, ANY, ANY), [((DEEP,512), F, VM), ((2,5,B,B), F, VM)],
        [vm((4,4,2,64,512)), vm((DEEP,2048), bf16), vm((DEEP,2048), bf16), D((2,))] + gram_scratch() + ag_scratch(), own, th, tl)
RA = pl.ds(0, 32); RB = pl.ds(32, 32)
HALF = 256

class RS3:
    def __init__(self, p, o, q, nb, scr, cols):
        (relA, finA, relB, finB, self.qa, self.qb, relA2, finA2, relB2, finB2,
         self.ra, self.rb, self.recx, ss, rs, self.sx, self.rx) = scr
        self.o, self.q, self.nb, self.cols = o, q, nb, cols
        y, x, z = q["y"], q["xl"], q["z"]
        self.a1 = RingRS(lambda k,h: p.at[k,h,:,RA,cols], y, nb["yp"], nb["ym"], relA, finA, ss.at[0], rs.at[0])
        self.b1 = RingRS(lambda k,h: p.at[:,h,k,RB,cols], z, nb["zp"], nb["zm"], relB, finB, ss.at[1], rs.at[1])
        self.a2 = RingRS(lambda k,h: self.qa.at[h,k], z, nb["zp"], nb["zm"], relA2, finA2, ss.at[2], rs.at[2])
        self.b2 = RingRS(lambda k,h: self.qb.at[h,k], y, nb["yp"], nb["ym"], relB2, finB2, ss.at[3], rs.at[3])
    def forward(self):
        self.a1.forward(); self.b1.forward()
    def second(self):
        self.a1.finish(self.qa); self.a2.start()
        self.b1.finish(self.qb); self.b2.start()
    def second_forward(self):
        self.a2.forward(); self.b2.forward()
    def third(self):
        x = self.q["xl"]
        self.a2.finish(self.ra)
        self.cxa = rc(self.ra.at[1-x], self.recx.at[0], self.sx.at[0], self.rx.at[0], self.nb["xd"]); self.cxa.start()
        self.b2.finish(self.rb)
        self.cxb = rc(self.rb.at[1-x], self.recx.at[1], self.sx.at[1], self.rx.at[1], self.nb["xd"]); self.cxb.start()
    def end(self):
        x = self.q["xl"]
        self.cxa.wait_recv()
        self.o[0:32, self.cols] = self.ra[x] + self.recx[0]
        self.cxb.wait_recv()
        self.o[32:64, self.cols] = self.rb[x] + self.recx[1]
        for t in (self.a1, self.b1, self.a2, self.b2): t.drain()
        self.cxa.wait_send(); self.cxb.wait_send()

def rs3_scratch():
    S = 32
    D = pltpu.SemaphoreType.DMA
    V = vm
    return [V((2,4,S,256)), V((2,2,4,S,256)), V((2,4,S,256)), V((2,2,4,S,256)), V((2,4,S,256)), V((2,4,S,256)),
            V((2,S,256)), V((2,2,S,256)), V((2,S,256)), V((2,2,S,256)), V((2,S,256)), V((2,S,256)), V((2,S,256)),
            D((4,6)), D((4,6)), D((2,)), D((2,))]
NRS = 17

class AG3:
    def __init__(self, o, q, nb, scr, cols):
        ss, rs, sx, rx = scr
        y, x, z = q["y"], q["xl"], q["z"]
        yp, ym, zp, zm, xd = nb["yp"], nb["ym"], nb["zp"], nb["zm"], nb["xd"]
        all_rows = pl.ds(0, 64)
        self.cx = rc(o.at[y,x,z,all_rows,cols], o.at[y,x,z,all_rows,cols], sx.at[0], rx.at[0], xd)
        self.cxr = rc(o.at[y,1-x,z,all_rows,cols], o.at[y,1-x,z,all_rows,cols], sx.at[0], rx.at[0], xd)
        self.a1 = RingAG(lambda k,h: o.at[y,h,k,RA,cols], z, zp, zm, ss.at[0], rs.at[0])
        self.b1 = RingAG(lambda k,h: o.at[k,h,z,RB,cols], y, yp, ym, ss.at[1], rs.at[1])
        self.a2 = RingAG(lambda k,h: o.at[k,h,:,RA,cols], y, yp, ym, ss.at[2], rs.at[2])
        self.b2 = RingAG(lambda k,h: o.at[:,h,k,RB,cols], z, zp, zm, ss.at[3], rs.at[3])
    def first(self):
        self.cx.start()
    def second(self):
        self.cxr.wait_recv()
        self.a1.start(); self.b1.start()
    def second_forward(self):
        self.a1.forward(); self.b1.forward()
    def third(self):
        self.a1.finish(); self.a2.start()
        self.b1.finish(); self.b2.start()
    def third_forward(self):
        self.a2.forward(); self.b2.forward()
    def near(self, t):
        t.r[2].wait_recv(); t.r[3].wait_recv()
    def far(self, t):
        t.r[4].wait_recv(); t.r[5].wait_recv()
    def drain(self):
        for t in (self.a1, self.b1, self.a2, self.b2): t.drain()
        self.cx.wait_send()

QROWS = DEEP // 4

def quarter(h, k):
    return pl.ds(pl.multiple_of((h*2 + k)*QROWS, 32), QROWS)

class RowRS:
    def __init__(self, w, o, q, nb, scr, cols):
        self.rec1, self.qf, self.rec2, s1, r1, s2, r2 = scr
        self.w, self.o, self.cols = w, o, cols
        h, k = self.h, self.k = q["xh"], q["core"]
        self.c = [rc(w.at[quarter(1-h, 1-k), cols], self.rec1.at[0], s1.at[0], r1.at[0], nb["other"]),
                  rc(w.at[quarter(h, 1-k), cols], self.rec1.at[1], s1.at[1], r1.at[1], nb["other"])]
        self.c2 = rc(self.qf, self.rec2, s2.at[0], r2.at[0], nb["far"])
    def start(self):
        for t in self.c: t.start()
    def middle(self):
        self.c[0].wait_recv()
        self.qf[...] = self.w[quarter(1-self.h, self.k), self.cols] + self.rec1[0]
        self.c2.start()
        self.c[1].wait_recv()
        self.o[:, self.cols] = self.w[quarter(self.h, self.k), self.cols] + self.rec1[1]
    def end(self):
        self.c2.wait_recv()
        self.o[:, self.cols] = self.o[:, self.cols] + self.rec2[...]
        for t in self.c: t.wait_send()
        self.c2.wait_send()

def row3_scratch():
    D = pltpu.SemaphoreType.DMA
    n = QROWS
    return [vm((2,n,HALF)), vm((n,HALF)), vm((n,HALF)), D((2,)), D((2,)), D((1,)), D((1,))]
NROW = 7

class RowAG:
    def __init__(self, o, q, nb, scr, cols):
        s1, r1, s2, r2 = scr
        h, k = q["xh"], q["core"]
        v = lambda a, b: o.at[quarter(a, b), cols]
        self.cf = rc(v(h,k), v(h,k), s1.at[0], r1.at[0], nb["far"])
        self.cfr = rc(v(1-h,k), v(1-h,k), s1.at[0], r1.at[0], nb["far"])
        self.co = rc(v(h,k), v(h,k), s2.at[0], r2.at[0], nb["other"])
        self.cor = rc(v(h,1-k), v(h,1-k), s2.at[0], r2.at[0], nb["other"])
        self.co2 = rc(v(1-h,k), v(1-h,k), s2.at[1], r2.at[1], nb["other"])
        self.co2r = rc(v(1-h,1-k), v(1-h,1-k), s2.at[1], r2.at[1], nb["other"])
    def start(self):
        self.cf.start(); self.co.start()
    def forward(self):
        self.cfr.wait_recv(); self.co2.start()
    def finish(self):
        self.cor.wait_recv(); self.co2r.wait_recv()
    def drain(self):
        self.cf.wait_send(); self.co.wait_send(); self.co2.wait_send()

XLAST = [(0, 2, "yzx"), (2, 2, "zyx"), (4, 1, "yzx")]
COLS = [pl.ds(0, HALF), pl.ds(HALF, HALF)]

def neighbours(r, c, q):
    nb = col_neighbours(r, q)
    nb.update(row_neighbours(c, q))
    return nb

def transpose_piece(av, bv, th, tl, i):
    def body(n, _):
        lanes = pl.ds(pl.multiple_of(n*128, 128), 128)
        cols = slice(i*128, i*128+128)
        if i < 8:
            y, x = divmod(i, 2)
            u, v = av[y, x, :, 0:32, lanes], bv[y, x, :, 0:32, lanes]
        else:
            z, g = divmod(i - 8, 2)
            u, v = av[2*g:2*g+2, :, z, 32:64, lanes], bv[2*g:2*g+2, :, z, 32:64, lanes]
        d = u.reshape(128, 128).astype(jnp.float32) + v.reshape(128, 128).astype(jnp.float32)
        h, l = split(d.T)
        th[lanes, cols] = h
        tl[lanes, cols] = l
        return 0
    lax.fori_loop(0, 13, body, 0)

def sketch3_kernel(a, b, x, o, th_o, tl_o, av, bv, xh, xl, p, th, tl, lsem, osem, *scr):
    r, c, q = mesh_place()
    order = row_order(q)
    loads = load_start(a, b, av, bv, lsem, order)
    nb = col_neighbours(r, q)
    barrier(list(nb.values()))
    rs = RS2(p, o, q, nb, scr)
    products(x, av, bv, xh, xl, p, loads, order, q, rs)
    for i in range(8): transpose_piece(av, bv, th, tl, i)
    rs.second()
    for i in range(8, 12): transpose_piece(av, bv, th, tl, i)
    rs.second_forward()
    for i in range(12, 16): transpose_piece(av, bv, th, tl, i)
    outs = [pltpu.make_async_copy(th, th_o, osem.at[0]), pltpu.make_async_copy(tl, tl_o, osem.at[1])]
    for t in outs: t.start()
    rs.third()
    rs.end()
    for t in outs: t.wait()

def sketch3(a, b, x):
    D = pltpu.SemaphoreType.DMA
    return call2(sketch3_kernel, "sketch", 1, (ANY, ANY, VM), [((64,512), F, VM), ((DEEP,2048), bf16, ANY), ((DEEP,2048), bf16, ANY)],
        product_scratch() + [vm((DEEP,2048), bf16), vm((DEEP,2048), bf16), D((2,4)), D((2,))] + rs_scratch(), a, b, x)

up = lambda v: lax.rem(v+1, 4)
dn = lambda v: lax.rem(v+3, 4)
far = lambda v: lax.rem(v+2, 4)

def cosketch3_kernel(own, th_i, tl_i, raw, x1, gb, o, th, tl, w, lsem, *scr):
    r, c, q = mesh_place()
    ct = [pltpu.make_async_copy(th_i, th, lsem.at[0]), pltpu.make_async_copy(tl_i, tl, lsem.at[1])]
    for t in ct: t.start()
    nb = neighbours(r, c, q)
    y, z = q["y"], q["z"]
    o[y, q["xl"], z] = own[...]
    barrier(gram_devices(c, q))
    s = list(scr)
    take = lambda n: [s.pop(0) for _ in range(n)]
    gr = gram_steps(own, gb, c, q, take(NGRAM))
    ag = [AG3(o, q, nb, take(4), COLS[i]) for i in range(2)]
    row = [RowRS(w, raw, q, nb, take(NROW), COLS[i]) for i in range(2)]
    ch = chol_steps(Blocks(gb), x1)
    def blockA(i, k, first=False):
        cols = pl.ds(pl.multiple_of(k*256, 256), 256)
        sh, sl = split(o[k, :, :, RA, COLS[i]].reshape(256, HALF))
        v = dot3(th[:, cols], tl[:, cols], sh, sl)
        w[:, COLS[i]] = v if first else w[:, COLS[i]] + v
    def blockB(i, k):
        cols = pl.ds(pl.multiple_of(1024 + k*256, 256), 256)
        sh, sl = split(o[:, :, k, RB, COLS[i]].reshape(256, HALF))
        w[:, COLS[i]] = w[:, COLS[i]] + dot3(th[:, cols], tl[:, cols], sh, sl)
    ag[0].first(); ag[1].first(); next(gr)
    ag[0].second(); next(gr)
    ag[0].second_forward(); next(gr)
    ag[0].third(); ag[1].second(); next(gr)
    for t in ct: t.wait()
    blockA(0, y, True); blockB(0, z)
    ag[0].third_forward(); ag[1].second_forward(); next(gr)
    ag[0].near(ag[0].a2); blockA(0, up(y)); blockA(0, dn(y))
    ag[0].near(ag[0].b2); ag[1].third(); next(gr)
    blockB(0, up(z)); blockB(0, dn(z))
    ag[0].far(ag[0].a2); blockA(0, far(y))
    ag[0].far(ag[0].b2); blockB(0, far(z))
    row[0].start(); next(gr)
    blockA(1, y, True); blockB(1, z)
    ag[1].third_forward()
    row[0].middle()
    run(gr)
    next(ch)
    ag[1].near(ag[1].a2); blockA(1, up(y)); blockA(1, dn(y))
    ag[1].near(ag[1].b2); blockB(1, up(z)); blockB(1, dn(z))
    ag[1].far(ag[1].a2); blockA(1, far(y))
    ag[1].far(ag[1].b2); blockB(1, far(z))
    row[1].start()
    row[0].end()
    row[1].middle()
    run(ch)
    row[1].end()
    for t in ag: t.drain()

def cosketch3(own, th, tl):
    D = pltpu.SemaphoreType.DMA
    return call2(cosketch3_kernel, "cosketch", 2, (VM, ANY, ANY), [((QROWS,512), F, VM), ((512,512), F, VM)],
        [vm((2,5,B,B)), vm((4,2,4,64,512)), vm((DEEP,2048), bf16), vm((DEEP,2048), bf16), vm((DEEP,512)), D((2,))]
        + gram_scratch() + ag_scratch()*2 + row3_scratch()*2, own, th, tl)

def resketch3_kernel(a, b, raw, x1, o, x2, gb, own, co, av, bv, xh, xl, p, lsem, *scr):
    r, c, q = mesh_place()
    order = row_order(q)
    loads = load_start(a, b, av, bv, lsem, order)
    nb = neighbours(r, c, q)
    y, z = q["y"], q["z"]
    mine = quarter(q["xh"], q["core"])
    s = list(scr)
    take = lambda n: [s.pop(0) for _ in range(n)]
    gr = gram_steps(own, gb, c, q, take(NGRAM), XLAST)
    rg = [RowAG(co, q, nb, take(4), COLS[i]) for i in range(2)]
    rs = [RS3(p, o, q, nb, take(NRS), COLS[i]) for i in range(2)]
    ch = chol_steps(Blocks(gb), x2)
    def normed(i):
        n = (i+1)*HALF
        v = apply_t(raw[:, 0:n], x1[i*HALF:n, 0:n])
        own[:, COLS[i]] = v
        co[mine, COLS[i]] = v
    def parts(i):
        h, l = split(co[:, COLS[i]])
        xh[:, COLS[i]] = h
        xl[:, COLS[i]] = l
    def blockA(i, k):
        v = dot3(av[k, :, :, RA].reshape(256, DEEP), bv[k, :, :, RA].reshape(256, DEEP), xh[:, COLS[i]], xl[:, COLS[i]])
        p[k, :, :, RA, COLS[i]] = v.reshape(2, 4, 32, HALF)
    def blockB(i, k):
        v = dot3(av[:, :, k, RB].reshape(256, DEEP), bv[:, :, k, RB].reshape(256, DEEP), xh[:, COLS[i]], xl[:, COLS[i]])
        p[:, :, k, RB, COLS[i]] = v.reshape(4, 2, 32, HALF)
    def first_blocks(i):
        blockA(i, far(y)); start_relay(rs[i].a1)
        blockB(i, far(z)); start_relay(rs[i].b1)
    def other_blocks(i):
        blockA(i, up(y)); blockA(i, dn(y)); start_direct(rs[i].a1)
        blockB(i, up(z)); blockB(i, dn(z)); start_direct(rs[i].b1)
    def own_blocks(i):
        blockA(i, y); blockB(i, z)
    def ready(i):
        loads[i][0].wait(); loads[i][1].wait()
        split_rows(av, bv, order[i])
    barrier(gram_devices(c, q))
    normed(0); rg[0].start()
    normed(1); next(gr)
    ready(0); ready(1); next(gr)
    ready(2); ready(3); next(gr)
    rg[0].forward(); rg[1].start(); next(gr)
    rg[0].finish(); parts(0)
    first_blocks(0); other_blocks(0); next(gr)
    rs[0].forward(); own_blocks(0); next(gr)
    rg[1].forward(); rg[1].finish(); parts(1)
    first_blocks(1); next(gr)
    rs[0].second()
    other_blocks(1); run(gr)
    rs[0].second_forward(); rs[1].forward()
    own_blocks(1)
    next(ch)
    rs[0].third(); rs[1].second()
    next(ch)
    rs[1].second_forward(); rs[0].end()
    next(ch)
    rs[1].third()
    run(ch)
    rs[1].end()
    for t in rg: t.drain()

def resketch3(a, b, raw, x1):
    D = pltpu.SemaphoreType.DMA
    return call2(resketch3_kernel, "resketch", 3, (ANY, ANY, VM, VM), [((64,512), F, VM), ((512,512), F, VM)],
        [vm((2,5,B,B)), vm((QROWS,512)), vm((DEEP,512))] + product_scratch() + [D((2,4))] + gram_scratch()
        + row_ag_scratch()*2 + rs3_scratch()*2, a, b, raw, x1)
def shards(adjusted_weight, base_weight, test_matrix):
    rows = (4, 2, 4, 64, DEEP)
    a, b = adjusted_weight.reshape(rows), base_weight.reshape(rows)
    own, th, tl = sketch3(a, b, test_matrix)
    raw, x1 = cosketch3(own, th, tl)
    raw, x2 = resketch3(a, b, raw, x1)
    return last(raw, x2)


def solution(mesh):
    return jax.shard_map(
        shards,
        mesh=mesh,
        in_specs=(P("row", "col"), P("row", "col"), P("col", None)),
        out_specs=P(("row", "col"), None),
        check_vma=False,
    )
```

```python
import jax
import jax.numpy as jnp
from jax import lax
from jax.experimental import pallas as pl
from jax.experimental.pallas import tpu as pltpu
from jax.sharding import PartitionSpec as P

MESH = pl.DeviceIdType.MESH
VM = pl.BlockSpec(memory_space=pltpu.VMEM)

def barrier(devs):
    sem = pltpu.get_barrier_semaphore()
    for d in devs:
        pl.semaphore_signal(sem, inc=1, device_id=d, device_id_type=MESH)
    pl.semaphore_wait(sem, len(devs))

def rc(src, dst, ssem, rsem, dev):
    return pltpu.make_async_remote_copy(src_ref=src, dst_ref=dst, send_sem=ssem, recv_sem=rsem, device_id=dev, device_id_type=MESH)

class RingRS:
    def __init__(self, part, me, devp, devm, relay, fin, ssem, rsem):
        self.part, self.me, self.devp, self.devm, self.relay, self.fin = part, me, devp, devm, relay, fin
        up = lax.rem(me+1, 4); dn = lax.rem(me+3, 4); far = lax.rem(me+2, 4)
        self.up, self.dn = up, dn
        self.c = [
            rc(part(far, 0), relay.at[0], ssem.at[0], rsem.at[0], devp),
            rc(part(far, 1), relay.at[1], ssem.at[1], rsem.at[1], devm),
            rc(part(up, 1), fin.at[0, 1], ssem.at[2], rsem.at[2], devp),
            rc(part(dn, 0), fin.at[1, 0], ssem.at[3], rsem.at[3], devm),
            rc(relay.at[0], fin.at[0, 0], ssem.at[4], rsem.at[4], devp),
            rc(relay.at[1], fin.at[1, 1], ssem.at[5], rsem.at[5], devm),
        ]
    def start(self):
        for i in range(4): self.c[i].start()
    def forward(self):
        self.c[0].wait_recv()
        self.relay[0] = self.relay[0] + self.part(self.up, 0)[...]
        self.c[4].start()
        self.c[1].wait_recv()
        self.relay[1] = self.relay[1] + self.part(self.dn, 1)[...]
        self.c[5].start()
    def finish(self, out):
        for i in (2, 3, 4, 5): self.c[i].wait_recv()
        for h in range(2):
            out[h] = self.part(self.me, h)[...] + self.fin[0, h] + self.fin[1, h]
    def drain(self):
        for i in range(6): self.c[i].wait_send()

class RingAG:
    def __init__(self, part, me, devp, devm, ssem, rsem):
        up = lax.rem(me+1, 4); dn = lax.rem(me+3, 4)
        far = lax.rem(me+2, 4)
        self.s = [rc(part(me,0), part(me,0), ssem.at[0], rsem.at[0], devp),
                  rc(part(me,1), part(me,1), ssem.at[1], rsem.at[1], devm),
                  rc(part(me,1), part(me,1), ssem.at[2], rsem.at[2], devp),
                  rc(part(me,0), part(me,0), ssem.at[3], rsem.at[3], devm),
                  rc(part(dn,0), part(dn,0), ssem.at[4], rsem.at[4], devp),
                  rc(part(up,1), part(up,1), ssem.at[5], rsem.at[5], devm)]
        self.r = [rc(part(dn,0), part(dn,0), ssem.at[0], rsem.at[0], devp),
                  rc(part(up,1), part(up,1), ssem.at[1], rsem.at[1], devm),
                  rc(part(dn,1), part(dn,1), ssem.at[2], rsem.at[2], devp),
                  rc(part(up,0), part(up,0), ssem.at[3], rsem.at[3], devm),
                  rc(part(far,0), part(far,0), ssem.at[4], rsem.at[4], devp),
                  rc(part(far,1), part(far,1), ssem.at[5], rsem.at[5], devm)]
    def start(self):
        for i in range(4): self.s[i].start()
    def forward(self):
        self.r[0].wait_recv(); self.s[4].start()
        self.r[1].wait_recv(); self.s[5].start()
    def finish(self):
        for i in (2,3,4,5): self.r[i].wait_recv()
    def drain(self):
        for i in range(6): self.s[i].wait_send()

HI = lax.Precision.HIGHEST
B = 128

def mm(a, b):
    return jnp.dot(a, b, precision=HI, preferred_element_type=jnp.float32)

def inverse(v):
    return 1.0 / v

def leaf_inverse(a, pause=0):
    n = B // 8
    lane = lax.broadcasted_iota(jnp.int32, (1, B), 1)
    sub = lax.broadcasted_iota(jnp.int32, (8, B), 0)
    lane8 = lax.broadcasted_iota(jnp.int32, (8, B), 1)
    ch = [a[8*t:8*t+8, :] for t in range(n)]
    drow = jnp.zeros((8, B), jnp.float32)
    for t in range(n):
        drow = drow + jnp.where(lane8 == sub + 8*t, ch[t], 0.0)
    srow = lax.rsqrt(jnp.sum(drow, axis=0, keepdims=True))
    srow8 = jnp.broadcast_to(srow, (8, B))
    for t in range(n):
        scol = jnp.sum(jnp.where(lane8 == sub + 8*t, srow8, 0.0), axis=1, keepdims=True)
        ch[t] = ch[t] * srow8 * scol
    for j in range(0, B, 4):
        if pause and j and j % pause == 0:
            yield
        t0, s = divmod(j, 8)
        c = [jnp.broadcast_to(ch[t0][:, j+b:j+b+1], (8, B)) for b in range(4)]
        pv = lambda i, k: c[k][s+i:s+i+1]
        piv = [lane == j+b for b in range(4)]
        inpiv = (lane >= j) & (lane < j+4)
        R = [jnp.where(piv[b], 1.0, jnp.where(inpiv, 0.0, ch[t0][s+b:s+b+1, :])) for b in range(4)]
        p, q, d = pv(0, 0), pv(1, 0), pv(1, 1)
        det = p*d - q*q
        idet = inverse(det)
        ip, iq, iD = d*idet, -q*idet, p*idet
        t00 = pv(2,0)*ip + pv(2,1)*iq; t01 = pv(2,0)*iq + pv(2,1)*iD
        t10 = pv(3,0)*ip + pv(3,1)*iq; t11 = pv(3,0)*iq + pv(3,1)*iD
        s00 = pv(2,2) - (t00*pv(2,0) + t01*pv(2,1))
        s10 = pv(3,2) - (t10*pv(2,0) + t11*pv(2,1))
        s11 = pv(3,3) - (t10*pv(3,0) + t11*pv(3,1))
        dets = s00*s11 - s10*s10
        idets = inverse(dets)
        v0 = R[2] - (t00*R[0] + t01*R[1])
        v1 = R[3] - (t10*R[0] + t11*R[1])
        w2 = (s11*v0 - s10*v1) * idets
        w3 = (s00*v1 - s10*v0) * idets
        w0 = (ip*R[0] + iq*R[1]) - (t00*w2 + t10*w3)
        w1 = (iq*R[0] + iD*R[1]) - (t01*w2 + t11*w3)
        W = [jnp.broadcast_to(w, (8, B)) for w in (w0, w1, w2, w3)]
        ipp = 1.0 / p; iss = 1.0 / s00
        F = [R[0]*lax.rsqrt(p), (R[1] - (q*ipp)*R[0])*lax.rsqrt(det*ipp), v0*lax.rsqrt(s00), (v1 - (s10*iss)*v0)*lax.rsqrt(dets*iss)]
        inpiv8 = (lane8 >= j) & (lane8 < j+4)
        for t in range(t0, n):
            if t == t0:
                m = [jnp.where(sub > s+3, c[b], 0.0) for b in range(4)]
            else:
                m = [jnp.broadcast_to(ch[t][:, j+b:j+b+1], (8, B)) for b in range(4)]
            u = (m[0]*W[0] + m[1]*W[1]) + (m[2]*W[2] + m[3]*W[3])
            ch[t] = jnp.where(inpiv8, 0.0, ch[t]) - u
            if t == t0:
                for b in range(4):
                    ch[t] = jnp.where(sub == s+b, jnp.broadcast_to(jnp.where(lane <= j+b, F[b], 0.0), (8, B)), ch[t])

    return jnp.concatenate([x * srow8 for x in ch], 0)

GROUPS = [(0, 2, "zyx"), (2, 2, "yxz"), (4, 1, "xzy")]


def chol_load(g, x_ref):
    n = 0
    for i in range(4):
        for k in range(4):
            if k >= i:
                x_ref[i*B:(i+1)*B, k*B:(k+1)*B] = g[n]
                n += 1
            else:
                x_ref[i*B:(i+1)*B, k*B:(k+1)*B] = jnp.zeros((B, B), jnp.float32)

def chol_steps(g, x_ref, pause=32):
    chol_load(g, x_ref)
    for J in range(4):
        lo, hi = J*B, (J+1)*B
        x = yield from leaf_inverse(x_ref[lo:hi, lo:hi], pause)
        x_ref[lo:hi, lo:hi] = x
        if J > 0:
            x_ref[lo:hi, 0:lo] = mm(x, x_ref[lo:hi, 0:lo])
        if J < 3:
            right = mm(x, x_ref[lo:hi, hi:])
            rt = right.T
            x_ref[lo:hi, hi:] = right
            x_ref[hi:, hi:] = x_ref[hi:, hi:] - mm(rt, right)
            left = mm(rt, x_ref[lo:hi, 0:hi])
            if J > 0:
                x_ref[hi:, 0:lo] = x_ref[hi:, 0:lo] - left[:, 0:lo]
            x_ref[hi:, lo:hi] = -left[:, lo:hi]
            x_ref[lo:hi, hi:] = jnp.zeros_like(right)
        yield

def run(gen):
    for _ in gen:
        pass

def mesh_place():
    r = lax.axis_index("row"); c = lax.axis_index("col")
    q = {"xh": lax.div(r, 2), "core": lax.rem(r, 2), "y": lax.div(c, 8), "xl": lax.rem(lax.div(c, 4), 2), "z": lax.rem(c, 4)}
    q["x"] = q["xh"]*2 + q["xl"]
    return r, c, q

def col_neighbours(r, q):
    def dev(y, x, z):
        return (r, y*8 + x*4 + z)
    y, x, z = q["y"], q["xl"], q["z"]
    return {"yp": dev(lax.rem(y+1,4),x,z), "ym": dev(lax.rem(y+3,4),x,z), "zp": dev(y,x,lax.rem(z+1,4)), "zm": dev(y,x,lax.rem(z+3,4)), "xd": dev(y,1-x,z)}

def row_neighbours(c, q):
    h, k = q["xh"], q["core"]
    return {"other": (h*2 + 1-k, c), "far": ((1-h)*2 + k, c)}

def axis_peer(q, ax, d):
    t = dict(q); t[ax] = lax.rem(q[ax]+d, 4)
    return t[ax], (lax.div(t["x"], 2)*2 + t["core"], t["y"]*8 + lax.rem(t["x"], 2)*4 + t["z"])

def gram_devices(c, q):
    return [row_neighbours(c, q)["other"]] + [axis_peer(q, ax, d)[1] for ax in "xyz" for d in (1, 2, 3)]

def gram_scratch():
    V = lambda *sh: pltpu.VMEM(sh, jnp.float32)
    D = pltpu.SemaphoreType.DMA
    bufs = [V(2,5,128,128), V(5,128,128)]
    for b0, nb, od in GROUPS:
        bufs += [V(5, nb, 32, 128), V(4, nb, 8, 128), V(4, nb, 8, 128)]
    return bufs + [D((2,)), D((2,)), D((15,4)), D((15,4))]
NGRAM = 15


def gram_steps(s, o, c, q, scr, GROUPS=GROUPS):
    g, crec, bufs, (ssc, rsc, ss, rs) = scr[0], scr[1], scr[2:11], scr[11:]
    k = q["core"]; at = q
    other = row_neighbours(c, q)["other"]
    n = 0
    for i in range(4):
        w = jnp.einsum("ni,nk->ik", s[:, i*128:(i+1)*128], s[:, i*128:], precision=HI, preferred_element_type=jnp.float32)
        for j in range(i, 4):
            g[n//5, n%5] = w[:, (j-i)*128:(j-i+1)*128]
            n += 1
    cc = rc(g.at[1-k], crec, ssc.at[0], rsc.at[0], other)
    cc.start()
    yield
    cc.wait_recv()
    g[k] = g[k] + crec[...]
    sends = []
    def exchange(src, buf, ax, sem):
        me = at[ax]
        for d in (1, 3, 2):
            to, dv = axis_peer(q, ax, d)
            t = rc(src(to), buf.at[me], ss.at[sem, d], rs.at[sem, me], dv)
            t.start(); sends.append(t)
        def done():
            for d in (1, 3, 2):
                fr, dv = axis_peer(q, ax, d)
                rc(src(fr), buf.at[fr], ss.at[sem, d], rs.at[sem, fr], dv).wait_recv()
        return done
    def gather(view, ax, sem):
        me = at[ax]
        for d in (1, 3, 2):
            to, dv = axis_peer(q, ax, d)
            t = rc(view(me), view(me), ss.at[sem, d], rs.at[sem, me], dv)
            t.start(); sends.append(t)
        def done():
            for d in (1, 3, 2):
                fr, dv = axis_peer(q, ax, d)
                rc(view(fr), view(fr), ss.at[sem, d], rs.at[sem, fr], dv).wait_recv()
        return done
    b1 = [bufs[3*i] for i in range(3)]; b2 = [bufs[3*i+1] for i in range(3)]; b3 = [bufs[3*i+2] for i in range(3)]
    m32 = lambda i: pl.ds(pl.multiple_of(i*32, 32), 32)
    m8 = lambda i: pl.ds(pl.multiple_of(i*8, 8), 8)
    f = []
    for i, (b0, nb, od) in enumerate(GROUPS):
        f.append(exchange(lambda t, b0=b0, nb=nb: g.at[k, pl.ds(b0, nb), m32(t)], b1[i], od[0], i*5))
    for i, (b0, nb, od) in enumerate(GROUPS):
        b1[i][at[od[0]]] = g[k, b0:b0+nb, m32(at[od[0]])]
    yield
    f2 = []
    for i, (b0, nb, od) in enumerate(GROUPS):
        f[i]()
        b1[i][4] = (b1[i][0] + b1[i][1]) + (b1[i][2] + b1[i][3])
        f2.append(exchange(lambda t, i=i: b1[i].at[4, :, m8(t)], b2[i], od[1], i*5+1))
        b2[i][at[od[1]]] = b1[i][4, :, m8(at[od[1]])]
    yield
    f3 = []
    for i, (b0, nb, od) in enumerate(GROUPS):
        f2[i]()
        b3[i][at[od[2]]] = (b2[i][0] + b2[i][1]) + (b2[i][2] + b2[i][3])
        f3.append(gather(lambda t, i=i: b3[i].at[t], od[2], i*5+2))
    yield
    f4 = []
    for i, (b0, nb, od) in enumerate(GROUPS):
        f3[i]()
        rows = lambda t, b0=b0, nb=nb, od=od: o.at[k, pl.ds(b0, nb), pl.ds(pl.multiple_of(at[od[0]]*32 + t*8, 8), 8)]
        rows(at[od[1]])[...] = (b3[i][0] + b3[i][1]) + (b3[i][2] + b3[i][3])
        f4.append(gather(rows, od[1], i*5+3))
    yield
    f5 = []
    for i, (b0, nb, od) in enumerate(GROUPS):
        f4[i]()
        f5.append(gather(lambda t, b0=b0, nb=nb: o.at[k, pl.ds(b0, nb), m32(t)], od[0], i*5+4))
    yield
    for t in f5: t()
    co = rc(o.at[k], o.at[k], ssc.at[1], rsc.at[1], other)
    co.start()
    yield
    rc(o.at[1-k], o.at[1-k], ssc.at[1], rsc.at[1], other).wait_recv()
    for t in sends: t.wait_send()
    cc.wait_send(); co.wait_send()

A = pl.ds(0, 256); Bc = pl.ds(256, 256)

def rs_scratch():
    S = 64
    V = lambda *s: pltpu.VMEM(s, jnp.float32)
    D = pltpu.SemaphoreType.DMA
    return [V(2,4,S,256), V(2,2,4,S,256), V(2,4,S,256), V(2,2,4,S,256), V(2,4,S,256), V(2,4,S,256),
            V(2,S,256), V(2,2,S,256), V(2,S,256), V(2,2,S,256), V(2,S,256), V(2,S,256), V(2,S,256),
            D((4,6)), D((4,6)), D((2,)), D((2,))]

def ag_scratch():
    D = pltpu.SemaphoreType.DMA
    return [D((4,6)), D((4,6)), D((1,)), D((1,))]

def row_ag_scratch():
    D = pltpu.SemaphoreType.DMA
    return [D((1,)), D((1,)), D((2,)), D((2,))]

def apply_t(rows, x):
    return lax.dot_general(rows, x, (((1,), (1,)), ((), ())), precision=HI, preferred_element_type=jnp.float32)

class Blocks:
    def __init__(self, ref): self.ref = ref
    def __getitem__(self, n): return self.ref[n//5, n%5]

SCALE = float(8192.0 ** 0.5)

DEEP = 1664
bf16 = jnp.bfloat16

def dot32(a, b):
    return jnp.dot(a, b, preferred_element_type=jnp.float32)

def dot3(ah, al, bh, bl):
    return dot32(ah, bh) + (dot32(ah, bl) + dot32(al, bh))

def split(v):
    h = v.astype(bf16)
    return h, (v - h.astype(jnp.float32)).astype(bf16)

class RS2:
    def __init__(self, p, o, q, nb, scr):
        (self.relA, self.finA, self.relB, self.finB, self.qa, self.qb, self.relA2, self.finA2, self.relB2, self.finB2,
         self.ra, self.rb, self.recx, self.ss, self.rs, self.sx, self.rx) = scr
        self.p, self.o, self.q, self.nb = p, o, q, nb
        y, x, z = q["y"], q["xl"], q["z"]
        self.a1 = RingRS(lambda k,h: p.at[k,h,:,:,A], y, nb["yp"], nb["ym"], self.relA, self.finA, self.ss.at[0], self.rs.at[0])
        self.b1 = RingRS(lambda k,h: p.at[:,h,k,:,Bc], z, nb["zp"], nb["zm"], self.relB, self.finB, self.ss.at[1], self.rs.at[1])
        self.a2 = RingRS(lambda k,h: self.qa.at[h,k], z, nb["zp"], nb["zm"], self.relA2, self.finA2, self.ss.at[2], self.rs.at[2])
        self.b2 = RingRS(lambda k,h: self.qb.at[h,k], y, nb["yp"], nb["ym"], self.relB2, self.finB2, self.ss.at[3], self.rs.at[3])
    def second(self):
        self.a1.finish(self.qa); self.a2.start()
        self.b1.finish(self.qb); self.b2.start()
    def second_forward(self):
        self.a2.forward(); self.b2.forward()
    def third(self):
        x = self.q["xl"]
        self.a2.finish(self.ra)
        self.cxa = rc(self.ra.at[1-x], self.recx.at[0], self.sx.at[0], self.rx.at[0], self.nb["xd"]); self.cxa.start()
        self.b2.finish(self.rb)
        self.cxb = rc(self.rb.at[1-x], self.recx.at[1], self.sx.at[1], self.rx.at[1], self.nb["xd"]); self.cxb.start()
    def end(self):
        x = self.q["xl"]
        self.cxa.wait_recv()
        self.o[:, 0:256] = self.ra[x] + self.recx[0]
        self.cxb.wait_recv()
        self.o[:, 256:512] = self.rb[x] + self.recx[1]
        for t in (self.a1, self.b1, self.a2, self.b2): t.drain()
        self.cxa.wait_send(); self.cxb.wait_send()

def start_relay(t):
    t.c[0].start(); t.c[1].start()

def start_direct(t):
    t.c[2].start(); t.c[3].start()

def split_rows(av, bv, k):
    def body(i, _):
        xx = lax.div(i, 4); zz = lax.rem(i, 4)
        for t in range(4):
            rows = pl.ds(16*t, 16)
            d = av[k, xx, zz, rows, :].astype(jnp.float32) - bv[k, xx, zz, rows, :].astype(jnp.float32)
            h, l = split(d)
            av[k, xx, zz, rows, :] = h
            bv[k, xx, zz, rows, :] = l
        return 0
    lax.fori_loop(0, 8, body, 0)

def load_start(a, b, av, bv, sem, order):
    cs = []
    for i, k in enumerate(order):
        ca = pltpu.make_async_copy(a.at[k], av.at[k], sem.at[0, i]); cb = pltpu.make_async_copy(b.at[k], bv.at[k], sem.at[1, i])
        ca.start(); cb.start()
        cs.append((ca, cb))
    return cs

def products(x, av, bv, xh, xl, p, loads, order, q, rs):
    y, z = q["y"], q["z"]
    far = lambda v: lax.rem(v+2, 4)
    up = lambda v: lax.rem(v+1, 4)
    dn = lambda v: lax.rem(v+3, 4)
    h, l = split(x[...])
    xh[...] = h
    xl[...] = l
    def blockA(k):
        w = dot3(av[k].reshape(512, DEEP), bv[k].reshape(512, DEEP), xh[:, 0:256], xl[:, 0:256])
        p[k, :, :, :, 0:256] = w.reshape(2, 4, 64, 256)
    def blockB(k):
        w = dot3(av[:, :, k].reshape(512, DEEP), bv[:, :, k].reshape(512, DEEP), xh[:, 256:512], xl[:, 256:512])
        p[:, :, k, :, 256:512] = w.reshape(4, 2, 64, 256)
    for i, k in enumerate(order):
        loads[i][0].wait(); loads[i][1].wait()
        split_rows(av, bv, k)
        if i == 0:
            blockA(far(y))
            start_relay(rs.a1)
    blockB(far(z)); start_relay(rs.b1)
    blockA(up(y)); blockA(dn(y)); start_direct(rs.a1)
    blockB(up(z)); blockB(dn(z)); start_direct(rs.b1)
    rs.a1.forward(); rs.b1.forward()
    blockA(y); blockB(z)

def row_order(q):
    y = q["y"]
    return [lax.rem(y+d, 4) for d in (2, 1, 3, 0)]

def vm(shape, dt=jnp.float32):
    return pltpu.VMEM(shape, dt)

def product_scratch():
    D = pltpu.SemaphoreType.DMA
    return [vm((4,2,4,64,DEEP), bf16), vm((4,2,4,64,DEEP), bf16), vm((DEEP,512), bf16), vm((DEEP,512), bf16), vm((4,2,4,64,512))]

ANY = pl.BlockSpec(memory_space=pl.ANY)

def call2(kernel, name, cid, ins, outs, scratch, *args):
    return pl.pallas_call(kernel, out_shape=[jax.ShapeDtypeStruct(s, d) for s, d, _ in outs],
        in_specs=list(ins), out_specs=[s for _, _, s in outs], scratch_shapes=scratch,
        compiler_params=pltpu.CompilerParams(collective_id=cid, has_side_effects=True, vmem_limit_bytes=62*2**20), name=name)(*args)

F = jnp.float32

RA = pl.ds(0, 32); RB = pl.ds(32, 32)
HALF = 256

class RS3:
    def __init__(self, p, o, q, nb, scr, cols):
        (relA, finA, relB, finB, self.qa, self.qb, relA2, finA2, relB2, finB2,
         self.ra, self.rb, self.recx, ss, rs, self.sx, self.rx) = scr
        self.o, self.q, self.nb, self.cols = o, q, nb, cols
        y, x, z = q["y"], q["xl"], q["z"]
        self.a1 = RingRS(lambda k,h: p.at[k,h,:,RA,cols], y, nb["yp"], nb["ym"], relA, finA, ss.at[0], rs.at[0])
        self.b1 = RingRS(lambda k,h: p.at[:,h,k,RB,cols], z, nb["zp"], nb["zm"], relB, finB, ss.at[1], rs.at[1])
        self.a2 = RingRS(lambda k,h: self.qa.at[h,k], z, nb["zp"], nb["zm"], relA2, finA2, ss.at[2], rs.at[2])
        self.b2 = RingRS(lambda k,h: self.qb.at[h,k], y, nb["yp"], nb["ym"], relB2, finB2, ss.at[3], rs.at[3])
    def forward(self):
        self.a1.forward(); self.b1.forward()
    def second(self):
        self.a1.finish(self.qa); self.a2.start()
        self.b1.finish(self.qb); self.b2.start()
    def second_forward(self):
        self.a2.forward(); self.b2.forward()
    def third(self):
        x = self.q["xl"]
        self.a2.finish(self.ra)
        self.cxa = rc(self.ra.at[1-x], self.recx.at[0], self.sx.at[0], self.rx.at[0], self.nb["xd"]); self.cxa.start()
        self.b2.finish(self.rb)
        self.cxb = rc(self.rb.at[1-x], self.recx.at[1], self.sx.at[1], self.rx.at[1], self.nb["xd"]); self.cxb.start()
    def end(self):
        x = self.q["xl"]
        self.cxa.wait_recv()
        self.o[0:32, self.cols] = self.ra[x] + self.recx[0]
        self.cxb.wait_recv()
        self.o[32:64, self.cols] = self.rb[x] + self.recx[1]
        for t in (self.a1, self.b1, self.a2, self.b2): t.drain()
        self.cxa.wait_send(); self.cxb.wait_send()

def rs3_scratch():
    S = 32
    D = pltpu.SemaphoreType.DMA
    V = vm
    return [V((2,4,S,256)), V((2,2,4,S,256)), V((2,4,S,256)), V((2,2,4,S,256)), V((2,4,S,256)), V((2,4,S,256)),
            V((2,S,256)), V((2,2,S,256)), V((2,S,256)), V((2,2,S,256)), V((2,S,256)), V((2,S,256)), V((2,S,256)),
            D((4,6)), D((4,6)), D((2,)), D((2,))]
NRS = 17

class AG3:
    def __init__(self, o, q, nb, scr, cols):
        ss, rs, sx, rx = scr
        y, x, z = q["y"], q["xl"], q["z"]
        yp, ym, zp, zm, xd = nb["yp"], nb["ym"], nb["zp"], nb["zm"], nb["xd"]
        all_rows = pl.ds(0, 64)
        self.cx = rc(o.at[y,x,z,all_rows,cols], o.at[y,x,z,all_rows,cols], sx.at[0], rx.at[0], xd)
        self.cxr = rc(o.at[y,1-x,z,all_rows,cols], o.at[y,1-x,z,all_rows,cols], sx.at[0], rx.at[0], xd)
        self.a1 = RingAG(lambda k,h: o.at[y,h,k,RA,cols], z, zp, zm, ss.at[0], rs.at[0])
        self.b1 = RingAG(lambda k,h: o.at[k,h,z,RB,cols], y, yp, ym, ss.at[1], rs.at[1])
        self.a2 = RingAG(lambda k,h: o.at[k,h,:,RA,cols], y, yp, ym, ss.at[2], rs.at[2])
        self.b2 = RingAG(lambda k,h: o.at[:,h,k,RB,cols], z, zp, zm, ss.at[3], rs.at[3])
    def first(self):
        self.cx.start()
    def second(self):
        self.cxr.wait_recv()
        self.a1.start(); self.b1.start()
    def second_forward(self):
        self.a1.forward(); self.b1.forward()
    def third(self):
        self.a1.finish(); self.a2.start()
        self.b1.finish(); self.b2.start()
    def third_forward(self):
        self.a2.forward(); self.b2.forward()
    def near(self, t):
        t.r[2].wait_recv(); t.r[3].wait_recv()
    def far(self, t):
        t.r[4].wait_recv(); t.r[5].wait_recv()
    def drain(self):
        for t in (self.a1, self.b1, self.a2, self.b2): t.drain()
        self.cx.wait_send()

QROWS = DEEP // 4

def quarter(h, k):
    return pl.ds(pl.multiple_of((h*2 + k)*QROWS, 32), QROWS)

class RowRS:
    def __init__(self, w, o, q, nb, scr, cols):
        self.rec1, self.qf, self.rec2, s1, r1, s2, r2 = scr
        self.w, self.o, self.cols = w, o, cols
        h, k = self.h, self.k = q["xh"], q["core"]
        self.c = [rc(w.at[quarter(1-h, 1-k), cols], self.rec1.at[0], s1.at[0], r1.at[0], nb["other"]),
                  rc(w.at[quarter(h, 1-k), cols], self.rec1.at[1], s1.at[1], r1.at[1], nb["other"])]
        self.c2 = rc(self.qf, self.rec2, s2.at[0], r2.at[0], nb["far"])
    def start(self):
        for t in self.c: t.start()
    def middle(self):
        self.c[0].wait_recv()
        self.qf[...] = self.w[quarter(1-self.h, self.k), self.cols] + self.rec1[0]
        self.c2.start()
        self.c[1].wait_recv()
        self.o[:, self.cols] = self.w[quarter(self.h, self.k), self.cols] + self.rec1[1]
    def end(self):
        self.c2.wait_recv()
        self.o[:, self.cols] = self.o[:, self.cols] + self.rec2[...]
        for t in self.c: t.wait_send()
        self.c2.wait_send()

def row3_scratch():
    D = pltpu.SemaphoreType.DMA
    n = QROWS
    return [vm((2,n,HALF)), vm((n,HALF)), vm((n,HALF)), D((2,)), D((2,)), D((1,)), D((1,))]
NROW = 7

class RowAG:
    def __init__(self, o, q, nb, scr, cols):
        s1, r1, s2, r2 = scr
        h, k = q["xh"], q["core"]
        v = lambda a, b: o.at[quarter(a, b), cols]
        self.cf = rc(v(h,k), v(h,k), s1.at[0], r1.at[0], nb["far"])
        self.cfr = rc(v(1-h,k), v(1-h,k), s1.at[0], r1.at[0], nb["far"])
        self.co = rc(v(h,k), v(h,k), s2.at[0], r2.at[0], nb["other"])
        self.cor = rc(v(h,1-k), v(h,1-k), s2.at[0], r2.at[0], nb["other"])
        self.co2 = rc(v(1-h,k), v(1-h,k), s2.at[1], r2.at[1], nb["other"])
        self.co2r = rc(v(1-h,1-k), v(1-h,1-k), s2.at[1], r2.at[1], nb["other"])
    def start(self):
        self.cf.start(); self.co.start()
    def forward(self):
        self.cfr.wait_recv(); self.co2.start()
    def finish(self):
        self.cor.wait_recv(); self.co2r.wait_recv()
    def drain(self):
        self.cf.wait_send(); self.co.wait_send(); self.co2.wait_send()

XLAST = [(0, 2, "yzx"), (2, 2, "zyx"), (4, 1, "yzx")]
COLS = [pl.ds(0, HALF), pl.ds(HALF, HALF)]

def neighbours(r, c, q):
    nb = col_neighbours(r, q)
    nb.update(row_neighbours(c, q))
    return nb

def transpose_pieces(av, bv, th, tl, lo, hi):
    def body(i, _):
        cols = pl.ds(pl.multiple_of(i*128, 128), 128)
        for n in range(13):
            lanes = slice(n*128, n*128+128)
            if hi <= 8:
                y = lax.div(i, 2); x = lax.rem(i, 2)
                u, v = av[y, x, :, 0:32, lanes], bv[y, x, :, 0:32, lanes]
            else:
                z = lax.div(i - 8, 2); g = lax.rem(i, 2)*2
                u, v = av[pl.ds(g, 2), :, z, 32:64, lanes], bv[pl.ds(g, 2), :, z, 32:64, lanes]
            d = u.reshape(128, 128).astype(jnp.float32) + v.reshape(128, 128).astype(jnp.float32)
            h, l = split(d.T)
            th[lanes, cols] = h
            tl[lanes, cols] = l
        return 0
    lax.fori_loop(lo, hi, body, 0)

def sketch3_kernel(a, b, x, o, th_o, tl_o, av, bv, xh, xl, p, th, tl, lsem, osem, *scr):
    r, c, q = mesh_place()
    order = row_order(q)
    loads = load_start(a, b, av, bv, lsem, order)
    nb = col_neighbours(r, q)
    barrier(list(nb.values()))
    rs = RS2(p, o, q, nb, scr)
    products(x, av, bv, xh, xl, p, loads, order, q, rs)
    transpose_pieces(av, bv, th, tl, 0, 8)
    transpose_pieces(av, bv, th, tl, 8, 12)
    rs.second()
    rs.second_forward()
    transpose_pieces(av, bv, th, tl, 12, 16)
    outs = [pltpu.make_async_copy(th, th_o, osem.at[0]), pltpu.make_async_copy(tl, tl_o, osem.at[1])]
    for t in outs: t.start()
    rs.third()
    rs.end()
    for t in outs: t.wait()

def sketch3(a, b, x):
    D = pltpu.SemaphoreType.DMA
    return call2(sketch3_kernel, "sketch", 1, (ANY, ANY, VM), [((64,512), F, VM), ((DEEP,2048), bf16, ANY), ((DEEP,2048), bf16, ANY)],
        product_scratch() + [vm((DEEP,2048), bf16), vm((DEEP,2048), bf16), D((2,4)), D((2,))] + rs_scratch(), a, b, x)

up = lambda v: lax.rem(v+1, 4)
dn = lambda v: lax.rem(v+3, 4)
far = lambda v: lax.rem(v+2, 4)

def steps(gen, n):
    for _ in range(n):
        next(gen, None)

def cosketch3_kernel(own, th_i, tl_i, raw, x1, gb, o, th, tl, w, lsem, *scr):
    r, c, q = mesh_place()
    ct = [pltpu.make_async_copy(th_i, th, lsem.at[0]), pltpu.make_async_copy(tl_i, tl, lsem.at[1])]
    for t in ct: t.start()
    nb = neighbours(r, c, q)
    y, z = q["y"], q["z"]
    o[y, q["xl"], z] = own[...]
    barrier(gram_devices(c, q))
    s = list(scr)
    take = lambda n: [s.pop(0) for _ in range(n)]
    gr = gram_steps(own, gb, c, q, take(NGRAM))
    ag = [AG3(o, q, nb, take(4), COLS[i]) for i in range(2)]
    row = [RowRS(w, raw, q, nb, take(NROW), COLS[i]) for i in range(2)]
    ch = chol_steps(Blocks(gb), x1)
    def blockA(i, k, first=False):
        cols = pl.ds(pl.multiple_of(k*256, 256), 256)
        sh, sl = split(o[k, :, :, RA, COLS[i]].reshape(256, HALF))
        v = dot3(th[:, cols], tl[:, cols], sh, sl)
        w[:, COLS[i]] = v if first else w[:, COLS[i]] + v
    def blockB(i, k):
        cols = pl.ds(pl.multiple_of(1024 + k*256, 256), 256)
        sh, sl = split(o[:, :, k, RB, COLS[i]].reshape(256, HALF))
        w[:, COLS[i]] = w[:, COLS[i]] + dot3(th[:, cols], tl[:, cols], sh, sl)
    ag[0].first(); ag[1].first(); next(gr)
    ag[0].second(); next(gr)
    ag[0].second_forward(); next(gr)
    ag[0].third(); ag[1].second(); next(gr)
    for t in ct: t.wait()
    blockA(0, y, True); blockB(0, z)
    ag[0].third_forward(); ag[1].second_forward(); next(gr)
    ag[0].near(ag[0].a2); blockA(0, up(y)); blockA(0, dn(y))
    ag[0].near(ag[0].b2); ag[1].third(); next(gr)
    blockB(0, up(z)); blockB(0, dn(z))
    ag[0].far(ag[0].a2); blockA(0, far(y))
    ag[0].far(ag[0].b2); blockB(0, far(z))
    row[0].start(); next(gr)
    blockA(1, y, True); blockB(1, z)
    ag[1].third_forward()
    row[0].middle()
    run(gr)
    steps(ch, 5)
    ag[1].near(ag[1].a2); blockA(1, up(y)); blockA(1, dn(y))
    ag[1].near(ag[1].b2); blockB(1, up(z)); blockB(1, dn(z))
    steps(ch, 1)
    ag[1].far(ag[1].a2); blockA(1, far(y))
    ag[1].far(ag[1].b2); blockB(1, far(z))
    row[1].start()
    steps(ch, 2)
    row[0].end()
    row[1].middle()
    run(ch)
    row[1].end()
    for t in ag: t.drain()

def cosketch3(own, th, tl):
    D = pltpu.SemaphoreType.DMA
    return call2(cosketch3_kernel, "cosketch", 2, (VM, ANY, ANY), [((QROWS,512), F, VM), ((512,512), F, VM)],
        [vm((2,5,B,B)), vm((4,2,4,64,512)), vm((DEEP,2048), bf16), vm((DEEP,2048), bf16), vm((DEEP,512)), D((2,))]
        + gram_scratch() + ag_scratch()*2 + row3_scratch()*2, own, th, tl)

def resketch3_kernel(a, b, raw, x1, out, o, x2, gb, own, co, last, g3, x3, av, bv, xh, xl, p, lsem, *scr):
    r, c, q = mesh_place()
    order = row_order(q)
    loads = load_start(a, b, av, bv, lsem, order)
    nb = neighbours(r, c, q)
    y, z = q["y"], q["z"]
    mine = quarter(q["xh"], q["core"])
    s = list(scr)
    take = lambda n: [s.pop(0) for _ in range(n)]
    gr = gram_steps(own, gb, c, q, take(NGRAM), XLAST)
    rg = [RowAG(co, q, nb, take(4), COLS[i]) for i in range(2)]
    rs = [RS3(p, o, q, nb, take(NRS), COLS[i]) for i in range(2)]
    ch = chol_steps(Blocks(gb), x2)
    def normed(i):
        n = (i+1)*HALF
        v = apply_t(raw[:, 0:n], x1[i*HALF:n, 0:n])
        own[:, COLS[i]] = v
        co[mine, COLS[i]] = v
    def parts(i):
        h, l = split(co[:, COLS[i]])
        xh[:, COLS[i]] = h
        xl[:, COLS[i]] = l
    def blockA(i, k):
        v = dot3(av[k, :, :, RA].reshape(256, DEEP), bv[k, :, :, RA].reshape(256, DEEP), xh[:, COLS[i]], xl[:, COLS[i]])
        p[k, :, :, RA, COLS[i]] = v.reshape(2, 4, 32, HALF)
    def blockB(i, k):
        v = dot3(av[:, :, k, RB].reshape(256, DEEP), bv[:, :, k, RB].reshape(256, DEEP), xh[:, COLS[i]], xl[:, COLS[i]])
        p[:, :, k, RB, COLS[i]] = v.reshape(4, 2, 32, HALF)
    def first_blocks(i):
        blockA(i, far(y)); start_relay(rs[i].a1)
        blockB(i, far(z)); start_relay(rs[i].b1)
    def other_blocks(i):
        blockA(i, up(y)); blockA(i, dn(y)); start_direct(rs[i].a1)
        blockB(i, up(z)); blockB(i, dn(z)); start_direct(rs[i].b1)
    def own_blocks(i):
        blockA(i, y); blockB(i, z)
    def ready(i):
        loads[i][0].wait(); loads[i][1].wait()
        split_rows(av, bv, order[i])
    barrier(gram_devices(c, q))
    normed(0); rg[0].start()
    normed(1); next(gr)
    ready(0); ready(1); next(gr)
    ready(2); ready(3); next(gr)
    rg[0].forward(); rg[1].start(); next(gr)
    rg[0].finish(); parts(0)
    first_blocks(0); other_blocks(0); next(gr)
    rs[0].forward(); own_blocks(0); next(gr)
    rg[1].forward(); rg[1].finish(); parts(1)
    first_blocks(1); next(gr)
    rs[0].second()
    other_blocks(1); run(gr)
    rs[0].second_forward(); rs[1].forward()
    own_blocks(1)
    steps(ch, 1)
    rs[0].third()
    steps(ch, 3)
    rs[1].second(); rs[0].end()
    steps(ch, 2)
    rs[1].second_forward()
    steps(ch, 2)
    rs[1].third()
    steps(ch, 2)
    rs[1].end()
    run(ch)
    for t in rg: t.drain()
    last[...] = apply_t(o[...], x2[...])
    run(gram_steps(last, g3, c, q, take(NGRAM)))
    run(chol_steps(Blocks(g3), x3, 0))
    out[...] = SCALE * apply_t(last[...], x3[...])

def resketch3(a, b, raw, x1):
    D = pltpu.SemaphoreType.DMA
    return call2(resketch3_kernel, "resketch", 3, (ANY, ANY, VM, VM), [((64,512), F, VM)],
        [vm((64,512)), vm((512,512)), vm((2,5,B,B)), vm((QROWS,512)), vm((DEEP,512)), vm((64,512)), vm((2,5,B,B)), vm((512,512))]
        + product_scratch() + [D((2,4))] + gram_scratch() + row_ag_scratch()*2 + rs3_scratch()*2 + gram_scratch(), a, b, raw, x1)[0]
def shards(adjusted_weight, base_weight, test_matrix):
    rows = (4, 2, 4, 64, DEEP)
    a, b = adjusted_weight.reshape(rows), base_weight.reshape(rows)
    own, th, tl = sketch3(a, b, test_matrix)
    raw, x1 = cosketch3(own, th, tl)
    return resketch3(a, b, raw, x1)


def solution(mesh):
    return jax.shard_map(
        shards,
        mesh=mesh,
        in_specs=(P("row", "col"), P("row", "col"), P("col", None)),
        out_specs=P(("row", "col"), None),
        check_vma=False,
    )
```

```python
import jax
import jax.numpy as jnp
from jax import lax
from jax.experimental import pallas as pl
from jax.experimental.pallas import tpu as pltpu
from jax.sharding import PartitionSpec as P

MESH = pl.DeviceIdType.MESH
VM = pl.BlockSpec(memory_space=pltpu.VMEM)

def barrier(devs):
    sem = pltpu.get_barrier_semaphore()
    for d in devs:
        pl.semaphore_signal(sem, inc=1, device_id=d, device_id_type=MESH)
    pl.semaphore_wait(sem, len(devs))

def rc(src, dst, ssem, rsem, dev):
    return pltpu.make_async_remote_copy(src_ref=src, dst_ref=dst, send_sem=ssem, recv_sem=rsem, device_id=dev, device_id_type=MESH)

class RingRS:
    def __init__(self, part, me, devp, devm, relay, fin, ssem, rsem):
        self.part, self.me, self.devp, self.devm, self.relay, self.fin = part, me, devp, devm, relay, fin
        up = lax.rem(me+1, 4); dn = lax.rem(me+3, 4); far = lax.rem(me+2, 4)
        self.up, self.dn = up, dn
        self.c = [
            rc(part(far, 0), relay.at[0], ssem.at[0], rsem.at[0], devp),
            rc(part(far, 1), relay.at[1], ssem.at[1], rsem.at[1], devm),
            rc(part(up, 1), fin.at[0, 1], ssem.at[2], rsem.at[2], devp),
            rc(part(dn, 0), fin.at[1, 0], ssem.at[3], rsem.at[3], devm),
            rc(relay.at[0], fin.at[0, 0], ssem.at[4], rsem.at[4], devp),
            rc(relay.at[1], fin.at[1, 1], ssem.at[5], rsem.at[5], devm),
        ]
    def start(self):
        for i in range(4): self.c[i].start()
    def forward(self):
        self.c[0].wait_recv()
        self.relay[0] = self.relay[0] + self.part(self.up, 0)[...]
        self.c[4].start()
        self.c[1].wait_recv()
        self.relay[1] = self.relay[1] + self.part(self.dn, 1)[...]
        self.c[5].start()
    def finish(self, out):
        for i in (2, 3, 4, 5): self.c[i].wait_recv()
        for h in range(2):
            out[h] = self.part(self.me, h)[...] + self.fin[0, h] + self.fin[1, h]
    def drain(self):
        for i in range(6): self.c[i].wait_send()

class RingAG:
    def __init__(self, part, me, devp, devm, ssem, rsem):
        up = lax.rem(me+1, 4); dn = lax.rem(me+3, 4)
        far = lax.rem(me+2, 4)
        self.s = [rc(part(me,0), part(me,0), ssem.at[0], rsem.at[0], devp),
                  rc(part(me,1), part(me,1), ssem.at[1], rsem.at[1], devm),
                  rc(part(me,1), part(me,1), ssem.at[2], rsem.at[2], devp),
                  rc(part(me,0), part(me,0), ssem.at[3], rsem.at[3], devm),
                  rc(part(dn,0), part(dn,0), ssem.at[4], rsem.at[4], devp),
                  rc(part(up,1), part(up,1), ssem.at[5], rsem.at[5], devm)]
        self.r = [rc(part(dn,0), part(dn,0), ssem.at[0], rsem.at[0], devp),
                  rc(part(up,1), part(up,1), ssem.at[1], rsem.at[1], devm),
                  rc(part(dn,1), part(dn,1), ssem.at[2], rsem.at[2], devp),
                  rc(part(up,0), part(up,0), ssem.at[3], rsem.at[3], devm),
                  rc(part(far,0), part(far,0), ssem.at[4], rsem.at[4], devp),
                  rc(part(far,1), part(far,1), ssem.at[5], rsem.at[5], devm)]
    def start(self):
        for i in range(4): self.s[i].start()
    def forward(self):
        self.r[0].wait_recv(); self.s[4].start()
        self.r[1].wait_recv(); self.s[5].start()
    def finish(self):
        for i in (2,3,4,5): self.r[i].wait_recv()
    def drain(self):
        for i in range(6): self.s[i].wait_send()

HI = lax.Precision.HIGHEST
B = 128

def mm(a, b):
    return jnp.dot(a, b, precision=HI, preferred_element_type=jnp.float32)

def inverse(v):
    return 1.0 / v

def leaf_inverse(a, pause=0):
    n = B // 8
    lane = lax.broadcasted_iota(jnp.int32, (1, B), 1)
    sub = lax.broadcasted_iota(jnp.int32, (8, B), 0)
    lane8 = lax.broadcasted_iota(jnp.int32, (8, B), 1)
    ch = [a[8*t:8*t+8, :] for t in range(n)]
    drow = jnp.zeros((8, B), jnp.float32)
    for t in range(n):
        drow = drow + jnp.where(lane8 == sub + 8*t, ch[t], 0.0)
    srow = lax.rsqrt(jnp.sum(drow, axis=0, keepdims=True))
    srow8 = jnp.broadcast_to(srow, (8, B))
    for t in range(n):
        scol = jnp.sum(jnp.where(lane8 == sub + 8*t, srow8, 0.0), axis=1, keepdims=True)
        ch[t] = ch[t] * srow8 * scol
    for j in range(0, B, 4):
        if pause and j and j % pause == 0:
            yield
        t0, s = divmod(j, 8)
        c = [jnp.broadcast_to(ch[t0][:, j+b:j+b+1], (8, B)) for b in range(4)]
        pv = lambda i, k: c[k][s+i:s+i+1]
        piv = [lane == j+b for b in range(4)]
        inpiv = (lane >= j) & (lane < j+4)
        R = [jnp.where(piv[b], 1.0, jnp.where(inpiv, 0.0, ch[t0][s+b:s+b+1, :])) for b in range(4)]
        p, q, d = pv(0, 0), pv(1, 0), pv(1, 1)
        det = p*d - q*q
        idet = inverse(det)
        ip, iq, iD = d*idet, -q*idet, p*idet
        t00 = pv(2,0)*ip + pv(2,1)*iq; t01 = pv(2,0)*iq + pv(2,1)*iD
        t10 = pv(3,0)*ip + pv(3,1)*iq; t11 = pv(3,0)*iq + pv(3,1)*iD
        s00 = pv(2,2) - (t00*pv(2,0) + t01*pv(2,1))
        s10 = pv(3,2) - (t10*pv(2,0) + t11*pv(2,1))
        s11 = pv(3,3) - (t10*pv(3,0) + t11*pv(3,1))
        dets = s00*s11 - s10*s10
        idets = inverse(dets)
        v0 = R[2] - (t00*R[0] + t01*R[1])
        v1 = R[3] - (t10*R[0] + t11*R[1])
        w2 = (s11*v0 - s10*v1) * idets
        w3 = (s00*v1 - s10*v0) * idets
        w0 = (ip*R[0] + iq*R[1]) - (t00*w2 + t10*w3)
        w1 = (iq*R[0] + iD*R[1]) - (t01*w2 + t11*w3)
        W = [jnp.broadcast_to(w, (8, B)) for w in (w0, w1, w2, w3)]
        ipp = 1.0 / p; iss = 1.0 / s00
        F = [R[0]*lax.rsqrt(p), (R[1] - (q*ipp)*R[0])*lax.rsqrt(det*ipp), v0*lax.rsqrt(s00), (v1 - (s10*iss)*v0)*lax.rsqrt(dets*iss)]
        inpiv8 = (lane8 >= j) & (lane8 < j+4)
        for t in range(t0, n):
            if t == t0:
                m = [jnp.where(sub > s+3, c[b], 0.0) for b in range(4)]
            else:
                m = [jnp.broadcast_to(ch[t][:, j+b:j+b+1], (8, B)) for b in range(4)]
            u = (m[0]*W[0] + m[1]*W[1]) + (m[2]*W[2] + m[3]*W[3])
            ch[t] = jnp.where(inpiv8, 0.0, ch[t]) - u
            if t == t0:
                for b in range(4):
                    ch[t] = jnp.where(sub == s+b, jnp.broadcast_to(jnp.where(lane <= j+b, F[b], 0.0), (8, B)), ch[t])

    return jnp.concatenate([x * srow8 for x in ch], 0)

GROUPS = [(0, 2, "zyx"), (2, 2, "yxz"), (4, 1, "xzy")]


def chol_load(g, x_ref):
    n = 0
    for i in range(4):
        for k in range(4):
            if k >= i:
                x_ref[i*B:(i+1)*B, k*B:(k+1)*B] = g[n]
                n += 1
            else:
                x_ref[i*B:(i+1)*B, k*B:(k+1)*B] = jnp.zeros((B, B), jnp.float32)

def chol_steps(g, x_ref, pause=32):
    chol_load(g, x_ref)
    for J in range(4):
        lo, hi = J*B, (J+1)*B
        x = yield from leaf_inverse(x_ref[lo:hi, lo:hi], pause)
        x_ref[lo:hi, lo:hi] = x
        if J > 0:
            x_ref[lo:hi, 0:lo] = mm(x, x_ref[lo:hi, 0:lo])
        if J < 3:
            right = mm(x, x_ref[lo:hi, hi:])
            rt = right.T
            x_ref[lo:hi, hi:] = right
            x_ref[hi:, hi:] = x_ref[hi:, hi:] - mm(rt, right)
            left = mm(rt, x_ref[lo:hi, 0:hi])
            if J > 0:
                x_ref[hi:, 0:lo] = x_ref[hi:, 0:lo] - left[:, 0:lo]
            x_ref[hi:, lo:hi] = -left[:, lo:hi]
            x_ref[lo:hi, hi:] = jnp.zeros_like(right)
        yield

def run(gen):
    for _ in gen:
        pass

def mesh_place():
    r = lax.axis_index("row"); c = lax.axis_index("col")
    q = {"xh": lax.div(r, 2), "core": lax.rem(r, 2), "y": lax.div(c, 8), "xl": lax.rem(lax.div(c, 4), 2), "z": lax.rem(c, 4)}
    q["x"] = q["xh"]*2 + q["xl"]
    return r, c, q

def col_neighbours(r, q):
    def dev(y, x, z):
        return (r, y*8 + x*4 + z)
    y, x, z = q["y"], q["xl"], q["z"]
    return {"yp": dev(lax.rem(y+1,4),x,z), "ym": dev(lax.rem(y+3,4),x,z), "zp": dev(y,x,lax.rem(z+1,4)), "zm": dev(y,x,lax.rem(z+3,4)), "xd": dev(y,1-x,z)}

def row_neighbours(c, q):
    h, k = q["xh"], q["core"]
    return {"other": (h*2 + 1-k, c), "far": ((1-h)*2 + k, c)}

def axis_peer(q, ax, d):
    t = dict(q); t[ax] = lax.rem(q[ax]+d, 4)
    return t[ax], (lax.div(t["x"], 2)*2 + t["core"], t["y"]*8 + lax.rem(t["x"], 2)*4 + t["z"])

def gram_devices(c, q):
    return [row_neighbours(c, q)["other"]] + [axis_peer(q, ax, d)[1] for ax in "xyz" for d in (1, 2, 3)]

def gram_scratch():
    V = lambda *sh: pltpu.VMEM(sh, jnp.float32)
    D = pltpu.SemaphoreType.DMA
    bufs = [V(2,5,128,128), V(5,128,128)]
    for b0, nb, od in GROUPS:
        bufs += [V(5, nb, 32, 128), V(4, nb, 8, 128), V(4, nb, 8, 128)]
    return bufs + [D((2,)), D((2,)), D((15,4)), D((15,4))]
NGRAM = 15


def gram_steps(s, o, c, q, scr, GROUPS=GROUPS):
    g, crec, bufs, (ssc, rsc, ss, rs) = scr[0], scr[1], scr[2:11], scr[11:]
    k = q["core"]; at = q
    other = row_neighbours(c, q)["other"]
    n = 0
    for i in range(4):
        w = jnp.einsum("ni,nk->ik", s[:, i*128:(i+1)*128], s[:, i*128:], precision=HI, preferred_element_type=jnp.float32)
        for j in range(i, 4):
            g[n//5, n%5] = w[:, (j-i)*128:(j-i+1)*128]
            n += 1
    cc = rc(g.at[1-k], crec, ssc.at[0], rsc.at[0], other)
    cc.start()
    yield
    cc.wait_recv()
    g[k] = g[k] + crec[...]
    sends = []
    def exchange(src, buf, ax, sem):
        me = at[ax]
        for d in (1, 3, 2):
            to, dv = axis_peer(q, ax, d)
            t = rc(src(to), buf.at[me], ss.at[sem, d], rs.at[sem, me], dv)
            t.start(); sends.append(t)
        def done():
            for d in (1, 3, 2):
                fr, dv = axis_peer(q, ax, d)
                rc(src(fr), buf.at[fr], ss.at[sem, d], rs.at[sem, fr], dv).wait_recv()
        return done
    def gather(view, ax, sem):
        me = at[ax]
        for d in (1, 3, 2):
            to, dv = axis_peer(q, ax, d)
            t = rc(view(me), view(me), ss.at[sem, d], rs.at[sem, me], dv)
            t.start(); sends.append(t)
        def done():
            for d in (1, 3, 2):
                fr, dv = axis_peer(q, ax, d)
                rc(view(fr), view(fr), ss.at[sem, d], rs.at[sem, fr], dv).wait_recv()
        return done
    b1 = [bufs[3*i] for i in range(3)]; b2 = [bufs[3*i+1] for i in range(3)]; b3 = [bufs[3*i+2] for i in range(3)]
    m32 = lambda i: pl.ds(pl.multiple_of(i*32, 32), 32)
    m8 = lambda i: pl.ds(pl.multiple_of(i*8, 8), 8)
    f = []
    for i, (b0, nb, od) in enumerate(GROUPS):
        f.append(exchange(lambda t, b0=b0, nb=nb: g.at[k, pl.ds(b0, nb), m32(t)], b1[i], od[0], i*5))
    for i, (b0, nb, od) in enumerate(GROUPS):
        b1[i][at[od[0]]] = g[k, b0:b0+nb, m32(at[od[0]])]
    yield
    f2 = []
    for i, (b0, nb, od) in enumerate(GROUPS):
        f[i]()
        b1[i][4] = (b1[i][0] + b1[i][1]) + (b1[i][2] + b1[i][3])
        f2.append(exchange(lambda t, i=i: b1[i].at[4, :, m8(t)], b2[i], od[1], i*5+1))
        b2[i][at[od[1]]] = b1[i][4, :, m8(at[od[1]])]
    yield
    f3 = []
    for i, (b0, nb, od) in enumerate(GROUPS):
        f2[i]()
        b3[i][at[od[2]]] = (b2[i][0] + b2[i][1]) + (b2[i][2] + b2[i][3])
        f3.append(gather(lambda t, i=i: b3[i].at[t], od[2], i*5+2))
    yield
    f4 = []
    for i, (b0, nb, od) in enumerate(GROUPS):
        f3[i]()
        rows = lambda t, b0=b0, nb=nb, od=od: o.at[k, pl.ds(b0, nb), pl.ds(pl.multiple_of(at[od[0]]*32 + t*8, 8), 8)]
        rows(at[od[1]])[...] = (b3[i][0] + b3[i][1]) + (b3[i][2] + b3[i][3])
        f4.append(gather(rows, od[1], i*5+3))
    yield
    f5 = []
    for i, (b0, nb, od) in enumerate(GROUPS):
        f4[i]()
        f5.append(gather(lambda t, b0=b0, nb=nb: o.at[k, pl.ds(b0, nb), m32(t)], od[0], i*5+4))
    yield
    for t in f5: t()
    co = rc(o.at[k], o.at[k], ssc.at[1], rsc.at[1], other)
    co.start()
    yield
    rc(o.at[1-k], o.at[1-k], ssc.at[1], rsc.at[1], other).wait_recv()
    for t in sends: t.wait_send()
    cc.wait_send(); co.wait_send()

A = pl.ds(0, 256); Bc = pl.ds(256, 256)

def rs_scratch():
    S = 64
    V = lambda *s: pltpu.VMEM(s, jnp.float32)
    D = pltpu.SemaphoreType.DMA
    return [V(2,4,S,256), V(2,2,4,S,256), V(2,4,S,256), V(2,2,4,S,256), V(2,4,S,256), V(2,4,S,256),
            V(2,S,256), V(2,2,S,256), V(2,S,256), V(2,2,S,256), V(2,S,256), V(2,S,256), V(2,S,256),
            D((4,6)), D((4,6)), D((2,)), D((2,))]

def ag_scratch():
    D = pltpu.SemaphoreType.DMA
    return [D((4,6)), D((4,6)), D((1,)), D((1,))]

def row_ag_scratch():
    D = pltpu.SemaphoreType.DMA
    return [D((1,)), D((1,)), D((2,)), D((2,))]

def apply_t(rows, x):
    return lax.dot_general(rows, x, (((1,), (1,)), ((), ())), precision=HI, preferred_element_type=jnp.float32)

class Blocks:
    def __init__(self, ref): self.ref = ref
    def __getitem__(self, n): return self.ref[n//5, n%5]

SCALE = float(8192.0 ** 0.5)

DEEP = 1664
bf16 = jnp.bfloat16

def dot32(a, b):
    return jnp.dot(a, b, preferred_element_type=jnp.float32)

def dot3(ah, al, bh, bl):
    return dot32(ah, bh) + (dot32(ah, bl) + dot32(al, bh))

def split(v):
    h = v.astype(bf16)
    return h, (v - h.astype(jnp.float32)).astype(bf16)

class RS2:
    def __init__(self, p, o, q, nb, scr):
        (self.relA, self.finA, self.relB, self.finB, self.qa, self.qb, self.relA2, self.finA2, self.relB2, self.finB2,
         self.ra, self.rb, self.recx, self.ss, self.rs, self.sx, self.rx) = scr
        self.p, self.o, self.q, self.nb = p, o, q, nb
        y, x, z = q["y"], q["xl"], q["z"]
        self.a1 = RingRS(lambda k,h: p.at[k,h,:,:,A], y, nb["yp"], nb["ym"], self.relA, self.finA, self.ss.at[0], self.rs.at[0])
        self.b1 = RingRS(lambda k,h: p.at[:,h,k,:,Bc], z, nb["zp"], nb["zm"], self.relB, self.finB, self.ss.at[1], self.rs.at[1])
        self.a2 = RingRS(lambda k,h: self.qa.at[h,k], z, nb["zp"], nb["zm"], self.relA2, self.finA2, self.ss.at[2], self.rs.at[2])
        self.b2 = RingRS(lambda k,h: self.qb.at[h,k], y, nb["yp"], nb["ym"], self.relB2, self.finB2, self.ss.at[3], self.rs.at[3])
    def second(self):
        self.a1.finish(self.qa); self.a2.start()
        self.b1.finish(self.qb); self.b2.start()
    def second_forward(self):
        self.a2.forward(); self.b2.forward()
    def third(self):
        x = self.q["xl"]
        self.a2.finish(self.ra)
        self.cxa = rc(self.ra.at[1-x], self.recx.at[0], self.sx.at[0], self.rx.at[0], self.nb["xd"]); self.cxa.start()
        self.b2.finish(self.rb)
        self.cxb = rc(self.rb.at[1-x], self.recx.at[1], self.sx.at[1], self.rx.at[1], self.nb["xd"]); self.cxb.start()
    def end(self):
        x = self.q["xl"]
        self.cxa.wait_recv()
        self.o[:, 0:256] = self.ra[x] + self.recx[0]
        self.cxb.wait_recv()
        self.o[:, 256:512] = self.rb[x] + self.recx[1]
        for t in (self.a1, self.b1, self.a2, self.b2): t.drain()
        self.cxa.wait_send(); self.cxb.wait_send()

def start_relay(t):
    t.c[0].start(); t.c[1].start()

def start_direct(t):
    t.c[2].start(); t.c[3].start()

def split_rows(av, bv, k):
    def body(i, _):
        xx = lax.div(i, 4); zz = lax.rem(i, 4)
        for t in range(4):
            rows = pl.ds(16*t, 16)
            d = av[k, xx, zz, rows, :].astype(jnp.float32) - bv[k, xx, zz, rows, :].astype(jnp.float32)
            h, l = split(d)
            av[k, xx, zz, rows, :] = h
            bv[k, xx, zz, rows, :] = l
        return 0
    lax.fori_loop(0, 8, body, 0)

def load_start(a, b, av, bv, sem, order):
    cs = []
    for i, k in enumerate(order):
        ca = pltpu.make_async_copy(a.at[k], av.at[k], sem.at[0, i]); cb = pltpu.make_async_copy(b.at[k], bv.at[k], sem.at[1, i])
        ca.start(); cb.start()
        cs.append((ca, cb))
    return cs

def products(x, av, bv, xh, xl, p, loads, order, q, rs):
    y, z = q["y"], q["z"]
    far = lambda v: lax.rem(v+2, 4)
    up = lambda v: lax.rem(v+1, 4)
    dn = lambda v: lax.rem(v+3, 4)
    h, l = split(x[...])
    xh[...] = h
    xl[...] = l
    def blockA(k):
        w = dot3(av[k].reshape(512, DEEP), bv[k].reshape(512, DEEP), xh[:, 0:256], xl[:, 0:256])
        p[k, :, :, :, 0:256] = w.reshape(2, 4, 64, 256)
    def blockB(k):
        w = dot3(av[:, :, k].reshape(512, DEEP), bv[:, :, k].reshape(512, DEEP), xh[:, 256:512], xl[:, 256:512])
        p[:, :, k, :, 256:512] = w.reshape(4, 2, 64, 256)
    for i, k in enumerate(order):
        loads[i][0].wait(); loads[i][1].wait()
        split_rows(av, bv, k)
        if i == 0:
            blockA(far(y))
            start_relay(rs.a1)
    blockB(far(z)); start_relay(rs.b1)
    blockA(up(y)); blockA(dn(y)); start_direct(rs.a1)
    blockB(up(z)); blockB(dn(z)); start_direct(rs.b1)
    rs.a1.forward(); rs.b1.forward()
    blockA(y); blockB(z)

def row_order(q):
    y = q["y"]
    return [lax.rem(y+d, 4) for d in (2, 1, 3, 0)]

def vm(shape, dt=jnp.float32):
    return pltpu.VMEM(shape, dt)

def product_scratch():
    D = pltpu.SemaphoreType.DMA
    return [vm((4,2,4,64,DEEP), bf16), vm((4,2,4,64,DEEP), bf16), vm((DEEP,512), bf16), vm((DEEP,512), bf16), vm((4,2,4,64,512))]

ANY = pl.BlockSpec(memory_space=pl.ANY)

def call2(kernel, name, cid, ins, outs, scratch, *args):
    return pl.pallas_call(kernel, out_shape=[jax.ShapeDtypeStruct(s, d) for s, d, _ in outs],
        in_specs=list(ins), out_specs=[s for _, _, s in outs], scratch_shapes=scratch,
        compiler_params=pltpu.CompilerParams(collective_id=cid, has_side_effects=True, vmem_limit_bytes=62*2**20), name=name)(*args)

F = jnp.float32

RA = pl.ds(0, 32); RB = pl.ds(32, 32)
HALF = 256

class RS3:
    def __init__(self, p, o, q, nb, scr, cols):
        (relA, finA, relB, finB, self.qa, self.qb, relA2, finA2, relB2, finB2,
         self.ra, self.rb, self.recx, ss, rs, self.sx, self.rx) = scr
        self.o, self.q, self.nb, self.cols = o, q, nb, cols
        y, x, z = q["y"], q["xl"], q["z"]
        self.a1 = RingRS(lambda k,h: p.at[k,h,:,RA,cols], y, nb["yp"], nb["ym"], relA, finA, ss.at[0], rs.at[0])
        self.b1 = RingRS(lambda k,h: p.at[:,h,k,RB,cols], z, nb["zp"], nb["zm"], relB, finB, ss.at[1], rs.at[1])
        self.a2 = RingRS(lambda k,h: self.qa.at[h,k], z, nb["zp"], nb["zm"], relA2, finA2, ss.at[2], rs.at[2])
        self.b2 = RingRS(lambda k,h: self.qb.at[h,k], y, nb["yp"], nb["ym"], relB2, finB2, ss.at[3], rs.at[3])
    def forward(self):
        self.a1.forward(); self.b1.forward()
    def second(self):
        self.a1.finish(self.qa); self.a2.start()
        self.b1.finish(self.qb); self.b2.start()
    def second_forward(self):
        self.a2.forward(); self.b2.forward()
    def third(self):
        x = self.q["xl"]
        self.a2.finish(self.ra)
        self.cxa = rc(self.ra.at[1-x], self.recx.at[0], self.sx.at[0], self.rx.at[0], self.nb["xd"]); self.cxa.start()
        self.b2.finish(self.rb)
        self.cxb = rc(self.rb.at[1-x], self.recx.at[1], self.sx.at[1], self.rx.at[1], self.nb["xd"]); self.cxb.start()
    def end(self):
        x = self.q["xl"]
        self.cxa.wait_recv()
        self.o[0:32, self.cols] = self.ra[x] + self.recx[0]
        self.cxb.wait_recv()
        self.o[32:64, self.cols] = self.rb[x] + self.recx[1]
        for t in (self.a1, self.b1, self.a2, self.b2): t.drain()
        self.cxa.wait_send(); self.cxb.wait_send()

def rs3_scratch():
    S = 32
    D = pltpu.SemaphoreType.DMA
    V = vm
    return [V((2,4,S,256)), V((2,2,4,S,256)), V((2,4,S,256)), V((2,2,4,S,256)), V((2,4,S,256)), V((2,4,S,256)),
            V((2,S,256)), V((2,2,S,256)), V((2,S,256)), V((2,2,S,256)), V((2,S,256)), V((2,S,256)), V((2,S,256)),
            D((4,6)), D((4,6)), D((2,)), D((2,))]
NRS = 17

class AG3:
    def __init__(self, o, q, nb, scr, cols):
        ss, rs, sx, rx = scr
        y, x, z = q["y"], q["xl"], q["z"]
        yp, ym, zp, zm, xd = nb["yp"], nb["ym"], nb["zp"], nb["zm"], nb["xd"]
        all_rows = pl.ds(0, 64)
        self.cx = rc(o.at[y,x,z,all_rows,cols], o.at[y,x,z,all_rows,cols], sx.at[0], rx.at[0], xd)
        self.cxr = rc(o.at[y,1-x,z,all_rows,cols], o.at[y,1-x,z,all_rows,cols], sx.at[0], rx.at[0], xd)
        self.a1 = RingAG(lambda k,h: o.at[y,h,k,RA,cols], z, zp, zm, ss.at[0], rs.at[0])
        self.b1 = RingAG(lambda k,h: o.at[k,h,z,RB,cols], y, yp, ym, ss.at[1], rs.at[1])
        self.a2 = RingAG(lambda k,h: o.at[k,h,:,RA,cols], y, yp, ym, ss.at[2], rs.at[2])
        self.b2 = RingAG(lambda k,h: o.at[:,h,k,RB,cols], z, zp, zm, ss.at[3], rs.at[3])
    def first(self):
        self.cx.start()
    def second(self):
        self.cxr.wait_recv()
        self.a1.start(); self.b1.start()
    def second_forward(self):
        self.a1.forward(); self.b1.forward()
    def third(self):
        self.a1.finish(); self.a2.start()
        self.b1.finish(); self.b2.start()
    def third_forward(self):
        self.a2.forward(); self.b2.forward()
    def near(self, t):
        t.r[2].wait_recv(); t.r[3].wait_recv()
    def far(self, t):
        t.r[4].wait_recv(); t.r[5].wait_recv()
    def drain(self):
        for t in (self.a1, self.b1, self.a2, self.b2): t.drain()
        self.cx.wait_send()

QROWS = DEEP // 4

def quarter(h, k):
    return pl.ds(pl.multiple_of((h*2 + k)*QROWS, 32), QROWS)

class RowRS:
    def __init__(self, w, o, q, nb, scr, cols):
        self.rec1, self.qf, self.rec2, s1, r1, s2, r2 = scr
        self.w, self.o, self.cols = w, o, cols
        h, k = self.h, self.k = q["xh"], q["core"]
        self.c = [rc(w.at[quarter(1-h, 1-k), cols], self.rec1.at[0], s1.at[0], r1.at[0], nb["other"]),
                  rc(w.at[quarter(h, 1-k), cols], self.rec1.at[1], s1.at[1], r1.at[1], nb["other"])]
        self.c2 = rc(self.qf, self.rec2, s2.at[0], r2.at[0], nb["far"])
    def start(self):
        for t in self.c: t.start()
    def middle(self):
        self.c[0].wait_recv()
        self.qf[...] = self.w[quarter(1-self.h, self.k), self.cols] + self.rec1[0]
        self.c2.start()
        self.c[1].wait_recv()
        self.o[:, self.cols] = self.w[quarter(self.h, self.k), self.cols] + self.rec1[1]
    def end(self):
        self.c2.wait_recv()
        self.o[:, self.cols] = self.o[:, self.cols] + self.rec2[...]
        for t in self.c: t.wait_send()
        self.c2.wait_send()

def row3_scratch():
    D = pltpu.SemaphoreType.DMA
    n = QROWS
    return [vm((2,n,HALF)), vm((n,HALF)), vm((n,HALF)), D((2,)), D((2,)), D((1,)), D((1,))]
NROW = 7

class RowAG:
    def __init__(self, o, q, nb, scr, cols):
        s1, r1, s2, r2 = scr
        h, k = q["xh"], q["core"]
        v = lambda a, b: o.at[quarter(a, b), cols]
        self.cf = rc(v(h,k), v(h,k), s1.at[0], r1.at[0], nb["far"])
        self.cfr = rc(v(1-h,k), v(1-h,k), s1.at[0], r1.at[0], nb["far"])
        self.co = rc(v(h,k), v(h,k), s2.at[0], r2.at[0], nb["other"])
        self.cor = rc(v(h,1-k), v(h,1-k), s2.at[0], r2.at[0], nb["other"])
        self.co2 = rc(v(1-h,k), v(1-h,k), s2.at[1], r2.at[1], nb["other"])
        self.co2r = rc(v(1-h,1-k), v(1-h,1-k), s2.at[1], r2.at[1], nb["other"])
    def start(self):
        self.cf.start(); self.co.start()
    def forward(self):
        self.cfr.wait_recv(); self.co2.start()
    def finish(self):
        self.cor.wait_recv(); self.co2r.wait_recv()
    def drain(self):
        self.cf.wait_send(); self.co.wait_send(); self.co2.wait_send()

XLAST = [(0, 2, "yzx"), (2, 2, "zyx"), (4, 1, "yzx")]
COLS = [pl.ds(0, HALF), pl.ds(HALF, HALF)]

def neighbours(r, c, q):
    nb = col_neighbours(r, q)
    nb.update(row_neighbours(c, q))
    return nb

def transpose_pieces(av, bv, th, tl, lo, hi):
    def body(i, _):
        cols = pl.ds(pl.multiple_of(i*128, 128), 128)
        for n in range(13):
            lanes = slice(n*128, n*128+128)
            if hi <= 8:
                y = lax.div(i, 2); x = lax.rem(i, 2)
                u, v = av[y, x, :, 0:32, lanes], bv[y, x, :, 0:32, lanes]
            else:
                z = lax.div(i - 8, 2); g = lax.rem(i, 2)*2
                u, v = av[pl.ds(g, 2), :, z, 32:64, lanes], bv[pl.ds(g, 2), :, z, 32:64, lanes]
            d = u.reshape(128, 128).astype(jnp.float32) + v.reshape(128, 128).astype(jnp.float32)
            h, l = split(d.T)
            th[lanes, cols] = h
            tl[lanes, cols] = l
        return 0
    lax.fori_loop(lo, hi, body, 0)

def sketch3_kernel(a, b, x, o, th_o, tl_o, av, bv, xh, xl, p, th, tl, lsem, osem, *scr):
    r, c, q = mesh_place()
    order = row_order(q)
    loads = load_start(a, b, av, bv, lsem, order)
    nb = col_neighbours(r, q)
    barrier(list(nb.values()))
    rs = RS2(p, o, q, nb, scr)
    products(x, av, bv, xh, xl, p, loads, order, q, rs)
    transpose_pieces(av, bv, th, tl, 0, 8)
    transpose_pieces(av, bv, th, tl, 8, 12)
    rs.second()
    rs.second_forward()
    transpose_pieces(av, bv, th, tl, 12, 16)
    outs = [pltpu.make_async_copy(th, th_o, osem.at[0]), pltpu.make_async_copy(tl, tl_o, osem.at[1])]
    for t in outs: t.start()
    rs.third()
    rs.end()
    for t in outs: t.wait()

def sketch3(a, b, x):
    D = pltpu.SemaphoreType.DMA
    return call2(sketch3_kernel, "sketch", 1, (ANY, ANY, VM), [((64,512), F, VM), ((DEEP,2048), bf16, ANY), ((DEEP,2048), bf16, ANY)],
        product_scratch() + [vm((DEEP,2048), bf16), vm((DEEP,2048), bf16), D((2,4)), D((2,))] + rs_scratch(), a, b, x)

up = lambda v: lax.rem(v+1, 4)
dn = lambda v: lax.rem(v+3, 4)
far = lambda v: lax.rem(v+2, 4)

CK = (3, 2, 4)
RK = (4, 4, 4, 4)

def steps(gen, n):
    for _ in range(n):
        next(gen, None)

def cosketch3_kernel(own, th_i, tl_i, raw, x1, gb, o, th, tl, w, lsem, *scr):
    r, c, q = mesh_place()
    ct = [pltpu.make_async_copy(th_i, th, lsem.at[0]), pltpu.make_async_copy(tl_i, tl, lsem.at[1])]
    for t in ct: t.start()
    nb = neighbours(r, c, q)
    y, z = q["y"], q["z"]
    o[y, q["xl"], z] = own[...]
    barrier(gram_devices(c, q))
    s = list(scr)
    take = lambda n: [s.pop(0) for _ in range(n)]
    gr = gram_steps(own, gb, c, q, take(NGRAM))
    ag = [AG3(o, q, nb, take(4), COLS[i]) for i in range(2)]
    row = [RowRS(w, raw, q, nb, take(NROW), COLS[i]) for i in range(2)]
    ch = chol_steps(Blocks(gb), x1)
    def blockA(i, k, first=False):
        cols = pl.ds(pl.multiple_of(k*256, 256), 256)
        sh, sl = split(o[k, :, :, RA, COLS[i]].reshape(256, HALF))
        v = dot3(th[:, cols], tl[:, cols], sh, sl)
        w[:, COLS[i]] = v if first else w[:, COLS[i]] + v
    def blockB(i, k):
        cols = pl.ds(pl.multiple_of(1024 + k*256, 256), 256)
        sh, sl = split(o[:, :, k, RB, COLS[i]].reshape(256, HALF))
        w[:, COLS[i]] = w[:, COLS[i]] + dot3(th[:, cols], tl[:, cols], sh, sl)
    ag[0].first(); ag[1].first(); next(gr)
    ag[0].second(); next(gr)
    ag[0].second_forward(); next(gr)
    ag[0].third(); ag[1].second(); next(gr)
    for t in ct: t.wait()
    blockA(0, y, True); blockB(0, z)
    ag[0].third_forward(); ag[1].second_forward(); next(gr)
    ag[0].near(ag[0].a2); blockA(0, up(y)); blockA(0, dn(y))
    ag[0].near(ag[0].b2); ag[1].third(); next(gr)
    blockB(0, up(z)); blockB(0, dn(z))
    ag[0].far(ag[0].a2); blockA(0, far(y))
    ag[0].far(ag[0].b2); blockB(0, far(z))
    row[0].start(); next(gr)
    blockA(1, y, True); blockB(1, z)
    ag[1].third_forward()
    row[0].middle()
    run(gr)
    steps(ch, CK[0])
    ag[1].near(ag[1].a2); blockA(1, up(y)); blockA(1, dn(y))
    ag[1].near(ag[1].b2); blockB(1, up(z)); blockB(1, dn(z))
    steps(ch, CK[1])
    ag[1].far(ag[1].a2); blockA(1, far(y))
    ag[1].far(ag[1].b2); blockB(1, far(z))
    row[1].start()
    steps(ch, CK[2])
    row[0].end()
    row[1].middle()
    run(ch)
    row[1].end()
    for t in ag: t.drain()

def cosketch3(own, th, tl):
    D = pltpu.SemaphoreType.DMA
    return call2(cosketch3_kernel, "cosketch", 2, (VM, ANY, ANY), [((QROWS,512), F, VM), ((512,512), F, VM)],
        [vm((2,5,B,B)), vm((4,2,4,64,512)), vm((DEEP,2048), bf16), vm((DEEP,2048), bf16), vm((DEEP,512)), D((2,))]
        + gram_scratch() + ag_scratch()*2 + row3_scratch()*2, own, th, tl)

def resketch3_kernel(a, b, raw, x1, o, x2, gb, own, co, av, bv, xh, xl, p, lsem, *scr):
    r, c, q = mesh_place()
    order = row_order(q)
    loads = load_start(a, b, av, bv, lsem, order)
    nb = neighbours(r, c, q)
    y, z = q["y"], q["z"]
    mine = quarter(q["xh"], q["core"])
    s = list(scr)
    take = lambda n: [s.pop(0) for _ in range(n)]
    gr = gram_steps(own, gb, c, q, take(NGRAM), XLAST)
    rg = [RowAG(co, q, nb, take(4), COLS[i]) for i in range(2)]
    rs = [RS3(p, o, q, nb, take(NRS), COLS[i]) for i in range(2)]
    ch = chol_steps(Blocks(gb), x2)
    def normed(i):
        n = (i+1)*HALF
        v = apply_t(raw[:, 0:n], x1[i*HALF:n, 0:n])
        own[:, COLS[i]] = v
        co[mine, COLS[i]] = v
    def parts(i):
        h, l = split(co[:, COLS[i]])
        xh[:, COLS[i]] = h
        xl[:, COLS[i]] = l
    def blockA(i, k):
        v = dot3(av[k, :, :, RA].reshape(256, DEEP), bv[k, :, :, RA].reshape(256, DEEP), xh[:, COLS[i]], xl[:, COLS[i]])
        p[k, :, :, RA, COLS[i]] = v.reshape(2, 4, 32, HALF)
    def blockB(i, k):
        v = dot3(av[:, :, k, RB].reshape(256, DEEP), bv[:, :, k, RB].reshape(256, DEEP), xh[:, COLS[i]], xl[:, COLS[i]])
        p[:, :, k, RB, COLS[i]] = v.reshape(4, 2, 32, HALF)
    def first_blocks(i):
        blockA(i, far(y)); start_relay(rs[i].a1)
        blockB(i, far(z)); start_relay(rs[i].b1)
    def other_blocks(i):
        blockA(i, up(y)); blockA(i, dn(y)); start_direct(rs[i].a1)
        blockB(i, up(z)); blockB(i, dn(z)); start_direct(rs[i].b1)
    def own_blocks(i):
        blockA(i, y); blockB(i, z)
    def ready(i):
        loads[i][0].wait(); loads[i][1].wait()
        split_rows(av, bv, order[i])
    barrier(gram_devices(c, q))
    normed(0); rg[0].start()
    normed(1); next(gr)
    ready(0); ready(1); next(gr)
    ready(2); ready(3); next(gr)
    rg[0].forward()
    next(gr)
    rg[1].start()
    rg[0].finish(); parts(0)
    first_blocks(0); other_blocks(0); next(gr)
    rs[0].forward(); own_blocks(0); next(gr)
    rg[1].forward(); rg[1].finish(); parts(1)
    first_blocks(1); next(gr)
    rs[0].second()
    other_blocks(1); run(gr)
    rs[0].second_forward(); rs[1].forward()
    own_blocks(1)
    steps(ch, RK[0])
    rs[0].third(); rs[1].second()
    steps(ch, RK[1])
    rs[1].second_forward(); rs[0].end()
    steps(ch, RK[2])
    rs[1].third()
    steps(ch, RK[3])
    rs[1].end()
    run(ch)
    for t in rg: t.drain()

def resketch3(a, b, raw, x1):
    D = pltpu.SemaphoreType.DMA
    return call2(resketch3_kernel, "resketch", 3, (ANY, ANY, VM, VM), [((64,512), F, VM), ((512,512), F, VM)],
        [vm((2,5,B,B)), vm((QROWS,512)), vm((DEEP,512))] + product_scratch() + [D((2,4))] + gram_scratch()
        + row_ag_scratch()*2 + rs3_scratch()*2, a, b, raw, x1)

def last_kernel(p, x2, o, own, gb, x3, *scr):
    r, c, q = mesh_place()
    own[...] = apply_t(p[...], x2[...])
    barrier(gram_devices(c, q))
    run(gram_steps(own, gb, c, q, scr))
    run(chol_steps(Blocks(gb), x3, 0))
    o[...] = SCALE * apply_t(own[...], x3[...])

def last(raw, x2):
    return call2(last_kernel, "last", 4, (VM, VM), [((64,512), F, VM)], [vm((64,512)), vm((2,5,B,B)), vm((512,512))] + gram_scratch(), raw, x2)[0]
def shards(adjusted_weight, base_weight, test_matrix):
    rows = (4, 2, 4, 64, DEEP)
    a, b = adjusted_weight.reshape(rows), base_weight.reshape(rows)
    own, th, tl = sketch3(a, b, test_matrix)
    raw, x1 = cosketch3(own, th, tl)
    raw, x2 = resketch3(a, b, raw, x1)
    return last(raw, x2)


def solution(mesh):
    return jax.shard_map(
        shards,
        mesh=mesh,
        in_specs=(P("row", "col"), P("row", "col"), P("col", None)),
        out_specs=P(("row", "col"), None),
        check_vma=False,
    )
```
